256 devices in a mesh: pool: 32 (over x, z_lo, y), tensor: 8 (over z_hi, core).
Axes of the slice: x: 4, y: 4, z: 8 (z_hi: 4, z_lo: 2; z = z_hi * 2 + z_lo), core: 2. Of those that a mesh axis runs over, the one named last changes fastest.
Arguments:
- queries: bfloat16 [16384, 4096], P('pool', 'tensor'), may hold values from -400 to 400
- new_key_value: bfloat16 [16384, 2, 1024], P('pool', None, 'tensor'), may hold values from -5 to 5
- saved_key_value: bfloat16 [1024, 128, 2, 1024], P('pool', None, None, 'tensor'), may hold values from -5 to 5
- out_weight: bfloat16 [4096, 5120], P('tensor'), may hold values from -5 to 5
- hist_owner: int32 [32, 64], P('pool'), may hold values from 0 to 31, as said below
- hist_block: int32 [32, 64], P('pool'), may hold values from 0 to 31
- hist_len: int32 [32], P('pool'), may hold values from 8 to 64, as said below
- evict: int32 [32], P('pool'), may hold values 0 or 1
- dest_owner: int32 [32, 4], P('pool'), may hold values from 0 to 31, as said below
- dest_slot: int32 [32, 4], P('pool'), may hold values from 0 to 31, as said below
Outputs:
- attn_out: bfloat16 [16384, 5120], P(('pool', 'tensor'))
- pool_out: bfloat16 [1024, 128, 2, 1024], P('pool', None, None, 'tensor')
The draws below stay inside these ranges and needn't reach their ends.
Inputs may be any that keep to these rules, and one draw needn't show every extreme that they name: `hist_owner`: in row p each owner appears exactly 2 times among all 64 entries, so at most 2 times among the first hist_len[p]. `hist_len`: some instance has all 64 blocks. `dest_owner`: the 4 owners of one row are distinct, and each column names every owner once. All pairs (dest_owner, dest_slot) are distinct.
All inputs are finite; a program needn't handle non-finite values. No bound on the sum of `evict` on one device may be relied on, other than what follows from the above.
Results may differ from the reference program's by a relative error of at most 0.017.
Values may be sent and summed in bfloat16 or wider, within the bound.
No kernel may reach another device: no remote copies, remote signals or barrier semaphores. Data moves between devices by JAX's collectives and lax.ppermute only.
A program may use at most 128 MiB of HBM per device.

```python
import math
import jax
import jax.numpy as jnp
from jax import lax

D = 5120
QUERY_HEADS = 32
KEY_VALUE_HEADS = 8
HEAD_SIZE = 128
BLOCK_POSITIONS = 128
NEW_TOKENS = 512
POOL_DEV = 32
SESSION_BLOCKS = 64
NEW_TOKEN_BLOCKS = 4
TOTAL_TOKENS = 16384
SAVED_POOL_BLOCKS = 1024
HEAD_GROUP = 4
N_POOL = 32
N_TENSOR = 8


TARGETS = (120.0, 240.0, 360.0)


def token_kv(key):
    sampled_inputs = jnp.clip(jax.random.normal(key, (N_POOL, NEW_TOKENS, 2, KEY_VALUE_HEADS, HEAD_SIZE), jnp.float32), -4.0, 4.0)
    for number, strength in enumerate(TARGETS):
        partner = sampled_inputs[:, 2 * number + 1, 0]
        shifted = partner
        sampled_inputs = sampled_inputs.at[:, 2 * number + 1, 0].set(shifted)
    return sampled_inputs


def draw_new_key_value(key, part):
    sampled_inputs = token_kv(key)
    return sampled_inputs.reshape(TOTAL_TOKENS, 2, KEY_VALUE_HEADS * HEAD_SIZE).astype(jnp.bfloat16)


def draw_queries(key, part):
    key = jax.random.fold_in(key, 3)
    sampled_inputs = jnp.clip(jax.random.normal(key, (N_POOL, NEW_TOKENS, QUERY_HEADS, HEAD_SIZE), jnp.float32), -4.0, 4.0)
    for number, strength in enumerate(TARGETS):
        sampled_inputs = sampled_inputs.at[:, NEW_TOKENS - 1 - number].set(sampled_inputs[:, NEW_TOKENS - 1 - number])
    return sampled_inputs.reshape(TOTAL_TOKENS, QUERY_HEADS * HEAD_SIZE).astype(jnp.bfloat16)


def shuffle_list(stream):
    return jax.random.permutation(stream, SESSION_BLOCKS)


def shuffle_pool(stream):
    return jax.random.permutation(stream, POOL_DEV)


def draw_hist_owner(key, part):
    key = jax.random.fold_in(key, 5)
    streams = jax.random.split(key, N_POOL)
    orders = jax.vmap(shuffle_list)(streams)
    return (orders % N_POOL).astype(jnp.int32)


def draw_hist_len(key, part):
    key = jax.random.fold_in(key, 7)
    split_one, split_two = jax.random.split(key)
    lengths = jax.random.randint(split_one, (N_POOL,), max(SESSION_BLOCKS // 8, 1), SESSION_BLOCKS + 1)
    chosen = jax.random.randint(split_two, (), 0, N_POOL)
    return jnp.where(jnp.arange(N_POOL) == chosen, SESSION_BLOCKS, lengths).astype(jnp.int32)


def destinations(key):
    key = jax.random.fold_in(key, 21)
    streams = jax.random.split(key, 4)
    outer_order = jax.random.permutation(streams[0], N_POOL)
    inner_order = jax.random.permutation(streams[1], N_POOL)
    shifts = jax.random.permutation(streams[2], N_POOL - 1)[:NEW_TOKEN_BLOCKS] + 1
    owners = outer_order[(inner_order[:, None] + shifts[None, :]) % N_POOL]
    slot_orders = jax.vmap(shuffle_pool)(jax.random.split(streams[3], N_POOL))
    slots = slot_orders[owners, jnp.arange(NEW_TOKEN_BLOCKS)[None, :]]
    return (owners.astype(jnp.int32), slots.astype(jnp.int32))


def draw_dest_owner(key, part):
    return destinations(key)[0]


def draw_dest_slot(key, part):
    return destinations(key)[1]


def plant(result, own_key, low, largest):
    shape = result.shape
    index_at = [jax.random.randint(jax.random.fold_in(own_key, axis), (), 0, shape[axis]) for axis in range(len(shape))]
    result = result.at[tuple(index_at)].set(low)
    longest = shape.index(max(shape))
    index_at[longest] = (index_at[longest] + 1) % shape[longest]
    return result.at[tuple(index_at)].set(largest)


def shard_levels(stream_key, dims, shards, smallest, high):
    gain, own = 1.0, jax.random.fold_in(stream_key, 6)
    for dim, shards_of in shards:
        heights = jnp.exp(jax.random.uniform(jax.random.fold_in(own, dim), (shards_of,), jnp.float32, smallest / len(shards), high / len(shards)))
        gain = gain * jnp.repeat(heights, dims[dim] // shards_of).reshape([-1 if axis == dim else 1 for axis in range(len(dims))])
    return gain


def noise(stream_key, dims, width, reach, pieces=(), held_as=jnp.bfloat16):
    values = jax.random.normal(stream_key, dims, jnp.float32) * width
    if len(pieces) > 0:
        values = shard_levels(stream_key, dims, pieces, -0.22, 0.18) * values
    return jnp.clip(values, min=-reach, max=reach).astype(held_as)


def setup_inputs(seed: int = 0) -> dict:
    arg_keys = jax.random.split(jax.random.key(seed), 11)
    return {
        "queries": draw_queries(jax.random.fold_in(arg_keys[10], 71), 0),
        "new_key_value": draw_new_key_value(jax.random.fold_in(arg_keys[10], 71), 0),
        "saved_key_value": noise(arg_keys[2], (SAVED_POOL_BLOCKS, BLOCK_POSITIONS, 2, KEY_VALUE_HEADS * HEAD_SIZE), 1.0, 5.0, ((0, 32), (3, 8))),
        "out_weight": noise(arg_keys[3], (QUERY_HEADS * HEAD_SIZE, D), 1.0, 5.0, ((0, 8),)),
        "hist_owner": draw_hist_owner(jax.random.fold_in(arg_keys[10], 71), 0),
        "hist_block": plant(jax.random.randint(arg_keys[5], (N_POOL, SESSION_BLOCKS), 0, POOL_DEV), jax.random.fold_in(arg_keys[5], 1), 0, POOL_DEV - 1).astype(jnp.int32),
        "hist_len": draw_hist_len(jax.random.fold_in(arg_keys[10], 71), 0),
        "evict": plant((jax.random.randint(arg_keys[7], (N_POOL,), 0, 2) < 1).astype(jnp.int32), jax.random.fold_in(arg_keys[7], 1), 0, 1),
        "dest_owner": draw_dest_owner(jax.random.fold_in(arg_keys[10], 71), 0),
        "dest_slot": draw_dest_slot(jax.random.fold_in(arg_keys[10], 71), 0),
    }


def reference(queries, new_key_value, saved_key_value, out_weight, hist_owner, hist_block, hist_len, evict, dest_owner, dest_slot):
    head_grouping = QUERY_HEADS // KEY_VALUE_HEADS
    score_scale = 1.0 / math.sqrt(HEAD_SIZE)
    causal = jnp.arange(NEW_TOKENS)[None, :] <= jnp.arange(NEW_TOKENS)[:, None]

    def instance(inputs):
        query_matrix, key_value_rows, owner_row, block_row, length = inputs
        selected_blocks = saved_key_value[(owner_row * POOL_DEV + block_row).astype(jnp.int32)]
        selected_blocks = selected_blocks.reshape(SESSION_BLOCKS * BLOCK_POSITIONS, 2, KEY_VALUE_HEADS, HEAD_SIZE)
        recent_key_value = key_value_rows.reshape(NEW_TOKENS, 2, KEY_VALUE_HEADS, HEAD_SIZE)
        key_rows = jnp.concatenate([selected_blocks[:, 0], recent_key_value[:, 0]], axis=0).transpose(1, 0, 2)
        value_rows = jnp.concatenate([selected_blocks[:, 1], recent_key_value[:, 1]], axis=0).transpose(1, 0, 2)
        live_keys = jnp.repeat(jnp.arange(SESSION_BLOCKS) < length, BLOCK_POSITIONS)
        allowed = jnp.concatenate([jnp.broadcast_to(live_keys[None, :], (NEW_TOKENS, SESSION_BLOCKS * BLOCK_POSITIONS)), causal], axis=1)
        allowed = jnp.tile(allowed, (head_grouping, 1))
        grouped_queries = query_matrix.reshape(NEW_TOKENS, KEY_VALUE_HEADS, head_grouping, HEAD_SIZE).transpose(1, 2, 0, 3).reshape(KEY_VALUE_HEADS, head_grouping * NEW_TOKENS, HEAD_SIZE)

        def one_head(head_parts):
            query_head, key_head, value_head = head_parts
            scores = jnp.dot(query_head, key_head.T, preferred_element_type=jnp.float32) * score_scale
            scores = jnp.where(allowed, scores, -jnp.inf)
            highest = lax.optimization_barrier(jnp.max(scores, axis=1, keepdims=True))
            weights = jnp.exp(scores - highest)
            normalized = (weights / lax.optimization_barrier(jnp.sum(weights, axis=1, keepdims=True))).astype(jnp.bfloat16)
            return jnp.dot(normalized, value_head, preferred_element_type=jnp.float32).astype(jnp.bfloat16)
        context_output = lax.map(one_head, (grouped_queries, key_rows, value_rows))
        return context_output.reshape(KEY_VALUE_HEADS, head_grouping, NEW_TOKENS, HEAD_SIZE).transpose(2, 0, 1, 3).reshape(NEW_TOKENS, QUERY_HEADS * HEAD_SIZE)
    stacked_queries = queries.reshape(N_POOL, NEW_TOKENS, QUERY_HEADS * HEAD_SIZE)
    stacked_key_value = new_key_value.reshape(N_POOL, NEW_TOKENS, 2, KEY_VALUE_HEADS * HEAD_SIZE)
    context_output = lax.map(instance, (stacked_queries, stacked_key_value, hist_owner, hist_block, hist_len)).reshape(TOTAL_TOKENS, QUERY_HEADS * HEAD_SIZE)
    span = HEAD_GROUP * HEAD_SIZE
    summed = jnp.zeros((TOTAL_TOKENS, D), jnp.float32)
    for member in range(N_TENSOR):
        partial_sum = jnp.dot(context_output[:, member * span:(member + 1) * span], out_weight[member * span:(member + 1) * span], preferred_element_type=jnp.float32)
        rounded = lax.optimization_barrier(partial_sum.astype(jnp.bfloat16))
        summed = summed + rounded.astype(jnp.float32)
    attn_out = summed.astype(jnp.bfloat16)
    targets = jnp.where(evict[:, None] > 0, dest_owner * POOL_DEV + dest_slot, SAVED_POOL_BLOCKS).reshape(-1).astype(jnp.int32)
    fresh_blocks = new_key_value.reshape(N_POOL * NEW_TOKEN_BLOCKS, BLOCK_POSITIONS, 2, KEY_VALUE_HEADS * HEAD_SIZE)
    pool_out = saved_key_value.at[targets].set(fresh_blocks, mode='drop')
    return (attn_out, pool_out)
```

```python
import functools
import math

import jax
import jax.numpy as jnp
from jax import lax
from jax.experimental import pallas as pl
from jax.experimental.pallas import tpu as pltpu
from jax.sharding import PartitionSpec as P

HEAD = 128
CHUNK = 4
NT = (((1,), (1,)), ((), ()))
SMEM = pl.BlockSpec(memory_space=pltpu.SMEM)
VMEM = pl.BlockSpec(memory_space=pltpu.VMEM)
ANY = pl.BlockSpec(memory_space=pl.ANY)


def meta_kernel(dest_owner, dest_slot, evict, owner_ref, block_ref, meta_ref, order_ref):
    pool, entries = meta_ref.shape[0], owner_ref.shape[1]
    owner = jnp.broadcast_to(owner_ref[...], (pool, entries))
    block = jnp.broadcast_to(block_ref[...], (pool, entries))
    row = lax.broadcasted_iota(jnp.int32, (pool, entries), 0)
    col = lax.broadcasted_iota(jnp.int32, (pool, entries), 1)
    match = owner == row
    first = jnp.min(jnp.where(match, col, entries), axis=1, keepdims=True)
    want0 = jnp.sum(jnp.where(match & (col == first), block, 0), axis=1, keepdims=True)
    want1 = jnp.sum(jnp.where(match & (col > first), block, 0), axis=1, keepdims=True)
    place = 2 * row + jnp.where(col > first, 1, 0)
    order_ref[...] = jnp.sum(jnp.where(match, place, 0), axis=0, keepdims=True)
    lane = lax.broadcasted_iota(jnp.int32, (pool, 128), 1)
    out = jnp.where(lane == 0, want0, jnp.where(lane == 1, want1, 0))
    for b in range(4):
        out = jnp.where(lane == 2 + b, dest_owner[0, b], out)
        out = jnp.where(lane == 6 + b, dest_slot[0, b], out)
    out = jnp.where(lane == 10, evict[0], out)
    for o in range(pool):
        meta_ref[o] = out[o : o + 1]


def exchange_table(hist_owner, hist_block, dest_owner, dest_slot, evict, pool):
    return pl.pallas_call(
        meta_kernel,
        out_shape=(
            jax.ShapeDtypeStruct((pool, 1, 128), jnp.int32),
            jax.ShapeDtypeStruct(hist_owner.shape, jnp.int32),
        ),
        in_specs=[SMEM, SMEM, SMEM, VMEM, VMEM],
        out_specs=(VMEM, VMEM),
        name="table",
    )(dest_owner, dest_slot, evict, hist_owner, hist_block)


def gather_kernel(wanted, pool_ref, out_ref, sems):
    copies = []
    for i in range(out_ref.shape[0]):
        copies.append(
            pltpu.make_async_copy(
                pool_ref.at[wanted[i // 2, 0, i % 2]], out_ref.at[i], sems.at[i]
            )
        )
        copies[-1].start()
    for copy in copies:
        copy.wait()


def gather_blocks(wanted, pool_blocks):
    count = 2 * wanted.shape[0]
    return pl.pallas_call(
        gather_kernel,
        out_shape=jax.ShapeDtypeStruct((count,) + pool_blocks.shape[1:], pool_blocks.dtype),
        in_specs=[SMEM, ANY],
        out_specs=ANY,
        scratch_shapes=[pltpu.SemaphoreType.DMA((count,))],
        name="gather",
    )(wanted, pool_blocks)


def attend_kernel(order, length, base, q_ref, kv_ref, kn_ref, vn_ref, o_ref, sbuf, *, tok, split):
    c = math.log2(math.e) / math.sqrt(HEAD)
    heads = q_ref.shape[1] // HEAD
    per = heads // split
    rows = per * tok
    new = kn_ref.shape[0]
    qs = [
        jnp.concatenate(
            [q_ref[:, (s * per + h) * HEAD : (s * per + h + 1) * HEAD] for h in range(per)], axis=0
        )
        for s in range(split)
    ]

    def scores(k, q):
        return lax.dot_general(k, q, NT, preferred_element_type=jnp.float32)

    def update(state, s, vt):
        m, l, acc = state
        top = jnp.maximum(m, jnp.max(s, axis=0, keepdims=True))
        p = jnp.exp2(s * c - top * c)
        keep = jnp.exp2((m - top) * c)
        l = l * keep + jnp.sum(p, axis=0, keepdims=True)
        acc = acc * keep + jnp.dot(
            vt, p.astype(jnp.bfloat16), preferred_element_type=jnp.float32
        )
        return top, l, acc

    key = lax.broadcasted_iota(jnp.int32, (new, rows), 0)
    at = lax.broadcasted_iota(jnp.int32, (new, rows), 1) & (tok - 1)
    token = base[0] + at
    for b in range(1, tok // 128):
        token = jnp.where(at >= 128 * b, base[b] + at - 128 * b, token)
    state = []
    for s in range(split):
        sc = jnp.where(key <= token, scores(kn_ref[...], qs[s]), -jnp.inf)
        m = jnp.max(sc, axis=0, keepdims=True)
        p = jnp.exp2(sc * c - m * c)
        state.append(
            (
                m,
                jnp.sum(p, axis=0, keepdims=True),
                jnp.dot(vn_ref[...], p.astype(jnp.bfloat16), preferred_element_type=jnp.float32),
            )
        )

    def keys_of(i):
        return jnp.concatenate(
            [kv_ref[order[0, i * CHUNK + u], 0:128, :] for u in range(CHUNK)], axis=0
        )

    def values_of(i):
        return jnp.concatenate(
            [kv_ref[order[0, i * CHUNK + u], 128:256, :] for u in range(CHUNK)], axis=1
        )

    n = length[0]
    full = n // CHUNK
    last = kv_ref.shape[0] // CHUNK - 1
    for s in range(split):
        sbuf[0, s] = scores(keys_of(0), qs[s])

    def step(i, state, a):
        k = keys_of(jnp.minimum(i + 1, last))
        vt = values_of(i)
        out = []
        for s in range(split):
            sbuf[1 - a, s] = scores(k, qs[s])
            out.append(update(state[s], sbuf[a, s], vt))
        return tuple(out)

    state = lax.fori_loop(
        0, full // 2, lambda i, st: step(2 * i + 1, step(2 * i, st, 0), 1), tuple(state)
    )
    state = lax.fori_loop(full // 2 * 2, full, lambda i, st: step(i, st, 0), state)

    def tail(i, state):
        k, vt = keys_of(i), values_of(i)
        position = i * (CHUNK * 128) + lax.broadcasted_iota(jnp.int32, (CHUNK * 128, rows), 0)
        live = position < n * 128
        return tuple(
            update(state[s], jnp.where(live, scores(k, qs[s]), -jnp.inf), vt) for s in range(split)
        )

    state = lax.fori_loop(full, (n + CHUNK - 1) // CHUNK, tail, state)
    for s in range(split):
        m, l, acc = state[s]
        context = (acc / l).T.astype(jnp.bfloat16)
        for h in range(per):
            hh = s * per + h
            o_ref[:, hh * HEAD : (hh + 1) * HEAD] = context[h * tok : (h + 1) * tok]


def attend(q, kv, k_new, vt_new, order, length, base):
    tok, width = q.shape
    heads = width // HEAD
    split = 2 if tok > 128 else 1
    return pl.pallas_call(
        functools.partial(attend_kernel, tok=tok, split=split),
        out_shape=jax.ShapeDtypeStruct(q.shape, jnp.bfloat16),
        in_specs=[SMEM, SMEM, SMEM, VMEM, VMEM, VMEM, VMEM],
        out_specs=VMEM,
        scratch_shapes=[pltpu.VMEM((2, split, CHUNK * 128, heads // split * tok), jnp.float32)],
        compiler_params=pltpu.CompilerParams(vmem_limit_bytes=40 * 2**20),
        cost_estimate=pl.CostEstimate(
            flops=tok * heads * 8704 * 128 * 4, bytes_accessed=5 * 2**20, transcendentals=0
        ),
        name=f"attend{tok}",
    )(order, length, base, q, kv, k_new, vt_new)


def write_kernel(slots, saved_ref, fresh_ref, out_ref, sem, sems):
    whole = pltpu.make_async_copy(saved_ref, out_ref, sem)
    whole.start()
    whole.wait()
    for b in range(fresh_ref.shape[0]):

        @pl.when(slots[b] >= 0)
        def _(b=b):
            copy = pltpu.make_async_copy(fresh_ref.at[b], out_ref.at[slots[b]], sems.at[b])
            copy.start()
            copy.wait()


def write_back(slots, saved, fresh):
    return pl.pallas_call(
        write_kernel,
        out_shape=jax.ShapeDtypeStruct(saved.shape, saved.dtype),
        in_specs=[SMEM, ANY, ANY],
        out_specs=ANY,
        scratch_shapes=[pltpu.SemaphoreType.DMA, pltpu.SemaphoreType.DMA((fresh.shape[0],))],
        name="write",
    )(slots, saved, fresh)


def swap_pool(x):
    return lax.all_to_all(x, "pool", split_axis=0, concat_axis=0, tiled=True)


def on_device(
    queries,
    new_key_value,
    saved,
    out_weight,
    hist_owner,
    hist_block,
    hist_len,
    evict,
    dest_owner,
    dest_slot,
):
    pool = lax.axis_size("pool")
    me = lax.axis_index("pool")
    table, order = exchange_table(hist_owner, hist_block, dest_owner, dest_slot, evict, pool)
    told = swap_pool(table)
    pool_blocks = jnp.concatenate(
        [saved[:, :, 0, :], saved[:, :, 1, :].transpose(0, 2, 1)], axis=1
    )
    k_new = new_key_value[:, 0]
    vt_new = new_key_value[:, 1].T
    fetched = swap_pool(gather_blocks(told, pool_blocks).reshape(pool, 512, 128))
    kv = fetched.reshape(2 * pool, 256, 128)

    contexts = []
    for g in range(2):
        base = jnp.array([256 * g, 256 * g + 128], jnp.int32)
        contexts.append(
            attend(queries[256 * g : 256 * (g + 1)], kv, k_new, vt_new, order, hist_len, base)
        )
    contexts = jnp.concatenate(contexts, axis=0)
    attn_out = lax.psum_scatter(
        jnp.dot(contexts, out_weight, preferred_element_type=jnp.float32).astype(jnp.bfloat16),
        "tensor",
        scatter_dimension=0,
        tiled=True,
    )

    pieces = new_key_value.reshape(4, pool, -1).transpose(1, 0, 2)
    pieces, _ = lax.optimization_barrier((pieces, contexts))
    held = swap_pool(pieces)
    targets = told[:, 0, 2:6]
    chosen = targets.T[:, None, :] == jnp.arange(pool, dtype=jnp.int32)[None, :, None]
    onward = jnp.einsum(
        "bop,pbx->obx", chosen.astype(jnp.bfloat16), held, preferred_element_type=jnp.float32
    ).astype(jnp.bfloat16)
    fresh = swap_pool(onward).transpose(1, 0, 2).reshape((4,) + saved.shape[1:])
    mine = (targets == me) & (told[:, 0, 10:11] > 0)
    slots = jnp.max(jnp.where(mine, told[:, 0, 6:10], -1), axis=0)
    pool_out = write_back(slots, saved, fresh)
    return attn_out, pool_out


def solution(mesh):
    in_specs = (
        P("pool", "tensor"),
        P("pool", None, "tensor"),
        P("pool", None, None, "tensor"),
        P("tensor", None),
        P("pool", None),
        P("pool", None),
        P("pool"),
        P("pool"),
        P("pool", None),
        P("pool", None),
    )
    out_specs = (P(("pool", "tensor"), None), P("pool", None, None, "tensor"))
    return jax.shard_map(
        on_device, mesh=mesh, in_specs=in_specs, out_specs=out_specs, check_vma=False
    )
```

```python
import functools
import math

import jax
import jax.numpy as jnp
from jax import lax
from jax.experimental import pallas as pl
from jax.experimental.pallas import tpu as pltpu
from jax.sharding import PartitionSpec as P

HEAD = 128
CHUNK = 4
NT = (((1,), (1,)), ((), ()))
SMEM = pl.BlockSpec(memory_space=pltpu.SMEM)
VMEM = pl.BlockSpec(memory_space=pltpu.VMEM)
ANY = pl.BlockSpec(memory_space=pl.ANY)


def meta_kernel(dest_owner, dest_slot, evict, owner_ref, block_ref, meta_ref, order_ref):
    pool, entries = meta_ref.shape[0], owner_ref.shape[1]
    owner = jnp.broadcast_to(owner_ref[...], (pool, entries))
    block = jnp.broadcast_to(block_ref[...], (pool, entries))
    row = lax.broadcasted_iota(jnp.int32, (pool, entries), 0)
    col = lax.broadcasted_iota(jnp.int32, (pool, entries), 1)
    match = owner == row
    first = jnp.min(jnp.where(match, col, entries), axis=1, keepdims=True)
    want0 = jnp.sum(jnp.where(match & (col == first), block, 0), axis=1, keepdims=True)
    want1 = jnp.sum(jnp.where(match & (col > first), block, 0), axis=1, keepdims=True)
    place = 2 * row + jnp.where(col > first, 1, 0)
    order_ref[...] = jnp.sum(jnp.where(match, place, 0), axis=0, keepdims=True)
    lane = lax.broadcasted_iota(jnp.int32, (pool, 128), 1)
    out = jnp.where(lane == 0, want0, jnp.where(lane == 1, want1, 0))
    for b in range(4):
        out = jnp.where(lane == 2 + b, dest_owner[0, b], out)
        out = jnp.where(lane == 6 + b, dest_slot[0, b], out)
    out = jnp.where(lane == 10, evict[0], out)
    for o in range(pool):
        meta_ref[o] = out[o : o + 1]


def exchange_table(hist_owner, hist_block, dest_owner, dest_slot, evict, pool):
    return pl.pallas_call(
        meta_kernel,
        out_shape=(
            jax.ShapeDtypeStruct((pool, 1, 128), jnp.int32),
            jax.ShapeDtypeStruct(hist_owner.shape, jnp.int32),
        ),
        in_specs=[SMEM, SMEM, SMEM, VMEM, VMEM],
        out_specs=(VMEM, VMEM),
        name="table",
    )(dest_owner, dest_slot, evict, hist_owner, hist_block)


def split_kernel(x_ref, o_ref):
    row = lax.broadcasted_iota(jnp.int32, (128, 256), 0)
    source = lax.broadcasted_iota(jnp.int32, (128, 256), 1)
    pick_k = jnp.where(source == 2 * row, 1.0, 0.0).astype(jnp.bfloat16)
    pick_v = jnp.where(source == 2 * row + 1, 1.0, 0.0).astype(jnp.bfloat16)
    for b in range(x_ref.shape[0]):
        x = x_ref[b]
        k = jnp.dot(pick_k, x, preferred_element_type=jnp.float32)
        v = jnp.dot(pick_v, x, preferred_element_type=jnp.float32)
        o_ref[b, 0:128, :] = k.astype(jnp.bfloat16)
        o_ref[b, 128:256, :] = v.T.astype(jnp.bfloat16)


def split_blocks(x):
    return pl.pallas_call(
        split_kernel,
        out_shape=jax.ShapeDtypeStruct(x.shape, x.dtype),
        in_specs=[VMEM],
        out_specs=VMEM,
        compiler_params=pltpu.CompilerParams(vmem_limit_bytes=12 * 2**20),
        name=f"split{x.shape[0]}",
    )(x)


def gather_kernel(wanted, pool_ref, pieces_ref, out_ref, sems):
    copies = []
    pool = out_ref.shape[0]
    for p in range(pool):
        for r in range(2):
            copies.append(
                pltpu.make_async_copy(
                    pool_ref.at[wanted[p, 0, r]],
                    out_ref.at[p, pl.ds(256 * r, 256)],
                    sems.at[2 * p + r],
                )
            )
            copies[-1].start()
    copies.append(
        pltpu.make_async_copy(
            pieces_ref, out_ref.at[:, pl.ds(512, pieces_ref.shape[1])], sems.at[2 * pool]
        )
    )
    copies[-1].start()
    for copy in copies:
        copy.wait()


def gather_blocks(wanted, pool_blocks, pieces):
    pool = wanted.shape[0]
    return pl.pallas_call(
        gather_kernel,
        out_shape=jax.ShapeDtypeStruct((pool, 512 + pieces.shape[1], 128), pool_blocks.dtype),
        in_specs=[SMEM, VMEM, VMEM],
        out_specs=ANY,
        scratch_shapes=[pltpu.SemaphoreType.DMA((2 * pool + 1,))],
        name="gather",
    )(wanted, pool_blocks, pieces)


def attend_kernel(
    order, length, base, q_ref, kv_ref, new_ref, mine_ref, theirs_ref, sbuf, *, group, tok
):
    c = math.log2(math.e) / math.sqrt(HEAD)
    heads = q_ref.shape[1] // HEAD
    rows = heads * tok
    new_blocks = new_ref.shape[0]
    new = new_blocks * 128
    parts = base.shape[1]
    part = tok // parts
    q = jnp.concatenate(
        [
            q_ref[pl.ds(pl.multiple_of(base[group, i], part), part), h * HEAD : (h + 1) * HEAD]
            for h in range(heads)
            for i in range(parts)
        ],
        axis=0,
    )

    def scores(k):
        return lax.dot_general(k, q, NT, preferred_element_type=jnp.float32)

    def update(state, s, vt):
        m, l, acc = state
        top = jnp.maximum(m, jnp.max(s, axis=0, keepdims=True))
        p = jnp.exp2(s * c - top * c)
        keep = jnp.exp2((m - top) * c)
        l = l * keep + jnp.sum(p, axis=0, keepdims=True)
        acc = acc * keep + jnp.dot(
            vt, p.astype(jnp.bfloat16), preferred_element_type=jnp.float32
        )
        return top, l, acc

    key = lax.broadcasted_iota(jnp.int32, (new, rows), 0)
    at = lax.broadcasted_iota(jnp.int32, (1, rows), 1) & (tok - 1)
    token = base[group, 0] + at
    for i in range(1, parts):
        token = jnp.where(at >= part * i, base[group, i] + at - part * i, token)
    k_new = jnp.concatenate([new_ref[i, 0:128, :] for i in range(new_blocks)], axis=0)
    vt_new = jnp.concatenate([new_ref[i, 128:256, :] for i in range(new_blocks)], axis=1)
    s = jnp.where(key <= token, scores(k_new), -jnp.inf)
    m = jnp.max(s, axis=0, keepdims=True)
    p = jnp.exp2(s * c - m * c)
    state = (
        m,
        jnp.sum(p, axis=0, keepdims=True),
        jnp.dot(vt_new, p.astype(jnp.bfloat16), preferred_element_type=jnp.float32),
    )

    def half(i, u, value):
        place = order[0, i * CHUNK + u]
        start = pl.multiple_of((place % 2) * 256 + 128 * value, 128)
        return kv_ref[place // 2, pl.ds(start, 128), :]

    def keys_of(i):
        return jnp.concatenate([half(i, u, 0) for u in range(CHUNK)], axis=0)

    def values_of(i):
        return jnp.concatenate([half(i, u, 1) for u in range(CHUNK)], axis=1)

    n = length[0]
    full = n // CHUNK
    last = order.shape[1] // CHUNK - 1
    sbuf[0] = scores(keys_of(0))

    def step(i, state, a):
        sbuf[1 - a] = scores(keys_of(jnp.minimum(i + 1, last)))
        return update(state, sbuf[a], values_of(i))

    state = lax.fori_loop(
        0, full // 2, lambda i, st: step(2 * i + 1, step(2 * i, st, 0), 1), state
    )
    state = lax.fori_loop(full // 2 * 2, full, lambda i, st: step(i, st, 0), state)

    def tail(i, state):
        position = i * (CHUNK * 128) + lax.broadcasted_iota(jnp.int32, (CHUNK * 128, rows), 0)
        s = jnp.where(position < n * 128, scores(keys_of(i)), -jnp.inf)
        return update(state, s, values_of(i))

    m, l, acc = lax.fori_loop(full, (n + CHUNK - 1) // CHUNK, tail, state)
    context = (acc / l).T.astype(jnp.bfloat16)
    own = tok // 2
    for h in range(heads):
        mine_ref[:, h * HEAD : (h + 1) * HEAD] = context[h * tok : h * tok + own]
        theirs_ref[:, h * HEAD : (h + 1) * HEAD] = context[h * tok + own : (h + 1) * tok]


def attend(queries, kv, fresh, order, length, base, group):
    width = queries.shape[1]
    tok = queries.shape[0] // base.shape[0]
    heads = width // HEAD
    out = jax.ShapeDtypeStruct((tok // 2, width), jnp.bfloat16)
    return pl.pallas_call(
        functools.partial(attend_kernel, group=group, tok=tok),
        out_shape=(out, out),
        in_specs=[SMEM, SMEM, SMEM, VMEM, VMEM, VMEM],
        out_specs=(VMEM, VMEM),
        scratch_shapes=[pltpu.VMEM((2, CHUNK * 128, heads * tok), jnp.float32)],
        compiler_params=pltpu.CompilerParams(vmem_limit_bytes=16 * 2**20),
        cost_estimate=pl.CostEstimate(
            flops=tok * heads * 8704 * 128 * 4, bytes_accessed=5 * 2**20, transcendentals=0
        ),
        name=f"attend{group}",
    )(order, length, base, queries, kv, fresh)


def project_kernel(a_ref, b_ref, wa_ref, wb_ref, *refs):
    arrived, (up_ref, down_ref) = refs[:-2], refs[-2:]
    half = a_ref.shape[0] // 2
    tile = 512
    for j in range(wa_ref.shape[1] // tile):
        cols = slice(j * tile, (j + 1) * tile)
        total = jnp.dot(a_ref[...], wa_ref[:, cols], preferred_element_type=jnp.float32)
        total += jnp.dot(b_ref[...], wb_ref[:, cols], preferred_element_type=jnp.float32)
        up, down = total[:half], total[half:]
        if arrived:
            up += arrived[0][:, cols].astype(jnp.float32)
            down += arrived[1][:, cols].astype(jnp.float32)
        up_ref[:, cols] = up.astype(jnp.bfloat16)
        down_ref[:, cols] = down.astype(jnp.bfloat16)


def project(a, b, wa, wb, *arrived):
    out = jax.ShapeDtypeStruct((a.shape[0] // 2, wa.shape[1]), jnp.bfloat16)
    return pl.pallas_call(
        project_kernel,
        out_shape=(out, out),
        in_specs=[VMEM] * (4 + len(arrived)),
        out_specs=(VMEM, VMEM),
        cost_estimate=pl.CostEstimate(
            flops=4 * a.size * wa.shape[1], bytes_accessed=11 * 2**20, transcendentals=0
        ),
        name=f"project{len(arrived)}",
    )(a, b, wa, wb, *arrived)


def copy_kernel(x_ref, o_ref, buf, sem):
    for source, target in ((x_ref, buf), (buf, o_ref)):
        copy = pltpu.make_async_copy(source, target, sem)
        copy.start()
        copy.wait()


def copy_pool(x):
    return pl.pallas_call(
        copy_kernel,
        out_shape=jax.ShapeDtypeStruct(x.shape, x.dtype),
        in_specs=[ANY],
        out_specs=ANY,
        scratch_shapes=[pltpu.VMEM(x.shape, x.dtype), pltpu.SemaphoreType.DMA],
        name="copy_pool",
    )(x)


def write_kernel(slots, fresh_ref, kept_ref, out_ref, sems):
    del kept_ref
    for b in range(fresh_ref.shape[0]):

        @pl.when(slots[b] >= 0)
        def _(b=b):
            copy = pltpu.make_async_copy(fresh_ref.at[b], out_ref.at[slots[b]], sems.at[b])
            copy.start()
            copy.wait()


def write_back(slots, fresh, kept):
    return pl.pallas_call(
        write_kernel,
        out_shape=jax.ShapeDtypeStruct(kept.shape, kept.dtype),
        in_specs=[SMEM, VMEM, ANY],
        out_specs=ANY,
        input_output_aliases={2: 0},
        scratch_shapes=[pltpu.SemaphoreType.DMA((fresh.shape[0],))],
        name="write",
    )(slots, fresh, kept)


def swap_pool(x):
    return lax.all_to_all(x, "pool", split_axis=0, concat_axis=0, tiled=True)


def on_device(
    queries,
    new_key_value,
    saved,
    out_weight,
    hist_owner,
    hist_block,
    hist_len,
    evict,
    dest_owner,
    dest_slot,
):
    pool = lax.axis_size("pool")
    me = lax.axis_index("pool")
    chips = lax.axis_size("tensor") // 2
    chip, core = lax.axis_index("tensor") // 2, lax.axis_index("tensor") % 2
    other_core = [(2 * z + c, 2 * z + 1 - c) for z in range(chips) for c in range(2)]
    upward = [(2 * z + c, 2 * ((z + 1) % chips) + c) for z in range(chips) for c in range(2)]
    downward = [(target, source) for source, target in upward]
    swap = functools.partial(lax.ppermute, axis_name="tensor", perm=other_core)
    send_up = functools.partial(lax.ppermute, axis_name="tensor", perm=upward)
    send_down = functools.partial(lax.ppermute, axis_name="tensor", perm=downward)

    def part(offset, c, half):
        return 128 * ((chip + offset) % chips) + 64 * c + 32 * half

    plan = (((2, 0), (2, 1)), ((1, 1), (3, 0)), ((1, 0), (3, 1)), ((0, 0), (0, 1)))
    base = jnp.stack(
        [
            jnp.stack([part(o, c, h) for c in (core, 1 - core) for o, h in parts])
            for parts in plan
        ]
    ).astype(jnp.int32)

    table, order = exchange_table(hist_owner, hist_block, dest_owner, dest_slot, evict, pool)
    told = swap_pool(table)
    pool_blocks = split_blocks(saved.reshape(-1, 256, 128))
    fresh = split_blocks(new_key_value.reshape(-1, 256, 128))
    pieces = new_key_value.reshape(4, pool, 8, 128).transpose(1, 0, 2, 3).reshape(pool, 32, 128)
    kv = swap_pool(gather_blocks(told, pool_blocks, pieces))
    other_weight = swap(out_weight)
    kept = copy_pool(saved.reshape(-1, 256, 128))

    def contexts(group, after):
        first, _ = lax.optimization_barrier((order, after))
        mine, theirs = attend(queries, kv, fresh, first, hist_len, base, group)
        return mine, swap(theirs)

    up, down = project(*contexts(0, order), out_weight, other_weight)
    through_up, through_down = send_up(up), send_down(down)
    up, down = project(*contexts(1, up), out_weight, other_weight)
    near_up, near_down = send_up(up), send_down(down)
    up, down = project(*contexts(2, up), out_weight, other_weight, through_up, through_down)
    far_up, far_down = send_up(up), send_down(down)

    held, _ = lax.optimization_barrier((kv[:, 512:], up))
    held = held.reshape(pool, 4, -1)
    targets = told[:, 0, 2:6]
    chosen = targets.T[:, None, :] == jnp.arange(pool, dtype=jnp.int32)[None, :, None]
    onward = jnp.einsum(
        "bop,pbx->obx", chosen.astype(jnp.bfloat16), held, preferred_element_type=jnp.float32
    ).astype(jnp.bfloat16)
    returned = swap_pool(onward).reshape(pool, 4, 8, 128).transpose(1, 0, 2, 3)
    mine = (targets == me) & (told[:, 0, 10:11] > 0)
    slots = jnp.max(jnp.where(mine, told[:, 0, 6:10], -1), axis=0)

    top, bottom = project(*contexts(3, up), out_weight, other_weight)
    pool_out = write_back(slots, returned.reshape(4, 256, 128), kept).reshape(saved.shape)
    wide = lambda x: x.astype(jnp.float32)
    attn_out = jnp.concatenate(
        [
            wide(top) + wide(far_up) + wide(near_down),
            wide(bottom) + wide(near_up) + wide(far_down),
        ]
    ).astype(jnp.bfloat16)
    return attn_out, pool_out


def solution(mesh):
    in_specs = (
        P("pool", "tensor"),
        P("pool", None, "tensor"),
        P("pool", None, None, "tensor"),
        P("tensor", None),
        P("pool", None),
        P("pool", None),
        P("pool"),
        P("pool"),
        P("pool", None),
        P("pool", None),
    )
    out_specs = (P(("pool", "tensor"), None), P("pool", None, None, "tensor"))
    return jax.shard_map(
        on_device, mesh=mesh, in_specs=in_specs, out_specs=out_specs, check_vma=False
    )
```

```python
import functools
import math

import jax
import jax.numpy as jnp
from jax import lax
from jax.experimental import pallas as pl
from jax.experimental.pallas import tpu as pltpu
from jax.sharding import PartitionSpec as P

HEAD = 128
CHUNK = 4
NT = (((1,), (1,)), ((), ()))
SMEM = pl.BlockSpec(memory_space=pltpu.SMEM)
VMEM = pl.BlockSpec(memory_space=pltpu.VMEM)
ANY = pl.BlockSpec(memory_space=pl.ANY)
HBM = pl.BlockSpec(memory_space=pltpu.HBM)


def limit(mebibytes):
    return pltpu.CompilerParams(vmem_limit_bytes=mebibytes * 2**20)


def meta_kernel(
    dest_owner, dest_slot, evict, owner_ref, block_ref, pieces_ref, meta_ref, order_ref
):
    pool, entries = meta_ref.shape[0], owner_ref.shape[1]
    owner = jnp.broadcast_to(owner_ref[...], (pool, entries))
    block = jnp.broadcast_to(block_ref[...], (pool, entries))
    row = lax.broadcasted_iota(jnp.int32, (pool, entries), 0)
    col = lax.broadcasted_iota(jnp.int32, (pool, entries), 1)
    match = owner == row
    first = jnp.min(jnp.where(match, col, entries), axis=1, keepdims=True)
    want0 = jnp.sum(jnp.where(match & (col == first), block, 0), axis=1, keepdims=True)
    want1 = jnp.sum(jnp.where(match & (col > first), block, 0), axis=1, keepdims=True)
    place = 2 * row + jnp.where(col > first, 1, 0)
    order_ref[...] = jnp.sum(jnp.where(match, place, 0), axis=0, keepdims=True)
    lane = lax.broadcasted_iota(jnp.int32, (pool, 128), 1)
    out = jnp.where(lane == 0, want0, jnp.where(lane == 1, want1, 0))
    for b in range(4):
        out = jnp.where(lane == 2 + b, dest_owner[0, b], out)
        out = jnp.where(lane == 6 + b, dest_slot[0, b], out)
    out = jnp.where(lane == 10, evict[0], out)
    for o in range(pool):
        meta_ref[o, 0 : pieces_ref.shape[1], :] = pieces_ref[o]
        meta_ref[o, pieces_ref.shape[1] :, :] = jnp.broadcast_to(
            out[o : o + 1].astype(jnp.float32), (16, 128)
        ).astype(jnp.bfloat16)


def exchange_table(hist_owner, hist_block, dest_owner, dest_slot, evict, pieces):
    pool, rows, _ = pieces.shape
    return pl.pallas_call(
        meta_kernel,
        out_shape=(
            jax.ShapeDtypeStruct((pool, rows + 16, 128), jnp.bfloat16),
            jax.ShapeDtypeStruct(hist_owner.shape, jnp.int32),
        ),
        in_specs=[SMEM, SMEM, SMEM, VMEM, VMEM, VMEM],
        out_specs=(VMEM, VMEM),
        compiler_params=limit(4),
        name="table",
    )(dest_owner, dest_slot, evict, hist_owner, hist_block, pieces)


def split_kernel(x_ref, o_ref):
    row = lax.broadcasted_iota(jnp.int32, (128, 256), 0)
    source = lax.broadcasted_iota(jnp.int32, (128, 256), 1)
    pick_k = jnp.where(source == 2 * row, 1.0, 0.0).astype(jnp.bfloat16)
    pick_v = jnp.where(source == 2 * row + 1, 1.0, 0.0).astype(jnp.bfloat16)
    for b in range(x_ref.shape[0]):
        x = x_ref[b]
        k = jnp.dot(pick_k, x, preferred_element_type=jnp.float32)
        v = jnp.dot(pick_v, x, preferred_element_type=jnp.float32)
        o_ref[b, 0:128, :] = k.astype(jnp.bfloat16)
        o_ref[b, 128:256, :] = v.T.astype(jnp.bfloat16)


def split_blocks(x):
    return pl.pallas_call(
        split_kernel,
        out_shape=jax.ShapeDtypeStruct(x.shape, x.dtype),
        in_specs=[VMEM],
        out_specs=VMEM,
        compiler_params=limit(12),
        name=f"split{x.shape[0]}",
    )(x)


def gather_kernel(told, pool_ref, held_ref, out_ref, held, onward, packed, sems):
    pool, rows = packed.shape[:2]
    copies = []
    for p in range(pool):
        for r in range(2):
            copies.append(
                pltpu.make_async_copy(
                    pool_ref.at[told[p, r]], out_ref.at[p, pl.ds(256 * r, 256)], sems.at[2 * p + r]
                )
            )
            copies[-1].start()
    held[...] = held_ref[...].astype(jnp.float32)
    for b in range(4):
        for p in range(pool):
            onward[told[p, 2 + b], 8 * b : 8 * b + 8, :] = held[p, 8 * b : 8 * b + 8, :]
    packed[...] = onward[...].astype(jnp.bfloat16)
    copies.append(
        pltpu.make_async_copy(packed, out_ref.at[:, pl.ds(512, rows)], sems.at[2 * pool])
    )
    copies[-1].start()
    for copy in copies:
        copy.wait()


def gather_blocks(told, pool_blocks, held):
    pool, rows, _ = held.shape
    return pl.pallas_call(
        gather_kernel,
        out_shape=jax.ShapeDtypeStruct((pool, 512 + rows, 128), pool_blocks.dtype),
        in_specs=[SMEM, VMEM, VMEM],
        out_specs=HBM,
        scratch_shapes=[
            pltpu.VMEM(held.shape, jnp.float32),
            pltpu.VMEM(held.shape, jnp.float32),
            pltpu.VMEM(held.shape, jnp.bfloat16),
            pltpu.SemaphoreType.DMA((2 * pool + 1,)),
        ],
        compiler_params=limit(51),
        name="gather",
    )(told, pool_blocks, held)


def attend_kernel(
    order, length, base, q_ref, new_ref, kv_any, mine_ref, theirs_ref, sbuf, kv_ref, sem, *, group, tok
):
    fetch = pltpu.make_async_copy(kv_any.at[:, pl.ds(0, kv_ref.shape[1])], kv_ref, sem)
    fetch.start()
    c = math.log2(math.e) / math.sqrt(HEAD)
    heads = q_ref.shape[1] // HEAD
    rows = heads * tok
    new_blocks = new_ref.shape[0]
    new = new_blocks * 128
    parts = base.shape[1]
    part = tok // parts
    q = jnp.concatenate(
        [
            q_ref[pl.ds(pl.multiple_of(base[group, i], part), part), h * HEAD : (h + 1) * HEAD]
            for h in range(heads)
            for i in range(parts)
        ],
        axis=0,
    )

    def scores(k):
        return lax.dot_general(k, q, NT, preferred_element_type=jnp.float32)

    def update(state, s, vt):
        m, l, acc = state
        top = jnp.maximum(m, jnp.max(s, axis=0, keepdims=True))
        p = jnp.exp2(s * c - top * c)
        keep = jnp.exp2((m - top) * c)
        l = l * keep + jnp.sum(p, axis=0, keepdims=True)
        acc = acc * keep + jnp.dot(
            vt, p.astype(jnp.bfloat16), preferred_element_type=jnp.float32
        )
        return top, l, acc

    key = lax.broadcasted_iota(jnp.int32, (new, rows), 0)
    at = lax.broadcasted_iota(jnp.int32, (1, rows), 1) & (tok - 1)
    token = base[group, 0] + at
    for i in range(1, parts):
        token = jnp.where(at >= part * i, base[group, i] + at - part * i, token)
    k_new = jnp.concatenate([new_ref[i, 0:128, :] for i in range(new_blocks)], axis=0)
    vt_new = jnp.concatenate([new_ref[i, 128:256, :] for i in range(new_blocks)], axis=1)
    s = jnp.where(key <= token, scores(k_new), -jnp.inf)
    m = jnp.max(s, axis=0, keepdims=True)
    p = jnp.exp2(s * c - m * c)
    state = (
        m,
        jnp.sum(p, axis=0, keepdims=True),
        jnp.dot(vt_new, p.astype(jnp.bfloat16), preferred_element_type=jnp.float32),
    )

    def half(i, u, value):
        place = order[0, i * CHUNK + u]
        start = pl.multiple_of((place % 2) * 256 + 128 * value, 128)
        return kv_ref[place // 2, pl.ds(start, 128), :]

    def keys_of(i):
        return jnp.concatenate([half(i, u, 0) for u in range(CHUNK)], axis=0)

    def values_of(i):
        return jnp.concatenate([half(i, u, 1) for u in range(CHUNK)], axis=1)

    n = length[0]
    full = n // CHUNK
    last = order.shape[1] // CHUNK - 1
    fetch.wait()
    sbuf[0] = scores(keys_of(0))

    def step(i, state, a):
        sbuf[1 - a] = scores(keys_of(jnp.minimum(i + 1, last)))
        return update(state, sbuf[a], values_of(i))

    state = lax.fori_loop(
        0, full // 2, lambda i, st: step(2 * i + 1, step(2 * i, st, 0), 1), state
    )
    state = lax.fori_loop(full // 2 * 2, full, lambda i, st: step(i, st, 0), state)

    def tail(i, state):
        position = i * (CHUNK * 128) + lax.broadcasted_iota(jnp.int32, (CHUNK * 128, rows), 0)
        s = jnp.where(position < n * 128, scores(keys_of(i)), -jnp.inf)
        return update(state, s, values_of(i))

    m, l, acc = lax.fori_loop(full, (n + CHUNK - 1) // CHUNK, tail, state)
    context = (acc / l).T.astype(jnp.bfloat16)
    own = tok // 2
    for h in range(heads):
        mine_ref[:, h * HEAD : (h + 1) * HEAD] = context[h * tok : h * tok + own]
        theirs_ref[:, h * HEAD : (h + 1) * HEAD] = context[h * tok + own : (h + 1) * tok]


def attend(queries, kv, fresh, order, length, base, group):
    width = queries.shape[1]
    tok = queries.shape[0] // base.shape[0]
    heads = width // HEAD
    out = jax.ShapeDtypeStruct((tok // 2, width), jnp.bfloat16)
    return pl.pallas_call(
        functools.partial(attend_kernel, group=group, tok=tok),
        out_shape=(out, out),
        in_specs=[SMEM, SMEM, SMEM, VMEM, VMEM, HBM],
        out_specs=(VMEM, VMEM),
        scratch_shapes=[
            pltpu.VMEM((2, CHUNK * 128, heads * tok), jnp.float32),
            pltpu.VMEM((kv.shape[0], 512, 128), kv.dtype),
            pltpu.SemaphoreType.DMA,
        ],
        compiler_params=limit(16),
        name=f"attend{group}",
    )(order, length, base, queries, fresh, kv)


def project_kernel(a_ref, b_ref, *refs, arriving):
    arrived, (wa_any, wb_any, up_ref, down_ref, wa_ref, wb_ref, sems) = (
        refs[:arriving],
        refs[arriving:],
    )
    half = a_ref.shape[0] // 2
    tiles = sems.shape[0]
    tile = wa_ref.shape[1] // tiles
    copies = []
    for j in range(tiles):
        cols = pl.ds(j * tile, tile)
        copies.append(
            (
                pltpu.make_async_copy(wa_any.at[:, cols], wa_ref.at[:, cols], sems.at[j, 0]),
                pltpu.make_async_copy(wb_any.at[:, cols], wb_ref.at[:, cols], sems.at[j, 1]),
            )
        )
        for copy in copies[-1]:
            copy.start()
    for j in range(tiles):
        cols = slice(j * tile, (j + 1) * tile)
        for copy in copies[j]:
            copy.wait()
        total = jnp.dot(a_ref[...], wa_ref[:, cols], preferred_element_type=jnp.float32)
        total += jnp.dot(b_ref[...], wb_ref[:, cols], preferred_element_type=jnp.float32)
        up, down = total[:half], total[half:]
        if arrived:
            up += arrived[0][:, cols].astype(jnp.float32)
            down += arrived[1][:, cols].astype(jnp.float32)
        up_ref[:, cols] = up.astype(jnp.bfloat16)
        down_ref[:, cols] = down.astype(jnp.bfloat16)


def project(a, b, wa, wb, *arrived):
    out = jax.ShapeDtypeStruct((a.shape[0] // 2, wa.shape[1]), jnp.bfloat16)
    return pl.pallas_call(
        functools.partial(project_kernel, arriving=len(arrived)),
        out_shape=(out, out),
        in_specs=[VMEM] * (2 + len(arrived)) + [HBM, HBM],
        out_specs=(VMEM, VMEM),
        scratch_shapes=[
            pltpu.VMEM(wa.shape, wa.dtype),
            pltpu.VMEM(wb.shape, wb.dtype),
            pltpu.SemaphoreType.DMA((10, 2)),
        ],
        compiler_params=limit(52),
        name=f"project{len(arrived)}",
    )(a, b, *arrived, wa, wb)


def combine_kernel(top, bottom, far_up, near_down, near_up, far_down, o_ref):
    half = top.shape[0]
    for rows, parts in ((0, (top, far_up, near_down)), (half, (bottom, near_up, far_down))):
        total = sum(part[...].astype(jnp.float32) for part in parts)
        o_ref[rows : rows + half, :] = total.astype(jnp.bfloat16)


def combine(*parts):
    rows, width = parts[0].shape
    return pl.pallas_call(
        combine_kernel,
        out_shape=jax.ShapeDtypeStruct((2 * rows, width), jnp.bfloat16),
        in_specs=[VMEM] * 6,
        out_specs=VMEM,
        compiler_params=limit(8),
        name="combine",
    )(*parts)


def copy_kernel(x_ref, o_ref, buf, sem):
    for source, target in ((x_ref, buf), (buf, o_ref)):
        copy = pltpu.make_async_copy(source, target, sem)
        copy.start()
        copy.wait()


def copy_pool(x):
    return pl.pallas_call(
        copy_kernel,
        out_shape=jax.ShapeDtypeStruct(x.shape, x.dtype),
        in_specs=[HBM],
        out_specs=HBM,
        scratch_shapes=[pltpu.VMEM(x.shape, x.dtype), pltpu.SemaphoreType.DMA],
        compiler_params=limit(4),
        name="copy_pool",
    )(x)


def write_kernel(slots, fresh_ref, kept_ref, out_ref, sems):
    del kept_ref
    for b in range(fresh_ref.shape[0]):

        @pl.when(slots[b] >= 0)
        def _(b=b):
            copy = pltpu.make_async_copy(fresh_ref.at[b], out_ref.at[slots[b]], sems.at[b])
            copy.start()
            copy.wait()


def write_back(slots, fresh, kept):
    return pl.pallas_call(
        write_kernel,
        out_shape=jax.ShapeDtypeStruct(kept.shape, kept.dtype),
        in_specs=[SMEM, VMEM, ANY],
        out_specs=ANY,
        input_output_aliases={2: 0},
        scratch_shapes=[pltpu.SemaphoreType.DMA((fresh.shape[0],))],
        compiler_params=limit(4),
        name="write",
    )(slots, fresh, kept)


def swap_pool(x):
    return lax.all_to_all(x, "pool", split_axis=0, concat_axis=0, tiled=True)


def on_device(
    queries,
    new_key_value,
    saved,
    out_weight,
    hist_owner,
    hist_block,
    hist_len,
    evict,
    dest_owner,
    dest_slot,
):
    pool = lax.axis_size("pool")
    me = lax.axis_index("pool")
    chips = lax.axis_size("tensor") // 2
    chip, core = lax.axis_index("tensor") // 2, lax.axis_index("tensor") % 2
    other_core = [(2 * z + c, 2 * z + 1 - c) for z in range(chips) for c in range(2)]
    upward = [(2 * z + c, 2 * ((z + 1) % chips) + c) for z in range(chips) for c in range(2)]
    downward = [(target, source) for source, target in upward]
    swap = functools.partial(lax.ppermute, axis_name="tensor", perm=other_core)
    send_up = functools.partial(lax.ppermute, axis_name="tensor", perm=upward)
    send_down = functools.partial(lax.ppermute, axis_name="tensor", perm=downward)

    def part(offset, c, half):
        return 128 * ((chip + offset) % chips) + 64 * c + 32 * half

    plan = (((2, 0), (2, 1)), ((1, 1), (3, 0)), ((1, 0), (3, 1)), ((0, 0), (0, 1)))
    base = jnp.stack(
        [
            jnp.stack([part(o, c, h) for c in (core, 1 - core) for o, h in parts])
            for parts in plan
        ]
    ).astype(jnp.int32)

    pieces = new_key_value.reshape(4, pool, 8, 128).transpose(1, 0, 2, 3).reshape(pool, 32, 128)
    table, order = exchange_table(hist_owner, hist_block, dest_owner, dest_slot, evict, pieces)
    arrived = swap_pool(table)
    pool_blocks = split_blocks(saved.reshape(-1, 256, 128))
    fresh = split_blocks(new_key_value.reshape(-1, 256, 128))
    told = arrived[:, 32, :].astype(jnp.int32)
    kv = swap_pool(gather_blocks(told, pool_blocks, arrived[:, :32]))
    other_weight = swap(out_weight)
    kept = copy_pool(saved.reshape(-1, 256, 128))

    def contexts(group, after):
        first, _ = lax.optimization_barrier((order, after))
        mine, theirs = attend(queries, kv, fresh, first, hist_len, base, group)
        return mine, swap(theirs)

    up, down = project(*contexts(0, kept), out_weight, other_weight)
    through_up, through_down = send_up(up), send_down(down)
    up, down = project(*contexts(1, up), out_weight, other_weight)
    near_up, near_down = send_up(up), send_down(down)
    up, down = project(*contexts(2, up), out_weight, other_weight, through_up, through_down)
    far_up, far_down = send_up(up), send_down(down)

    returned = kv[:, 512:].reshape(pool, 4, 8, 128).transpose(1, 0, 2, 3)
    mine = (told[:, 2:6] == me) & (told[:, 10:11] > 0)
    slots = jnp.max(jnp.where(mine, told[:, 6:10], -1), axis=0)
    top, bottom = project(*contexts(3, (near_up, near_down)), out_weight, other_weight)
    pool_out = write_back(slots, returned.reshape(4, 256, 128), kept).reshape(saved.shape)
    attn_out = combine(top, bottom, far_up, near_down, near_up, far_down)
    return attn_out, pool_out


def solution(mesh):
    in_specs = (
        P("pool", "tensor"),
        P("pool", None, "tensor"),
        P("pool", None, None, "tensor"),
        P("tensor", None),
        P("pool", None),
        P("pool", None),
        P("pool"),
        P("pool"),
        P("pool", None),
        P("pool", None),
    )
    out_specs = (P(("pool", "tensor"), None), P("pool", None, None, "tensor"))
    return jax.shard_map(
        on_device, mesh=mesh, in_specs=in_specs, out_specs=out_specs, check_vma=False
    )
```

```python
import functools
import math

import jax
import jax.numpy as jnp
from jax import lax
from jax.experimental import pallas as pl
from jax.experimental.pallas import tpu as pltpu
from jax.sharding import PartitionSpec as P

HEAD = 128
CHUNK = 4
NT = (((1,), (1,)), ((), ()))
SMEM = pl.BlockSpec(memory_space=pltpu.SMEM)
VMEM = pl.BlockSpec(memory_space=pltpu.VMEM)
ANY = pl.BlockSpec(memory_space=pl.ANY)
HBM = pl.BlockSpec(memory_space=pltpu.HBM)


def limit(mebibytes):
    return pltpu.CompilerParams(vmem_limit_bytes=mebibytes * 2**20)


def table_kernel(
    length, dest_owner, dest_slot, evict, owner_ref, block_ref, new_ref, table_ref, list_ref, rows_ref
):
    pool, entries = table_ref.shape[0], owner_ref.shape[1]
    owner = jnp.broadcast_to(owner_ref[...], (pool, entries))
    block = jnp.broadcast_to(block_ref[...], (pool, entries))
    row = lax.broadcasted_iota(jnp.int32, (pool, entries), 0)
    col = lax.broadcasted_iota(jnp.int32, (pool, entries), 1)
    match = owner == row
    first = jnp.min(jnp.where(match, col, entries), axis=1, keepdims=True)
    second = jnp.max(jnp.where(match, col, -1), axis=1, keepdims=True)
    want0 = jnp.sum(jnp.where(match & (col == first), block, 0), axis=1, keepdims=True)
    want1 = jnp.sum(jnp.where(match & (col == second), block, 0), axis=1, keepdims=True)
    row = lax.broadcasted_iota(jnp.int32, (pool, 128), 0)
    lane = lax.broadcasted_iota(jnp.int32, (pool, 128), 1)
    used0 = jnp.where(jnp.broadcast_to(first, (pool, 128)) < length[0], 1, 0)
    used1 = jnp.where(jnp.broadcast_to(second, (pool, 128)) < length[0], 1, 0)
    used = (used0 + used1).astype(jnp.float32)
    earlier = jnp.where(
        lax.broadcasted_iota(jnp.int32, (pool, pool), 1)
        < lax.broadcasted_iota(jnp.int32, (pool, pool), 0),
        1.0,
        0.0,
    )
    before = jnp.dot(earlier, used, preferred_element_type=jnp.float32).astype(jnp.int32)
    place = jnp.where((used0 > 0) & (before == lane), 2 * row, 0)
    place += jnp.where((used1 > 0) & (before + used0 == lane), 2 * row + 1, 0)
    quarter = pool // 4
    counts = jnp.where(row < quarter * (lane + 1), used0 + used1, 0)
    list_ref[...] = jnp.zeros(list_ref.shape, jnp.int32)
    list_ref[0:1] = jnp.sum(place, axis=0, keepdims=True)
    list_ref[1:2] = jnp.sum(counts, axis=0, keepdims=True)

    out = jnp.where(lane == 0, want0, jnp.where(lane == 1, want1, 0))
    for b in range(4):
        out = jnp.where(lane == 2 + b, dest_owner[0, b], out)
        out = jnp.where(lane == 6 + b, dest_slot[0, b], out)
    out = jnp.where(lane == 10, evict[0], out).astype(jnp.float32)
    for b in range(4):
        fresh = new_ref[b].astype(jnp.float32)
        for o in range(pool):
            rows_ref[o, 8 * b : 8 * b + 8, :] = fresh[8 * o : 8 * o + 8]
    for o in range(pool):
        rows_ref[o, 32:48, :] = jnp.broadcast_to(out[o : o + 1], (16, 128))
    table_ref[...] = rows_ref[...].astype(jnp.bfloat16)


def exchange_table(hist_owner, hist_block, hist_len, dest_owner, dest_slot, evict, new_blocks, pool):
    return pl.pallas_call(
        table_kernel,
        out_shape=(
            jax.ShapeDtypeStruct((pool, 48, 128), jnp.bfloat16),
            jax.ShapeDtypeStruct((8, 128), jnp.int32),
        ),
        in_specs=[SMEM, SMEM, SMEM, SMEM, VMEM, VMEM, VMEM],
        out_specs=(VMEM, VMEM),
        scratch_shapes=[pltpu.VMEM((pool, 48, 128), jnp.float32)],
        compiler_params=limit(58),
        name="table",
    )(hist_len, dest_owner, dest_slot, evict, hist_owner, hist_block, new_blocks)


def split_kernel(x_ref, o_ref):
    row = lax.broadcasted_iota(jnp.int32, (128, 256), 0)
    source = lax.broadcasted_iota(jnp.int32, (128, 256), 1)
    pick_k = jnp.where(source == 2 * row, 1.0, 0.0).astype(jnp.bfloat16)
    pick_v = jnp.where(source == 2 * row + 1, 1.0, 0.0).astype(jnp.bfloat16)
    for b in range(x_ref.shape[0]):
        x = x_ref[b]
        k = jnp.dot(pick_k, x, preferred_element_type=jnp.float32)
        v = jnp.dot(pick_v, x, preferred_element_type=jnp.float32)
        o_ref[b, 0:128, :] = k.astype(jnp.bfloat16)
        o_ref[b, 128:256, :] = v.T.astype(jnp.bfloat16)


def split_blocks(x):
    return pl.pallas_call(
        split_kernel,
        out_shape=jax.ShapeDtypeStruct(x.shape, x.dtype),
        in_specs=[VMEM],
        out_specs=VMEM,
        compiler_params=limit(12),
        name=f"split{x.shape[0]}",
    )(x)


def gather_kernel(told, pool_ref, held_ref, out_ref, held, onward, packed, sems):
    pool, rows = packed.shape[:2]
    copies = []
    for p in range(pool):
        for r in range(2):
            copies.append(
                pltpu.make_async_copy(
                    pool_ref.at[told[p, r]], out_ref.at[p, pl.ds(256 * r, 256)], sems.at[2 * p + r]
                )
            )
            copies[-1].start()
    held[...] = held_ref[...].astype(jnp.float32)
    for b in range(4):
        for p in range(pool):
            onward[told[p, 2 + b], 8 * b : 8 * b + 8, :] = held[p, 8 * b : 8 * b + 8, :]
    packed[...] = onward[...].astype(jnp.bfloat16)
    copies.append(
        pltpu.make_async_copy(packed, out_ref.at[:, pl.ds(512, rows)], sems.at[2 * pool])
    )
    copies[-1].start()
    for copy in copies:
        copy.wait()


def gather_blocks(told, pool_blocks, held):
    pool, rows, _ = held.shape
    return pl.pallas_call(
        gather_kernel,
        out_shape=jax.ShapeDtypeStruct((pool, 512 + rows, 128), pool_blocks.dtype),
        in_specs=[SMEM, VMEM, VMEM],
        out_specs=HBM,
        scratch_shapes=[
            pltpu.VMEM(held.shape, jnp.float32),
            pltpu.VMEM(held.shape, jnp.float32),
            pltpu.VMEM(held.shape, jnp.bfloat16),
            pltpu.SemaphoreType.DMA((2 * pool + 1,)),
        ],
        compiler_params=limit(51),
        name="gather",
    )(told, pool_blocks, held)


def accumulate(state, s, vt):
    m, l, acc = state
    c = math.log2(math.e) / math.sqrt(HEAD)
    top = jnp.maximum(m, jnp.max(s, axis=0, keepdims=True))
    p = jnp.exp2(s * c - top * c)
    keep = jnp.exp2((m - top) * c)
    l = l * keep + jnp.sum(p, axis=0, keepdims=True)
    acc = acc * keep + jnp.dot(vt, p.astype(jnp.bfloat16), preferred_element_type=jnp.float32)
    return top, l, acc


def begin_kernel(base, q_ref, new_ref, *refs):
    c = math.log2(math.e) / math.sqrt(HEAD)
    groups, parts = base.shape
    heads = q_ref.shape[1] // HEAD
    tok = q_ref.shape[0] // groups
    rows = heads * tok
    part = tok // parts
    blocks = new_ref.shape[0]
    k = jnp.concatenate([new_ref[i, 0:128, :] for i in range(blocks)], axis=0)
    vt = jnp.concatenate([new_ref[i, 128:256, :] for i in range(blocks)], axis=1)
    key = lax.broadcasted_iota(jnp.int32, (blocks * 128, rows), 0)
    at = lax.broadcasted_iota(jnp.int32, (1, rows), 1) & (tok - 1)
    for group in range(groups):
        out_q, out_m, out_l, out_acc = refs[4 * group : 4 * group + 4]
        token = base[group, 0] + at
        for i in range(1, parts):
            token = jnp.where(at >= part * i, base[group, i] + at - part * i, token)
        for h in range(heads):
            for i in range(parts):
                first = pl.multiple_of(base[group, i], part)
                out_q[pl.ds(h * tok + i * part, part), :] = q_ref[
                    pl.ds(first, part), h * HEAD : (h + 1) * HEAD
                ]
        s = lax.dot_general(k, out_q[...], NT, preferred_element_type=jnp.float32)
        s = jnp.where(key <= token, s, -jnp.inf)
        m = jnp.max(s, axis=0, keepdims=True)
        p = jnp.exp2(s * c - m * c)
        out_m[...] = m
        out_l[...] = jnp.sum(p, axis=0, keepdims=True)
        out_acc[...] = jnp.dot(vt, p.astype(jnp.bfloat16), preferred_element_type=jnp.float32)


def begin(queries, fresh, base):
    groups = base.shape[0]
    rows = queries.size // (groups * HEAD)
    one = (
        jax.ShapeDtypeStruct((rows, HEAD), queries.dtype),
        jax.ShapeDtypeStruct((1, rows), jnp.float32),
        jax.ShapeDtypeStruct((1, rows), jnp.float32),
        jax.ShapeDtypeStruct((HEAD, rows), jnp.float32),
    )
    out = pl.pallas_call(
        begin_kernel,
        out_shape=one * groups,
        in_specs=[SMEM, VMEM, VMEM],
        out_specs=(VMEM,) * (4 * groups),
        compiler_params=limit(24),
        name="begin",
    )(base, queries, fresh)
    return [out[4 * g : 4 * g + 4] for g in range(groups)]


def attend_kernel(
    blocks, length, q_ref, m_ref, l_ref, acc_ref, kv_any, mine_ref, theirs_ref, sbuf, kv_ref, sems
):
    quarters = sems.shape[0]
    share = kv_ref.shape[0] // quarters

    def quarter(k):
        owners = pl.ds(pl.multiple_of(k * share, share), share)
        return pltpu.make_async_copy(
            kv_any.at[owners, pl.ds(0, kv_ref.shape[1])], kv_ref.at[owners], sems.at[k]
        )

    def wait(k, _):
        quarter(k).wait()
        return 0

    for k in range(quarters):
        quarter(k).start()
    rows = q_ref.shape[0]
    tok = mine_ref.shape[0] * 2
    heads = rows // tok
    q = q_ref[...]

    def half(i, u, value):
        place = blocks[0, i * CHUNK + u]
        start = pl.multiple_of((place % 2) * 256 + 128 * value, 128)
        return kv_ref[place // 2, pl.ds(start, 128), :]

    def values_of(i):
        return jnp.concatenate([half(i, u, 1) for u in range(CHUNK)], axis=1)

    def scores(i):
        keys = jnp.concatenate([half(i, u, 0) for u in range(CHUNK)], axis=0)
        return lax.dot_general(keys, q, NT, preferred_element_type=jnp.float32)

    n = length[0]
    full = n // CHUNK
    last = 2 * kv_ref.shape[0] // CHUNK - 1
    opening = sum(jnp.where(blocks[1, k] < CHUNK, 1, 0) for k in range(quarters - 1))
    lax.fori_loop(0, opening + 1, wait, 0)
    sbuf[0] = scores(0)

    def step(i, state, a):
        sbuf[1 - a] = scores(jnp.minimum(i + 1, last))
        return accumulate(state, sbuf[a], values_of(i))

    def two(i, state):
        return step(2 * i + 1, step(2 * i, state, 0), 1)

    def upto(k):
        some = jnp.maximum(blocks[1, k] // CHUNK - 1, 0) // 2
        return jnp.where(k == quarters - 1, full // 2, some)

    def part(k, state):
        lax.fori_loop(jnp.where(k == opening, k + 1, k), k + 1, wait, 0)
        start = jnp.where(k == opening, 0, upto(jnp.maximum(k - 1, 0)))
        return lax.fori_loop(start, upto(k), two, state)

    state = (m_ref[...], l_ref[...], acc_ref[...])
    state = lax.fori_loop(opening, quarters, part, state)
    state = lax.fori_loop(full // 2 * 2, full, lambda i, st: step(i, st, 0), state)

    def tail(i, state):
        position = i * (CHUNK * 128) + lax.broadcasted_iota(jnp.int32, (CHUNK * 128, rows), 0)
        s = jnp.where(position < n * 128, scores(i), -jnp.inf)
        return accumulate(state, s, values_of(i))

    m, l, acc = lax.fori_loop(full, (n + CHUNK - 1) // CHUNK, tail, state)
    context = (acc / l).T.astype(jnp.bfloat16)
    own = tok // 2
    for h in range(heads):
        mine_ref[:, h * HEAD : (h + 1) * HEAD] = context[h * tok : h * tok + own]
        theirs_ref[:, h * HEAD : (h + 1) * HEAD] = context[h * tok + own : (h + 1) * tok]


def attend(start, kv, blocks, length, heads, group):
    q, m, l, acc = start
    rows = q.shape[0]
    out = jax.ShapeDtypeStruct((rows // heads // 2, heads * HEAD), jnp.bfloat16)
    return pl.pallas_call(
        attend_kernel,
        out_shape=(out, out),
        in_specs=[SMEM, SMEM, VMEM, VMEM, VMEM, VMEM, HBM],
        out_specs=(VMEM, VMEM),
        scratch_shapes=[
            pltpu.VMEM((2, CHUNK * 128, rows), jnp.float32),
            pltpu.VMEM((kv.shape[0], 512, 128), kv.dtype),
            pltpu.SemaphoreType.DMA((4,)),
        ],
        compiler_params=limit(50),
        name=f"attend{group}",
    )(blocks, length, q, m, l, acc, kv)


def project_kernel(a_ref, b_ref, *refs, arriving):
    arrived, (wa_any, wb_any, up_ref, down_ref, wa_ref, wb_ref, sems) = (
        refs[:arriving],
        refs[arriving:],
    )
    half = a_ref.shape[0] // 2
    tiles = sems.shape[0]
    tile = wa_ref.shape[1] // tiles
    copies = []
    for j in range(tiles):
        cols = pl.ds(j * tile, tile)
        copies.append(
            (
                pltpu.make_async_copy(wa_any.at[:, cols], wa_ref.at[:, cols], sems.at[j, 0]),
                pltpu.make_async_copy(wb_any.at[:, cols], wb_ref.at[:, cols], sems.at[j, 1]),
            )
        )
        for copy in copies[-1]:
            copy.start()
    for j in range(tiles):
        cols = slice(j * tile, (j + 1) * tile)
        for copy in copies[j]:
            copy.wait()
        total = jnp.dot(a_ref[...], wa_ref[:, cols], preferred_element_type=jnp.float32)
        total += jnp.dot(b_ref[...], wb_ref[:, cols], preferred_element_type=jnp.float32)
        up, down = total[:half], total[half:]
        if arrived:
            up += arrived[0][:, cols].astype(jnp.float32)
            down += arrived[1][:, cols].astype(jnp.float32)
        up_ref[:, cols] = up.astype(jnp.bfloat16)
        down_ref[:, cols] = down.astype(jnp.bfloat16)


def project(a, b, wa, wb, *arrived):
    out = jax.ShapeDtypeStruct((a.shape[0] // 2, wa.shape[1]), jnp.bfloat16)
    return pl.pallas_call(
        functools.partial(project_kernel, arriving=len(arrived)),
        out_shape=(out, out),
        in_specs=[VMEM] * (2 + len(arrived)) + [HBM, HBM],
        out_specs=(VMEM, VMEM),
        scratch_shapes=[
            pltpu.VMEM(wa.shape, wa.dtype),
            pltpu.VMEM(wb.shape, wb.dtype),
            pltpu.SemaphoreType.DMA((10, 2)),
        ],
        compiler_params=limit(50),
        name=f"project{len(arrived)}",
    )(a, b, *arrived, wa, wb)


def combine_kernel(top, bottom, far_up, near_down, near_up, far_down, o_ref):
    half = top.shape[0]
    for rows, parts in ((0, (top, far_up, near_down)), (half, (bottom, near_up, far_down))):
        total = sum(part[...].astype(jnp.float32) for part in parts)
        o_ref[rows : rows + half, :] = total.astype(jnp.bfloat16)


def combine(*parts):
    rows, width = parts[0].shape
    return pl.pallas_call(
        combine_kernel,
        out_shape=jax.ShapeDtypeStruct((2 * rows, width), jnp.bfloat16),
        in_specs=[VMEM] * 6,
        out_specs=VMEM,
        compiler_params=limit(8),
        name="combine",
    )(*parts)


def copy_kernel(x_ref, o_ref, buf, sem):
    for source, target in ((x_ref, buf), (buf, o_ref)):
        copy = pltpu.make_async_copy(source, target, sem)
        copy.start()
        copy.wait()


def copy_pool(x):
    return pl.pallas_call(
        copy_kernel,
        out_shape=jax.ShapeDtypeStruct(x.shape, x.dtype),
        in_specs=[HBM],
        out_specs=HBM,
        scratch_shapes=[pltpu.VMEM(x.shape, x.dtype), pltpu.SemaphoreType.DMA],
        compiler_params=limit(4),
        name="copy_pool",
    )(x)


def write_kernel(slots, fresh_ref, kept_ref, out_ref, sems):
    del kept_ref
    for b in range(fresh_ref.shape[0]):

        @pl.when(slots[b] >= 0)
        def _(b=b):
            copy = pltpu.make_async_copy(fresh_ref.at[b], out_ref.at[slots[b]], sems.at[b])
            copy.start()
            copy.wait()


def write_back(slots, fresh, kept):
    return pl.pallas_call(
        write_kernel,
        out_shape=jax.ShapeDtypeStruct(kept.shape, kept.dtype),
        in_specs=[SMEM, VMEM, ANY],
        out_specs=ANY,
        input_output_aliases={2: 0},
        scratch_shapes=[pltpu.SemaphoreType.DMA((fresh.shape[0],))],
        compiler_params=limit(4),
        name="write",
    )(slots, fresh, kept)


def swap_pool(x):
    return lax.all_to_all(x, "pool", split_axis=0, concat_axis=0, tiled=True)


def on_device(
    queries,
    new_key_value,
    saved,
    out_weight,
    hist_owner,
    hist_block,
    hist_len,
    evict,
    dest_owner,
    dest_slot,
):
    pool = lax.axis_size("pool")
    me = lax.axis_index("pool")
    chips = lax.axis_size("tensor") // 2
    chip, core = lax.axis_index("tensor") // 2, lax.axis_index("tensor") % 2
    other_core = [(2 * z + c, 2 * z + 1 - c) for z in range(chips) for c in range(2)]
    upward = [(2 * z + c, 2 * ((z + 1) % chips) + c) for z in range(chips) for c in range(2)]
    downward = [(target, source) for source, target in upward]
    swap = functools.partial(lax.ppermute, axis_name="tensor", perm=other_core)
    send_up = functools.partial(lax.ppermute, axis_name="tensor", perm=upward)
    send_down = functools.partial(lax.ppermute, axis_name="tensor", perm=downward)

    def part(offset, c, half):
        return 128 * ((chip + offset) % chips) + 64 * c + 32 * half

    plan = (((2, 0), (2, 1)), ((1, 1), (3, 0)), ((1, 0), (3, 1)), ((0, 0), (0, 1)))
    base = jnp.stack(
        [
            jnp.stack([part(o, c, h) for c in (core, 1 - core) for o, h in parts])
            for parts in plan
        ]
    ).astype(jnp.int32)

    new_blocks = new_key_value.reshape(-1, 256, 128)
    table, blocks = exchange_table(
        hist_owner, hist_block, hist_len, dest_owner, dest_slot, evict, new_blocks, pool
    )
    arrived = swap_pool(table)
    pool_blocks = split_blocks(saved.reshape(-1, 256, 128))
    told = arrived[:, 32, :].astype(jnp.int32)
    kv = swap_pool(gather_blocks(told, pool_blocks, arrived[:, :32]))
    starts = begin(queries, split_blocks(new_blocks), base)
    other_weight = swap(out_weight)
    kept = copy_pool(saved.reshape(-1, 256, 128))

    heads = queries.shape[1] // HEAD

    def contexts(group, after):
        used, _ = lax.optimization_barrier((blocks, after))
        mine, theirs = attend(starts[group], kv, used, hist_len, heads, group)
        return mine, swap(theirs)

    up, down = project(*contexts(0, (kept, starts)), out_weight, other_weight)
    through_up, through_down = send_up(up), send_down(down)
    up, down = project(*contexts(1, up), out_weight, other_weight)
    near_up, near_down = send_up(up), send_down(down)
    up, down = project(*contexts(2, up), out_weight, other_weight, through_up, through_down)
    far_up, far_down = send_up(up), send_down(down)

    returned = kv[:, 512:].reshape(pool, 4, 8, 128).transpose(1, 0, 2, 3)
    mine = (told[:, 2:6] == me) & (told[:, 10:11] > 0)
    slots = jnp.max(jnp.where(mine, told[:, 6:10], -1), axis=0)
    top, bottom = project(*contexts(3, (near_up, near_down)), out_weight, other_weight)
    returned, _ = lax.optimization_barrier((returned, top))
    pool_out = write_back(slots, returned.reshape(4, 256, 128), kept).reshape(saved.shape)
    attn_out = combine(top, bottom, far_up, near_down, near_up, far_down)
    return attn_out, pool_out


def solution(mesh):
    in_specs = (
        P("pool", "tensor"),
        P("pool", None, "tensor"),
        P("pool", None, None, "tensor"),
        P("tensor", None),
        P("pool", None),
        P("pool", None),
        P("pool"),
        P("pool"),
        P("pool", None),
        P("pool", None),
    )
    out_specs = (P(("pool", "tensor"), None), P("pool", None, None, "tensor"))
    return jax.shard_map(
        on_device, mesh=mesh, in_specs=in_specs, out_specs=out_specs, check_vma=False
    )
```

```python
import functools
import math

import jax
import jax.numpy as jnp
from jax import lax
from jax.experimental import pallas as pl
from jax.experimental.pallas import tpu as pltpu
from jax.sharding import PartitionSpec as P

HEAD = 128
CHUNK = 8
PART = 32
NT = (((1,), (1,)), ((), ()))
SMEM = pl.BlockSpec(memory_space=pltpu.SMEM)
VMEM = pl.BlockSpec(memory_space=pltpu.VMEM)
ANY = pl.BlockSpec(memory_space=pl.ANY)
HBM = pl.BlockSpec(memory_space=pltpu.HBM)


def limit(mebibytes):
    return pltpu.CompilerParams(vmem_limit_bytes=mebibytes * 2**20)


def table_kernel(
    length, dest_owner, dest_slot, evict, owner_ref, block_ref, new_ref, table_ref, list_ref, rows_ref
):
    pool, entries = table_ref.shape[0], owner_ref.shape[1]
    owner = jnp.broadcast_to(owner_ref[...], (pool, entries))
    block = jnp.broadcast_to(block_ref[...], (pool, entries))
    row = lax.broadcasted_iota(jnp.int32, (pool, entries), 0)
    col = lax.broadcasted_iota(jnp.int32, (pool, entries), 1)
    match = owner == row
    first = jnp.min(jnp.where(match, col, entries), axis=1, keepdims=True)
    second = jnp.max(jnp.where(match, col, -1), axis=1, keepdims=True)
    want0 = jnp.sum(jnp.where(match & (col == first), block, 0), axis=1, keepdims=True)
    want1 = jnp.sum(jnp.where(match & (col == second), block, 0), axis=1, keepdims=True)
    row = lax.broadcasted_iota(jnp.int32, (pool, 128), 0)
    lane = lax.broadcasted_iota(jnp.int32, (pool, 128), 1)
    used0 = jnp.where(jnp.broadcast_to(first, (pool, 128)) < length[0], 1, 0)
    used1 = jnp.where(jnp.broadcast_to(second, (pool, 128)) < length[0], 1, 0)
    used = (used0 + used1).astype(jnp.float32)
    earlier = jnp.where(
        lax.broadcasted_iota(jnp.int32, (pool, pool), 1)
        < lax.broadcasted_iota(jnp.int32, (pool, pool), 0),
        1.0,
        0.0,
    )
    before = jnp.dot(earlier, used, preferred_element_type=jnp.float32).astype(jnp.int32)
    place = jnp.where((used0 > 0) & (before == lane), 2 * row, 0)
    place += jnp.where((used1 > 0) & (before + used0 == lane), 2 * row + 1, 0)
    quarter = pool // 4
    counts = jnp.where(row < quarter * (lane + 1), used0 + used1, 0)
    list_ref[...] = jnp.zeros(list_ref.shape, jnp.int32)
    list_ref[0:1] = jnp.sum(place, axis=0, keepdims=True)
    list_ref[1:2] = jnp.sum(counts, axis=0, keepdims=True)

    out = jnp.where(lane == 0, want0, jnp.where(lane == 1, want1, 0))
    for b in range(4):
        out = jnp.where(lane == 2 + b, dest_owner[0, b], out)
        out = jnp.where(lane == 6 + b, dest_slot[0, b], out)
    out = jnp.where(lane == 10, evict[0], out).astype(jnp.float32)
    for b in range(4):
        fresh = new_ref[b].astype(jnp.float32)
        for o in range(pool):
            rows_ref[o, 8 * b : 8 * b + 8, :] = fresh[8 * o : 8 * o + 8]
    for o in range(pool):
        rows_ref[o, 32:48, :] = jnp.broadcast_to(out[o : o + 1], (16, 128))
    table_ref[...] = rows_ref[...].astype(jnp.bfloat16)


def exchange_table(hist_owner, hist_block, hist_len, dest_owner, dest_slot, evict, new_blocks, pool):
    return pl.pallas_call(
        table_kernel,
        out_shape=(
            jax.ShapeDtypeStruct((pool, 48, 128), jnp.bfloat16),
            jax.ShapeDtypeStruct((8, 128), jnp.int32),
        ),
        in_specs=[SMEM, SMEM, SMEM, SMEM, VMEM, VMEM, VMEM],
        out_specs=(VMEM, VMEM),
        scratch_shapes=[pltpu.VMEM((pool, 48, 128), jnp.float32)],
        compiler_params=limit(58),
        name="table",
    )(hist_len, dest_owner, dest_slot, evict, hist_owner, hist_block, new_blocks)


def split_kernel(x_ref, o_ref):
    row = lax.broadcasted_iota(jnp.int32, (128, 256), 0)
    source = lax.broadcasted_iota(jnp.int32, (128, 256), 1)
    pick_k = jnp.where(source == 2 * row, 1.0, 0.0).astype(jnp.bfloat16)
    pick_v = jnp.where(source == 2 * row + 1, 1.0, 0.0).astype(jnp.bfloat16)
    for b in range(x_ref.shape[0]):
        x = x_ref[b]
        k = jnp.dot(pick_k, x, preferred_element_type=jnp.float32)
        v = jnp.dot(pick_v, x, preferred_element_type=jnp.float32)
        o_ref[b, 0:128, :] = k.astype(jnp.bfloat16)
        o_ref[b, 128:256, :] = v.T.astype(jnp.bfloat16)


def split_blocks(x):
    return pl.pallas_call(
        split_kernel,
        out_shape=jax.ShapeDtypeStruct(x.shape, x.dtype),
        in_specs=[VMEM],
        out_specs=VMEM,
        compiler_params=limit(12),
        name=f"split{x.shape[0]}",
    )(x)


def gather_kernel(told, pool_ref, held_ref, out_ref, held, onward, packed, sems):
    pool, rows = packed.shape[:2]
    copies = []
    for p in range(pool):
        for r in range(2):
            copies.append(
                pltpu.make_async_copy(
                    pool_ref.at[told[p, r]], out_ref.at[p, pl.ds(256 * r, 256)], sems.at[2 * p + r]
                )
            )
            copies[-1].start()
    held[...] = held_ref[...].astype(jnp.float32)
    for b in range(4):
        for p in range(pool):
            onward[told[p, 2 + b], 8 * b : 8 * b + 8, :] = held[p, 8 * b : 8 * b + 8, :]
    packed[...] = onward[...].astype(jnp.bfloat16)
    copies.append(
        pltpu.make_async_copy(packed, out_ref.at[:, pl.ds(512, rows)], sems.at[2 * pool])
    )
    copies[-1].start()
    for copy in copies:
        copy.wait()


def gather_blocks(told, pool_blocks, held):
    pool, rows, _ = held.shape
    return pl.pallas_call(
        gather_kernel,
        out_shape=jax.ShapeDtypeStruct((pool, 512 + rows, 128), pool_blocks.dtype),
        in_specs=[SMEM, VMEM, VMEM],
        out_specs=HBM,
        scratch_shapes=[
            pltpu.VMEM(held.shape, jnp.float32),
            pltpu.VMEM(held.shape, jnp.float32),
            pltpu.VMEM(held.shape, jnp.bfloat16),
            pltpu.SemaphoreType.DMA((2 * pool + 1,)),
        ],
        compiler_params=limit(51),
        name="gather",
    )(told, pool_blocks, held)


def accumulate(state, s, vt):
    m, l, acc = state
    c = math.log2(math.e) / math.sqrt(HEAD)
    top = jnp.maximum(m, jnp.max(s, axis=0, keepdims=True))
    p = jnp.exp2(s * c - top * c)
    keep = jnp.exp2((m - top) * c)
    l = l * keep + jnp.sum(p, axis=0, keepdims=True)
    acc = acc * keep + jnp.dot(vt, p.astype(jnp.bfloat16), preferred_element_type=jnp.float32)
    return top, l, acc


def begin_kernel(base, q_ref, new_ref, *refs):
    c = math.log2(math.e) / math.sqrt(HEAD)
    heads = q_ref.shape[1] // HEAD
    blocks = new_ref.shape[0]
    k = jnp.concatenate([new_ref[i, 0:128, :] for i in range(blocks)], axis=0)
    vt = jnp.concatenate([new_ref[i, 128:256, :] for i in range(blocks)], axis=1)
    before = 0
    for group in range(len(refs) // 4):
        out_q, out_m, out_l, out_acc = refs[4 * group : 4 * group + 4]
        rows = out_q.shape[0]
        tok = rows // heads
        parts = tok // PART
        key = lax.broadcasted_iota(jnp.int32, (blocks * 128, rows), 0)
        at = lax.broadcasted_iota(jnp.int32, (1, rows), 1) & (tok - 1)
        token = base[before] + at
        for i in range(1, parts):
            token = jnp.where(at >= PART * i, base[before + i] + at - PART * i, token)
        for i in range(parts):
            first = pl.multiple_of(base[before + i], PART)
            for h in range(heads):
                out_q[pl.ds(h * tok + i * PART, PART), :] = q_ref[
                    pl.ds(first, PART), h * HEAD : (h + 1) * HEAD
                ]
        s = lax.dot_general(k, out_q[...], NT, preferred_element_type=jnp.float32)
        s = jnp.where(key <= token, s, -jnp.inf)
        m = jnp.max(s, axis=0, keepdims=True)
        p = jnp.exp2(s * c - m * c)
        out_m[...] = m
        out_l[...] = jnp.sum(p, axis=0, keepdims=True)
        out_acc[...] = jnp.dot(vt, p.astype(jnp.bfloat16), preferred_element_type=jnp.float32)
        before += parts


def begin(queries, fresh, base, sizes):
    out_shape = ()
    for parts in sizes:
        rows = parts * PART * queries.shape[1] // HEAD
        out_shape += (
            jax.ShapeDtypeStruct((rows, HEAD), queries.dtype),
            jax.ShapeDtypeStruct((1, rows), jnp.float32),
            jax.ShapeDtypeStruct((1, rows), jnp.float32),
            jax.ShapeDtypeStruct((HEAD, rows), jnp.float32),
        )
    out = pl.pallas_call(
        begin_kernel,
        out_shape=out_shape,
        in_specs=[SMEM, VMEM, VMEM],
        out_specs=(VMEM,) * len(out_shape),
        compiler_params=limit(24),
        name="begin",
    )(base, queries, fresh)
    return [out[4 * g : 4 * g + 4] for g in range(len(sizes))]


def attend_kernel(
    blocks, length, q_ref, m_ref, l_ref, acc_ref, kv_any, mine_ref, theirs_ref, sbuf, kv_ref, sems
):
    quarters = sems.shape[0]
    share = kv_ref.shape[0] // quarters

    def quarter(k):
        owners = pl.ds(pl.multiple_of(k * share, share), share)
        return pltpu.make_async_copy(
            kv_any.at[owners, pl.ds(0, kv_ref.shape[1])], kv_ref.at[owners], sems.at[k]
        )

    def wait(k, _):
        quarter(k).wait()
        return 0

    for k in range(quarters):
        quarter(k).start()
    rows = q_ref.shape[0]
    tok = mine_ref.shape[0] * 2
    heads = rows // tok
    q = q_ref[...]

    def half(i, u, value):
        place = blocks[0, i * CHUNK + u]
        start = pl.multiple_of((place % 2) * 256 + 128 * value, 128)
        return kv_ref[place // 2, pl.ds(start, 128), :]

    def values_of(i):
        return jnp.concatenate([half(i, u, 1) for u in range(CHUNK)], axis=1)

    def scores(i):
        keys = jnp.concatenate([half(i, u, 0) for u in range(CHUNK)], axis=0)
        return lax.dot_general(keys, q, NT, preferred_element_type=jnp.float32)

    n = length[0]
    full = n // CHUNK
    last = 2 * kv_ref.shape[0] // CHUNK - 1
    opening = sum(jnp.where(blocks[1, k] < CHUNK, 1, 0) for k in range(quarters - 1))
    lax.fori_loop(0, opening + 1, wait, 0)
    sbuf[0] = scores(0)

    def step(i, state, a):
        sbuf[1 - a] = scores(jnp.minimum(i + 1, last))
        return accumulate(state, sbuf[a], values_of(i))

    def two(i, state):
        return step(2 * i + 1, step(2 * i, state, 0), 1)

    def upto(k):
        some = jnp.maximum(blocks[1, k] // CHUNK - 1, 0) // 2
        return jnp.where(k == quarters - 1, full // 2, some)

    def part(k, state):
        lax.fori_loop(jnp.where(k == opening, k + 1, k), k + 1, wait, 0)
        start = jnp.where(k == opening, 0, upto(jnp.maximum(k - 1, 0)))
        return lax.fori_loop(start, upto(k), two, state)

    state = (m_ref[...], l_ref[...], acc_ref[...])
    state = lax.fori_loop(opening, quarters, part, state)
    state = lax.fori_loop(full // 2 * 2, full, lambda i, st: step(i, st, 0), state)

    def tail(i, state):
        position = i * (CHUNK * 128) + lax.broadcasted_iota(jnp.int32, (CHUNK * 128, rows), 0)
        s = jnp.where(position < n * 128, scores(i), -jnp.inf)
        return accumulate(state, s, values_of(i))

    m, l, acc = lax.fori_loop(full, (n + CHUNK - 1) // CHUNK, tail, state)
    context = (acc / l).T.astype(jnp.bfloat16)
    own = tok // 2
    for h in range(heads):
        mine_ref[:, h * HEAD : (h + 1) * HEAD] = context[h * tok : h * tok + own]
        theirs_ref[:, h * HEAD : (h + 1) * HEAD] = context[h * tok + own : (h + 1) * tok]


def attend(start, kv, blocks, length, heads, group):
    q, m, l, acc = start
    rows = q.shape[0]
    out = jax.ShapeDtypeStruct((rows // heads // 2, heads * HEAD), jnp.bfloat16)
    return pl.pallas_call(
        attend_kernel,
        out_shape=(out, out),
        in_specs=[SMEM, SMEM, VMEM, VMEM, VMEM, VMEM, HBM],
        out_specs=(VMEM, VMEM),
        scratch_shapes=[
            pltpu.VMEM((2, CHUNK * 128, rows), jnp.float32),
            pltpu.VMEM((kv.shape[0], 512, 128), kv.dtype),
            pltpu.SemaphoreType.DMA((4,)),
        ],
        compiler_params=limit(50),
        name=f"attend{group}",
    )(blocks, length, q, m, l, acc, kv)


def project_kernel(a_ref, b_ref, *refs, arriving):
    arrived, (wa_any, wb_any) = refs[:arriving], refs[arriving : arriving + 2]
    outs, (wa_ref, wb_ref, sems) = refs[arriving + 2 : -3], refs[-3:]
    tiles = sems.shape[0]
    tile = wa_ref.shape[1] // tiles
    copies = []
    for j in range(tiles):
        cols = pl.ds(j * tile, tile)
        copies.append(
            (
                pltpu.make_async_copy(wa_any.at[:, cols], wa_ref.at[:, cols], sems.at[j, 0]),
                pltpu.make_async_copy(wb_any.at[:, cols], wb_ref.at[:, cols], sems.at[j, 1]),
            )
        )
        for copy in copies[-1]:
            copy.start()
    for j in range(tiles):
        cols = slice(j * tile, (j + 1) * tile)
        for copy in copies[j]:
            copy.wait()
        total = jnp.dot(a_ref[...], wa_ref[:, cols], preferred_element_type=jnp.float32)
        total += jnp.dot(b_ref[...], wb_ref[:, cols], preferred_element_type=jnp.float32)
        for i, out_ref in enumerate(outs):
            one = total[i * PART : (i + 1) * PART]
            if arrived:
                one += arrived[i][:, cols].astype(jnp.float32)
            out_ref[:, cols] = one.astype(jnp.bfloat16)


def project(a, b, wa, wb, *arrived):
    out = jax.ShapeDtypeStruct((PART, wa.shape[1]), jnp.bfloat16)
    parts = a.shape[0] // PART
    return pl.pallas_call(
        functools.partial(project_kernel, arriving=len(arrived)),
        out_shape=(out,) * parts,
        in_specs=[VMEM] * (2 + len(arrived)) + [HBM, HBM],
        out_specs=(VMEM,) * parts,
        scratch_shapes=[
            pltpu.VMEM(wa.shape, wa.dtype),
            pltpu.VMEM(wb.shape, wb.dtype),
            pltpu.SemaphoreType.DMA((10, 2)),
        ],
        compiler_params=limit(50),
        name=f"project{parts}",
    )(a, b, *arrived, wa, wb)


def combine_kernel(top, bottom, far_up, near_down, near_up, far_down, o_ref):
    half = top.shape[0]
    for rows, parts in ((0, (top, far_up, near_down)), (half, (bottom, near_up, far_down))):
        total = sum(part[...].astype(jnp.float32) for part in parts)
        o_ref[rows : rows + half, :] = total.astype(jnp.bfloat16)


def combine(*parts):
    rows, width = parts[0].shape
    return pl.pallas_call(
        combine_kernel,
        out_shape=jax.ShapeDtypeStruct((2 * rows, width), jnp.bfloat16),
        in_specs=[VMEM] * 6,
        out_specs=VMEM,
        compiler_params=limit(8),
        name="combine",
    )(*parts)


def copy_kernel(x_ref, o_ref, buf, sem):
    for source, target in ((x_ref, buf), (buf, o_ref)):
        copy = pltpu.make_async_copy(source, target, sem)
        copy.start()
        copy.wait()


def copy_pool(x):
    return pl.pallas_call(
        copy_kernel,
        out_shape=jax.ShapeDtypeStruct(x.shape, x.dtype),
        in_specs=[HBM],
        out_specs=HBM,
        scratch_shapes=[pltpu.VMEM(x.shape, x.dtype), pltpu.SemaphoreType.DMA],
        compiler_params=limit(4),
        name="copy_pool",
    )(x)


def write_kernel(slots, fresh_ref, kept_ref, out_ref, sems):
    del kept_ref
    for b in range(fresh_ref.shape[0]):

        @pl.when(slots[b] >= 0)
        def _(b=b):
            copy = pltpu.make_async_copy(fresh_ref.at[b], out_ref.at[slots[b]], sems.at[b])
            copy.start()
            copy.wait()


def write_back(slots, fresh, kept):
    return pl.pallas_call(
        write_kernel,
        out_shape=jax.ShapeDtypeStruct(kept.shape, kept.dtype),
        in_specs=[SMEM, VMEM, ANY],
        out_specs=ANY,
        input_output_aliases={2: 0},
        scratch_shapes=[pltpu.SemaphoreType.DMA((fresh.shape[0],))],
        compiler_params=limit(4),
        name="write",
    )(slots, fresh, kept)


def swap_pool(x):
    return lax.all_to_all(x, "pool", split_axis=0, concat_axis=0, tiled=True)


def on_device(
    queries,
    new_key_value,
    saved,
    out_weight,
    hist_owner,
    hist_block,
    hist_len,
    evict,
    dest_owner,
    dest_slot,
):
    pool = lax.axis_size("pool")
    me = lax.axis_index("pool")
    chips = lax.axis_size("tensor") // 2
    chip, core = lax.axis_index("tensor") // 2, lax.axis_index("tensor") % 2
    other_core = [(2 * z + c, 2 * z + 1 - c) for z in range(chips) for c in range(2)]
    upward = [(2 * z + c, 2 * ((z + 1) % chips) + c) for z in range(chips) for c in range(2)]
    downward = [(target, source) for source, target in upward]
    swap = functools.partial(lax.ppermute, axis_name="tensor", perm=other_core)
    send_up = functools.partial(lax.ppermute, axis_name="tensor", perm=upward)
    send_down = functools.partial(lax.ppermute, axis_name="tensor", perm=downward)

    def part(offset, c, half):
        return 128 * ((chip + offset) % chips) + 64 * c + PART * half

    plan = (((2, 0), (2, 1), (1, 1), (3, 0)), ((1, 0), (3, 1)), ((0, 0), (0, 1)))
    base = jnp.stack(
        [part(o, c, h) for parts in plan for c in (core, 1 - core) for o, h in parts]
    ).astype(jnp.int32)

    new_blocks = new_key_value.reshape(-1, 256, 128)
    table, blocks = exchange_table(
        hist_owner, hist_block, hist_len, dest_owner, dest_slot, evict, new_blocks, pool
    )
    arrived = swap_pool(table)
    pool_blocks = split_blocks(saved.reshape(-1, 256, 128))
    told = arrived[:, 32, :].astype(jnp.int32)
    kv = swap_pool(gather_blocks(told, pool_blocks, arrived[:, :32]))
    starts = begin(
        queries, split_blocks(new_blocks), base, [2 * len(parts) for parts in plan]
    )
    other_weight = swap(out_weight)
    kept = copy_pool(saved.reshape(-1, 256, 128))

    heads = queries.shape[1] // HEAD

    def contexts(group, after):
        used, _ = lax.optimization_barrier((blocks, after))
        mine, theirs = attend(starts[group], kv, used, hist_len, heads, group)
        return mine, swap(theirs)

    up, down, near_up, near_down = project(
        *contexts(0, (kept, starts)), out_weight, other_weight
    )
    through_up, through_down = send_up(up), send_down(down)
    near_up, near_down = send_up(near_up), send_down(near_down)
    up, down = project(*contexts(1, up), out_weight, other_weight, through_up, through_down)
    far_up, far_down = send_up(up), send_down(down)

    returned = kv[:, 512:].reshape(pool, 4, 8, 128).transpose(1, 0, 2, 3)
    mine = (told[:, 2:6] == me) & (told[:, 10:11] > 0)
    slots = jnp.max(jnp.where(mine, told[:, 6:10], -1), axis=0)
    top, bottom = project(*contexts(2, up), out_weight, other_weight)
    returned, _ = lax.optimization_barrier((returned, top))
    pool_out = write_back(slots, returned.reshape(4, 256, 128), kept).reshape(saved.shape)
    attn_out = combine(top, bottom, far_up, near_down, near_up, far_down)
    return attn_out, pool_out


def solution(mesh):
    in_specs = (
        P("pool", "tensor"),
        P("pool", None, "tensor"),
        P("pool", None, None, "tensor"),
        P("tensor", None),
        P("pool", None),
        P("pool", None),
        P("pool"),
        P("pool"),
        P("pool", None),
        P("pool", None),
    )
    out_specs = (P(("pool", "tensor"), None), P("pool", None, None, "tensor"))
    return jax.shard_map(
        on_device, mesh=mesh, in_specs=in_specs, out_specs=out_specs, check_vma=False
    )
```

```python
import functools
import math

import jax
import jax.numpy as jnp
from jax import lax
from jax.experimental import pallas as pl
from jax.experimental.pallas import tpu as pltpu
from jax.sharding import PartitionSpec as P

HEAD = 128
CHUNK = 8
PART = 32
NT = (((1,), (1,)), ((), ()))
SMEM = pl.BlockSpec(memory_space=pltpu.SMEM)
VMEM = pl.BlockSpec(memory_space=pltpu.VMEM)
ANY = pl.BlockSpec(memory_space=pl.ANY)
HBM = pl.BlockSpec(memory_space=pltpu.HBM)


def limit(mebibytes):
    return pltpu.CompilerParams(vmem_limit_bytes=mebibytes * 2**20)


def table_kernel(
    length, dest_owner, dest_slot, evict, owner_ref, block_ref, new_ref, table_ref, list_ref, rows_ref
):
    pool, entries = table_ref.shape[0], owner_ref.shape[1]
    owner = jnp.broadcast_to(owner_ref[...], (pool, entries))
    block = jnp.broadcast_to(block_ref[...], (pool, entries))
    row = lax.broadcasted_iota(jnp.int32, (pool, entries), 0)
    col = lax.broadcasted_iota(jnp.int32, (pool, entries), 1)
    match = owner == row
    first = jnp.min(jnp.where(match, col, entries), axis=1, keepdims=True)
    second = jnp.max(jnp.where(match, col, -1), axis=1, keepdims=True)
    want0 = jnp.sum(jnp.where(match & (col == first), block, 0), axis=1, keepdims=True)
    want1 = jnp.sum(jnp.where(match & (col == second), block, 0), axis=1, keepdims=True)
    row = lax.broadcasted_iota(jnp.int32, (pool, 128), 0)
    lane = lax.broadcasted_iota(jnp.int32, (pool, 128), 1)
    used0 = jnp.where(jnp.broadcast_to(first, (pool, 128)) < length[0], 1, 0)
    used1 = jnp.where(jnp.broadcast_to(second, (pool, 128)) < length[0], 1, 0)
    used = (used0 + used1).astype(jnp.float32)
    earlier = jnp.where(
        lax.broadcasted_iota(jnp.int32, (pool, pool), 1)
        < lax.broadcasted_iota(jnp.int32, (pool, pool), 0),
        1.0,
        0.0,
    )
    before = jnp.dot(earlier, used, preferred_element_type=jnp.float32).astype(jnp.int32)
    place = jnp.where((used0 > 0) & (before == lane), 2 * row, 0)
    place += jnp.where((used1 > 0) & (before + used0 == lane), 2 * row + 1, 0)
    quarter = pool // 4
    counts = jnp.where(row < quarter * (lane + 1), used0 + used1, 0)
    list_ref[...] = jnp.zeros(list_ref.shape, jnp.int32)
    list_ref[0:1] = jnp.sum(place, axis=0, keepdims=True)
    list_ref[1:2] = jnp.sum(counts, axis=0, keepdims=True)

    out = jnp.where(lane == 0, want0, jnp.where(lane == 1, want1, 0))
    for b in range(4):
        out = jnp.where(lane == 2 + b, dest_owner[0, b], out)
        out = jnp.where(lane == 6 + b, dest_slot[0, b], out)
    out = jnp.where(lane == 10, evict[0], out).astype(jnp.float32)
    for b in range(4):
        fresh = new_ref[b].astype(jnp.float32)
        for o in range(pool):
            rows_ref[o, 8 * b : 8 * b + 8, :] = fresh[8 * o : 8 * o + 8]
    for o in range(pool):
        rows_ref[o, 32:48, :] = jnp.broadcast_to(out[o : o + 1], (16, 128))
    table_ref[...] = rows_ref[...].astype(jnp.bfloat16)


def exchange_table(hist_owner, hist_block, hist_len, dest_owner, dest_slot, evict, new_blocks, pool):
    return pl.pallas_call(
        table_kernel,
        out_shape=(
            jax.ShapeDtypeStruct((pool, 48, 128), jnp.bfloat16),
            jax.ShapeDtypeStruct((8, 128), jnp.int32),
        ),
        in_specs=[SMEM, SMEM, SMEM, SMEM, VMEM, VMEM, VMEM],
        out_specs=(VMEM, VMEM),
        scratch_shapes=[pltpu.VMEM((pool, 48, 128), jnp.float32)],
        compiler_params=limit(58),
        name="table",
    )(hist_len, dest_owner, dest_slot, evict, hist_owner, hist_block, new_blocks)


def split_kernel(x_ref, o_ref):
    row = lax.broadcasted_iota(jnp.int32, (128, 256), 0)
    source = lax.broadcasted_iota(jnp.int32, (128, 256), 1)
    pick_k = jnp.where(source == 2 * row, 1.0, 0.0).astype(jnp.bfloat16)
    pick_v = jnp.where(source == 2 * row + 1, 1.0, 0.0).astype(jnp.bfloat16)
    for b in range(x_ref.shape[0]):
        x = x_ref[b]
        k = jnp.dot(pick_k, x, preferred_element_type=jnp.float32)
        v = jnp.dot(pick_v, x, preferred_element_type=jnp.float32)
        o_ref[b, 0:128, :] = k.astype(jnp.bfloat16)
        o_ref[b, 128:256, :] = v.T.astype(jnp.bfloat16)


def split_blocks(x):
    return pl.pallas_call(
        split_kernel,
        out_shape=jax.ShapeDtypeStruct(x.shape, x.dtype),
        in_specs=[VMEM],
        out_specs=VMEM,
        compiler_params=limit(12),
        name=f"split{x.shape[0]}",
    )(x)


def gather_kernel(told, pool_ref, held_ref, out_ref, held, onward, packed, sems):
    pool, rows = packed.shape[:2]
    copies = []
    for p in range(pool):
        for r in range(2):
            copies.append(
                pltpu.make_async_copy(
                    pool_ref.at[told[p, r]], out_ref.at[p, pl.ds(256 * r, 256)], sems.at[2 * p + r]
                )
            )
            copies[-1].start()
    held[...] = held_ref[...].astype(jnp.float32)
    for b in range(4):
        for p in range(pool):
            onward[told[p, 2 + b], 8 * b : 8 * b + 8, :] = held[p, 8 * b : 8 * b + 8, :]
    packed[...] = onward[...].astype(jnp.bfloat16)
    copies.append(
        pltpu.make_async_copy(packed, out_ref.at[:, pl.ds(512, rows)], sems.at[2 * pool])
    )
    copies[-1].start()
    for copy in copies:
        copy.wait()


def gather_blocks(told, pool_blocks, held):
    pool, rows, _ = held.shape
    return pl.pallas_call(
        gather_kernel,
        out_shape=jax.ShapeDtypeStruct((pool, 512 + rows, 128), pool_blocks.dtype),
        in_specs=[SMEM, VMEM, VMEM],
        out_specs=HBM,
        scratch_shapes=[
            pltpu.VMEM(held.shape, jnp.float32),
            pltpu.VMEM(held.shape, jnp.float32),
            pltpu.VMEM(held.shape, jnp.bfloat16),
            pltpu.SemaphoreType.DMA((2 * pool + 1,)),
        ],
        compiler_params=limit(51),
        name="gather",
    )(told, pool_blocks, held)


def accumulate(state, s, vt):
    m, l, acc = state
    c = math.log2(math.e) / math.sqrt(HEAD)
    top = jnp.maximum(m, jnp.max(s, axis=0, keepdims=True))
    p = jnp.exp2(s * c - top * c)
    keep = jnp.exp2((m - top) * c)
    l = l * keep + jnp.sum(p, axis=0, keepdims=True)
    acc = acc * keep + jnp.dot(vt, p.astype(jnp.bfloat16), preferred_element_type=jnp.float32)
    return top, l, acc


def begin_kernel(base, q_ref, new_ref, *refs):
    c = math.log2(math.e) / math.sqrt(HEAD)
    heads = q_ref.shape[1] // HEAD
    blocks = new_ref.shape[0]
    k = jnp.concatenate([new_ref[i, 0:128, :] for i in range(blocks)], axis=0)
    vt = jnp.concatenate([new_ref[i, 128:256, :] for i in range(blocks)], axis=1)
    before = 0
    for group in range(len(refs) // 4):
        out_q, out_m, out_l, out_acc = refs[4 * group : 4 * group + 4]
        rows = out_q.shape[0]
        tok = rows // heads
        parts = tok // PART
        key = lax.broadcasted_iota(jnp.int32, (blocks * 128, rows), 0)
        at = lax.broadcasted_iota(jnp.int32, (1, rows), 1) & (tok - 1)
        token = base[before] + at
        for i in range(1, parts):
            token = jnp.where(at >= PART * i, base[before + i] + at - PART * i, token)
        for i in range(parts):
            first = pl.multiple_of(base[before + i], PART)
            for h in range(heads):
                out_q[pl.ds(h * tok + i * PART, PART), :] = q_ref[
                    pl.ds(first, PART), h * HEAD : (h + 1) * HEAD
                ]
        s = lax.dot_general(k, out_q[...], NT, preferred_element_type=jnp.float32)
        s = jnp.where(key <= token, s, -jnp.inf)
        m = jnp.max(s, axis=0, keepdims=True)
        p = jnp.exp2(s * c - m * c)
        out_m[...] = m
        out_l[...] = jnp.sum(p, axis=0, keepdims=True)
        out_acc[...] = jnp.dot(vt, p.astype(jnp.bfloat16), preferred_element_type=jnp.float32)
        before += parts


def begin(queries, fresh, base, sizes):
    out_shape = ()
    for parts in sizes:
        rows = parts * PART * queries.shape[1] // HEAD
        out_shape += (
            jax.ShapeDtypeStruct((rows, HEAD), queries.dtype),
            jax.ShapeDtypeStruct((1, rows), jnp.float32),
            jax.ShapeDtypeStruct((1, rows), jnp.float32),
            jax.ShapeDtypeStruct((HEAD, rows), jnp.float32),
        )
    out = pl.pallas_call(
        begin_kernel,
        out_shape=out_shape,
        in_specs=[SMEM, VMEM, VMEM],
        out_specs=(VMEM,) * len(out_shape),
        compiler_params=limit(24),
        name="begin",
    )(base, queries, fresh)
    return [out[4 * g : 4 * g + 4] for g in range(len(sizes))]


def attend_kernel(
    blocks, length, q_ref, m_ref, l_ref, acc_ref, kv_any, mine_ref, theirs_ref, sbuf, kv_ref, sems
):
    quarters = sems.shape[0]
    share = kv_ref.shape[0] // quarters

    def quarter(k):
        owners = pl.ds(pl.multiple_of(k * share, share), share)
        return pltpu.make_async_copy(
            kv_any.at[owners, pl.ds(0, kv_ref.shape[1])], kv_ref.at[owners], sems.at[k]
        )

    def wait(k, _):
        quarter(k).wait()
        return 0

    for k in range(quarters):
        quarter(k).start()
    rows = q_ref.shape[0]
    tok = mine_ref.shape[0] * 2
    heads = rows // tok
    q = q_ref[...]

    def half(i, u, value):
        place = blocks[0, i * CHUNK + u]
        start = pl.multiple_of((place % 2) * 256 + 128 * value, 128)
        return kv_ref[place // 2, pl.ds(start, 128), :]

    def values_of(i):
        return jnp.concatenate([half(i, u, 1) for u in range(CHUNK)], axis=1)

    def scores(i):
        keys = jnp.concatenate([half(i, u, 0) for u in range(CHUNK)], axis=0)
        return lax.dot_general(keys, q, NT, preferred_element_type=jnp.float32)

    n = length[0]
    full = n // CHUNK
    last = 2 * kv_ref.shape[0] // CHUNK - 1
    opening = sum(jnp.where(blocks[1, k] < CHUNK, 1, 0) for k in range(quarters - 1))
    lax.fori_loop(0, opening + 1, wait, 0)
    sbuf[0] = scores(0)

    def step(i, state, a):
        sbuf[1 - a] = scores(jnp.minimum(i + 1, last))
        return accumulate(state, sbuf[a], values_of(i))

    def two(i, state):
        return step(2 * i + 1, step(2 * i, state, 0), 1)

    def upto(k):
        some = jnp.maximum(blocks[1, k] // CHUNK - 1, 0) // 2
        return jnp.where(k == quarters - 1, full // 2, some)

    def part(k, state):
        lax.fori_loop(jnp.where(k == opening, k + 1, k), k + 1, wait, 0)
        start = jnp.where(k == opening, 0, upto(jnp.maximum(k - 1, 0)))
        return lax.fori_loop(start, upto(k), two, state)

    state = (m_ref[...], l_ref[...], acc_ref[...])
    state = lax.fori_loop(opening, quarters, part, state)
    state = lax.fori_loop(full // 2 * 2, full, lambda i, st: step(i, st, 0), state)

    def tail(i, state):
        position = i * (CHUNK * 128) + lax.broadcasted_iota(jnp.int32, (CHUNK * 128, rows), 0)
        s = jnp.where(position < n * 128, scores(i), -jnp.inf)
        return accumulate(state, s, values_of(i))

    m, l, acc = lax.fori_loop(full, (n + CHUNK - 1) // CHUNK, tail, state)
    context = (acc / l).T.astype(jnp.bfloat16)
    own = tok // 2
    for h in range(heads):
        mine_ref[:, h * HEAD : (h + 1) * HEAD] = context[h * tok : h * tok + own]
        theirs_ref[:, h * HEAD : (h + 1) * HEAD] = context[h * tok + own : (h + 1) * tok]


def attend(start, kv, blocks, length, heads, group):
    q, m, l, acc = start
    rows = q.shape[0]
    out = jax.ShapeDtypeStruct((rows // heads // 2, heads * HEAD), jnp.bfloat16)
    return pl.pallas_call(
        attend_kernel,
        out_shape=(out, out),
        in_specs=[SMEM, SMEM, VMEM, VMEM, VMEM, VMEM, HBM],
        out_specs=(VMEM, VMEM),
        scratch_shapes=[
            pltpu.VMEM((2, CHUNK * 128, rows), jnp.float32),
            pltpu.VMEM((kv.shape[0], 512, 128), kv.dtype),
            pltpu.SemaphoreType.DMA((4,)),
        ],
        compiler_params=limit(50),
        name=f"attend{group}",
    )(blocks, length, q, m, l, acc, kv)


def project_kernel(a_ref, b_ref, *refs, arriving):
    arrived, (wa_any, wb_any) = refs[:arriving], refs[arriving : arriving + 2]
    outs, (wa_ref, wb_ref, sems) = refs[arriving + 2 : -3], refs[-3:]
    tiles = sems.shape[0]
    tile = wa_ref.shape[1] // tiles
    copies = []
    for j in range(tiles):
        cols = pl.ds(j * tile, tile)
        copies.append(
            (
                pltpu.make_async_copy(wa_any.at[:, cols], wa_ref.at[:, cols], sems.at[j, 0]),
                pltpu.make_async_copy(wb_any.at[:, cols], wb_ref.at[:, cols], sems.at[j, 1]),
            )
        )
        for copy in copies[-1]:
            copy.start()
    for j in range(tiles):
        cols = slice(j * tile, (j + 1) * tile)
        for copy in copies[j]:
            copy.wait()
        total = jnp.dot(a_ref[...], wa_ref[:, cols], preferred_element_type=jnp.float32)
        total += jnp.dot(b_ref[...], wb_ref[:, cols], preferred_element_type=jnp.float32)
        for i, out_ref in enumerate(outs):
            one = total[i * PART : (i + 1) * PART]
            if arrived:
                one += arrived[i][:, cols].astype(jnp.float32)
            out_ref[:, cols] = one.astype(jnp.bfloat16)


def project(a, b, wa, wb, *arrived):
    out = jax.ShapeDtypeStruct((PART, wa.shape[1]), jnp.bfloat16)
    parts = a.shape[0] // PART
    return pl.pallas_call(
        functools.partial(project_kernel, arriving=len(arrived)),
        out_shape=(out,) * parts,
        in_specs=[VMEM] * (2 + len(arrived)) + [HBM, HBM],
        out_specs=(VMEM,) * parts,
        scratch_shapes=[
            pltpu.VMEM(wa.shape, wa.dtype),
            pltpu.VMEM(wb.shape, wb.dtype),
            pltpu.SemaphoreType.DMA((10, 2)),
        ],
        compiler_params=limit(50),
        name=f"project{parts}",
    )(a, b, *arrived, wa, wb)


def combine_kernel(top, bottom, far_up, near_down, near_up, far_down, o_ref):
    half = top.shape[0]
    for rows, parts in ((0, (top, far_up, near_down)), (half, (bottom, near_up, far_down))):
        total = sum(part[...].astype(jnp.float32) for part in parts)
        o_ref[rows : rows + half, :] = total.astype(jnp.bfloat16)


def combine(*parts):
    rows, width = parts[0].shape
    return pl.pallas_call(
        combine_kernel,
        out_shape=jax.ShapeDtypeStruct((2 * rows, width), jnp.bfloat16),
        in_specs=[VMEM] * 6,
        out_specs=VMEM,
        compiler_params=limit(8),
        name="combine",
    )(*parts)


def copy_kernel(x_ref, o_ref, buf, sem):
    for source, target in ((x_ref, buf), (buf, o_ref)):
        copy = pltpu.make_async_copy(source, target, sem)
        copy.start()
        copy.wait()


def copy_pool(x):
    return pl.pallas_call(
        copy_kernel,
        out_shape=jax.ShapeDtypeStruct(x.shape, x.dtype),
        in_specs=[HBM],
        out_specs=HBM,
        scratch_shapes=[pltpu.VMEM(x.shape, x.dtype), pltpu.SemaphoreType.DMA],
        compiler_params=limit(4),
        name="copy_pool",
    )(x)


def write_kernel(slots, fresh_ref, kept_ref, out_ref, sems):
    del kept_ref
    for b in range(fresh_ref.shape[0]):

        @pl.when(slots[b] >= 0)
        def _(b=b):
            copy = pltpu.make_async_copy(fresh_ref.at[b], out_ref.at[slots[b]], sems.at[b])
            copy.start()
            copy.wait()


def write_back(slots, fresh, kept):
    return pl.pallas_call(
        write_kernel,
        out_shape=jax.ShapeDtypeStruct(kept.shape, kept.dtype),
        in_specs=[SMEM, VMEM, ANY],
        out_specs=ANY,
        input_output_aliases={2: 0},
        scratch_shapes=[pltpu.SemaphoreType.DMA((fresh.shape[0],))],
        compiler_params=limit(4),
        name="write",
    )(slots, fresh, kept)


def swap_pool(x):
    return lax.all_to_all(x, "pool", split_axis=0, concat_axis=0, tiled=True)


def on_device(
    queries,
    new_key_value,
    saved,
    out_weight,
    hist_owner,
    hist_block,
    hist_len,
    evict,
    dest_owner,
    dest_slot,
):
    pool = lax.axis_size("pool")
    me = lax.axis_index("pool")
    chips = lax.axis_size("tensor") // 2
    chip, core = lax.axis_index("tensor") // 2, lax.axis_index("tensor") % 2
    other_core = [(2 * z + c, 2 * z + 1 - c) for z in range(chips) for c in range(2)]
    upward = [(2 * z + c, 2 * ((z + 1) % chips) + c) for z in range(chips) for c in range(2)]
    downward = [(target, source) for source, target in upward]
    swap = functools.partial(lax.ppermute, axis_name="tensor", perm=other_core)
    send_up = functools.partial(lax.ppermute, axis_name="tensor", perm=upward)
    send_down = functools.partial(lax.ppermute, axis_name="tensor", perm=downward)

    def part(offset, c, half):
        return 128 * ((chip + offset) % chips) + 64 * c + PART * half

    plan = (((2, 0), (2, 1), (1, 1), (3, 0)), ((1, 0), (3, 1)), ((0, 0), (0, 1)))
    base = jnp.stack(
        [part(o, c, h) for parts in plan for c in (core, 1 - core) for o, h in parts]
    ).astype(jnp.int32)

    new_blocks = new_key_value.reshape(-1, 256, 128)
    table, blocks = exchange_table(
        hist_owner, hist_block, hist_len, dest_owner, dest_slot, evict, new_blocks, pool
    )
    arrived = swap_pool(table)
    pool_blocks = split_blocks(saved.reshape(-1, 256, 128))
    told = arrived[:, 32, :].astype(jnp.int32)
    kv = swap_pool(gather_blocks(told, pool_blocks, arrived[:, :32]))
    starts = begin(
        queries, split_blocks(new_blocks), base, [2 * len(parts) for parts in plan]
    )
    other_weight = swap(out_weight)
    kept = copy_pool(saved.reshape(-1, 256, 128))

    heads = queries.shape[1] // HEAD

    def contexts(group, after, before_swap=()):
        used, _ = lax.optimization_barrier((blocks, after))
        mine, theirs = attend(starts[group], kv, used, hist_len, heads, group)
        theirs, _ = lax.optimization_barrier((theirs, before_swap))
        return mine, swap(theirs)

    up, down, near_up, near_down = project(
        *contexts(0, (kept, starts)), out_weight, other_weight
    )
    through_up, through_down = send_up(up), send_down(down)
    near_up, near_down = send_up(near_up), send_down(near_down)
    up, down = project(*contexts(1, up), out_weight, other_weight, through_up, through_down)
    far_up, far_down = send_up(up), send_down(down)

    returned = kv[:, 512:].reshape(pool, 4, 8, 128).transpose(1, 0, 2, 3)
    mine = (told[:, 2:6] == me) & (told[:, 10:11] > 0)
    slots = jnp.max(jnp.where(mine, told[:, 6:10], -1), axis=0)
    top, bottom = project(*contexts(2, up, (near_up, near_down)), out_weight, other_weight)
    returned, _ = lax.optimization_barrier((returned, top))
    pool_out = write_back(slots, returned.reshape(4, 256, 128), kept).reshape(saved.shape)
    attn_out = combine(top, bottom, far_up, near_down, near_up, far_down)
    return attn_out, pool_out


def solution(mesh):
    in_specs = (
        P("pool", "tensor"),
        P("pool", None, "tensor"),
        P("pool", None, None, "tensor"),
        P("tensor", None),
        P("pool", None),
        P("pool", None),
        P("pool"),
        P("pool"),
        P("pool", None),
        P("pool", None),
    )
    out_specs = (P(("pool", "tensor"), None), P("pool", None, None, "tensor"))
    return jax.shard_map(
        on_device, mesh=mesh, in_specs=in_specs, out_specs=out_specs, check_vma=False
    )
```

```python
import functools
import math

import jax
import jax.numpy as jnp
from jax import lax
from jax.experimental import pallas as pl
from jax.experimental.pallas import tpu as pltpu
from jax.sharding import PartitionSpec as P

HEAD = 128
CHUNK = 8
PART = 32
NT = (((1,), (1,)), ((), ()))
SMEM = pl.BlockSpec(memory_space=pltpu.SMEM)
VMEM = pl.BlockSpec(memory_space=pltpu.VMEM)
ANY = pl.BlockSpec(memory_space=pl.ANY)
HBM = pl.BlockSpec(memory_space=pltpu.HBM)


def limit(mebibytes):
    return pltpu.CompilerParams(vmem_limit_bytes=mebibytes * 2**20)


def table_kernel(
    length, dest_owner, dest_slot, evict, owner_ref, block_ref, new_ref, table_ref, list_ref, rows_ref
):
    pool, entries = table_ref.shape[0], owner_ref.shape[1]
    owner = jnp.broadcast_to(owner_ref[...], (pool, entries))
    block = jnp.broadcast_to(block_ref[...], (pool, entries))
    row = lax.broadcasted_iota(jnp.int32, (pool, entries), 0)
    col = lax.broadcasted_iota(jnp.int32, (pool, entries), 1)
    match = owner == row
    first = jnp.min(jnp.where(match, col, entries), axis=1, keepdims=True)
    second = jnp.max(jnp.where(match, col, -1), axis=1, keepdims=True)
    want0 = jnp.sum(jnp.where(match & (col == first), block, 0), axis=1, keepdims=True)
    want1 = jnp.sum(jnp.where(match & (col == second), block, 0), axis=1, keepdims=True)
    row = lax.broadcasted_iota(jnp.int32, (pool, 128), 0)
    lane = lax.broadcasted_iota(jnp.int32, (pool, 128), 1)
    used0 = jnp.where(jnp.broadcast_to(first, (pool, 128)) < length[0], 1, 0)
    used1 = jnp.where(jnp.broadcast_to(second, (pool, 128)) < length[0], 1, 0)
    used = (used0 + used1).astype(jnp.float32)
    earlier = jnp.where(
        lax.broadcasted_iota(jnp.int32, (pool, pool), 1)
        < lax.broadcasted_iota(jnp.int32, (pool, pool), 0),
        1.0,
        0.0,
    )
    before = jnp.dot(earlier, used, preferred_element_type=jnp.float32).astype(jnp.int32)
    place = jnp.where((used0 > 0) & (before == lane), 2 * row, 0)
    place += jnp.where((used1 > 0) & (before + used0 == lane), 2 * row + 1, 0)
    quarter = pool // 4
    counts = jnp.where(row < quarter * (lane + 1), used0 + used1, 0)
    list_ref[...] = jnp.zeros(list_ref.shape, jnp.int32)
    list_ref[0:1] = jnp.sum(place, axis=0, keepdims=True)
    list_ref[1:2] = jnp.sum(counts, axis=0, keepdims=True)

    out = jnp.where(lane == 0, want0, jnp.where(lane == 1, want1, 0))
    for b in range(4):
        out = jnp.where(lane == 2 + b, dest_owner[0, b], out)
        out = jnp.where(lane == 6 + b, dest_slot[0, b], out)
    out = jnp.where(lane == 10, evict[0], out).astype(jnp.float32)
    for b in range(4):
        fresh = new_ref[b].astype(jnp.float32)
        for o in range(pool):
            rows_ref[o, 8 * b : 8 * b + 8, :] = fresh[8 * o : 8 * o + 8]
    for o in range(pool):
        rows_ref[o, 32:48, :] = jnp.broadcast_to(out[o : o + 1], (16, 128))
    table_ref[...] = rows_ref[...].astype(jnp.bfloat16)


def exchange_table(hist_owner, hist_block, hist_len, dest_owner, dest_slot, evict, new_blocks, pool):
    return pl.pallas_call(
        table_kernel,
        out_shape=(
            jax.ShapeDtypeStruct((pool, 48, 128), jnp.bfloat16),
            jax.ShapeDtypeStruct((8, 128), jnp.int32),
        ),
        in_specs=[SMEM, SMEM, SMEM, SMEM, VMEM, VMEM, VMEM],
        out_specs=(VMEM, VMEM),
        scratch_shapes=[pltpu.VMEM((pool, 48, 128), jnp.float32)],
        compiler_params=limit(58),
        name="table",
    )(hist_len, dest_owner, dest_slot, evict, hist_owner, hist_block, new_blocks)


def split_kernel(x_ref, o_ref):
    row = lax.broadcasted_iota(jnp.int32, (128, 256), 0)
    source = lax.broadcasted_iota(jnp.int32, (128, 256), 1)
    pick_k = jnp.where(source == 2 * row, 1.0, 0.0).astype(jnp.bfloat16)
    pick_v = jnp.where(source == 2 * row + 1, 1.0, 0.0).astype(jnp.bfloat16)
    for b in range(x_ref.shape[0]):
        x = x_ref[b]
        k = jnp.dot(pick_k, x, preferred_element_type=jnp.float32)
        v = jnp.dot(pick_v, x, preferred_element_type=jnp.float32)
        o_ref[b, 0:128, :] = k.astype(jnp.bfloat16)
        o_ref[b, 128:256, :] = v.T.astype(jnp.bfloat16)


def split_blocks(x):
    return pl.pallas_call(
        split_kernel,
        out_shape=jax.ShapeDtypeStruct(x.shape, x.dtype),
        in_specs=[VMEM],
        out_specs=VMEM,
        compiler_params=limit(12),
        name=f"split{x.shape[0]}",
    )(x)


def gather_kernel(told, pool_ref, held_ref, out_ref, held, onward, packed, sems):
    pool, rows = packed.shape[:2]
    copies = []
    for p in range(pool):
        for r in range(2):
            copies.append(
                pltpu.make_async_copy(
                    pool_ref.at[told[p, r]], out_ref.at[p, pl.ds(256 * r, 256)], sems.at[2 * p + r]
                )
            )
            copies[-1].start()
    held[...] = held_ref[...].astype(jnp.float32)
    for b in range(4):
        for p in range(pool):
            onward[told[p, 2 + b], 8 * b : 8 * b + 8, :] = held[p, 8 * b : 8 * b + 8, :]
    packed[...] = onward[...].astype(jnp.bfloat16)
    copies.append(
        pltpu.make_async_copy(packed, out_ref.at[:, pl.ds(512, rows)], sems.at[2 * pool])
    )
    copies[-1].start()
    for copy in copies:
        copy.wait()


def gather_blocks(told, pool_blocks, held):
    pool, rows, _ = held.shape
    return pl.pallas_call(
        gather_kernel,
        out_shape=jax.ShapeDtypeStruct((pool, 512 + rows, 128), pool_blocks.dtype),
        in_specs=[SMEM, VMEM, VMEM],
        out_specs=HBM,
        scratch_shapes=[
            pltpu.VMEM(held.shape, jnp.float32),
            pltpu.VMEM(held.shape, jnp.float32),
            pltpu.VMEM(held.shape, jnp.bfloat16),
            pltpu.SemaphoreType.DMA((2 * pool + 1,)),
        ],
        compiler_params=limit(51),
        name="gather",
    )(told, pool_blocks, held)


def accumulate(state, s, vt):
    m, l, acc = state
    c = math.log2(math.e) / math.sqrt(HEAD)
    top = jnp.maximum(m, jnp.max(s, axis=0, keepdims=True))
    p = jnp.exp2(s * c - top * c)
    keep = jnp.exp2((m - top) * c)
    l = l * keep + jnp.sum(p, axis=0, keepdims=True)
    acc = acc * keep + jnp.dot(vt, p.astype(jnp.bfloat16), preferred_element_type=jnp.float32)
    return top, l, acc


def begin_kernel(base, q_ref, new_ref, *refs):
    c = math.log2(math.e) / math.sqrt(HEAD)
    heads = q_ref.shape[1] // HEAD
    blocks = new_ref.shape[0]
    k = jnp.concatenate([new_ref[i, 0:128, :] for i in range(blocks)], axis=0)
    vt = jnp.concatenate([new_ref[i, 128:256, :] for i in range(blocks)], axis=1)
    before = 0
    for group in range(len(refs) // 4):
        out_q, out_m, out_l, out_acc = refs[4 * group : 4 * group + 4]
        rows = out_q.shape[0]
        tok = rows // heads
        parts = tok // PART
        key = lax.broadcasted_iota(jnp.int32, (blocks * 128, rows), 0)
        at = lax.broadcasted_iota(jnp.int32, (1, rows), 1) & (tok - 1)
        token = base[before] + at
        for i in range(1, parts):
            token = jnp.where(at >= PART * i, base[before + i] + at - PART * i, token)
        for i in range(parts):
            first = pl.multiple_of(base[before + i], PART)
            for h in range(heads):
                out_q[pl.ds(h * tok + i * PART, PART), :] = q_ref[
                    pl.ds(first, PART), h * HEAD : (h + 1) * HEAD
                ]
        s = lax.dot_general(k, out_q[...], NT, preferred_element_type=jnp.float32)
        s = jnp.where(key <= token, s, -jnp.inf)
        m = jnp.max(s, axis=0, keepdims=True)
        p = jnp.exp2(s * c - m * c)
        out_m[...] = m
        out_l[...] = jnp.sum(p, axis=0, keepdims=True)
        out_acc[...] = jnp.dot(vt, p.astype(jnp.bfloat16), preferred_element_type=jnp.float32)
        before += parts


def begin(queries, fresh, base, sizes):
    out_shape = ()
    for parts in sizes:
        rows = parts * PART * queries.shape[1] // HEAD
        out_shape += (
            jax.ShapeDtypeStruct((rows, HEAD), queries.dtype),
            jax.ShapeDtypeStruct((1, rows), jnp.float32),
            jax.ShapeDtypeStruct((1, rows), jnp.float32),
            jax.ShapeDtypeStruct((HEAD, rows), jnp.float32),
        )
    out = pl.pallas_call(
        begin_kernel,
        out_shape=out_shape,
        in_specs=[SMEM, VMEM, VMEM],
        out_specs=(VMEM,) * len(out_shape),
        compiler_params=limit(24),
        name="begin",
    )(base, queries, fresh)
    return [out[4 * g : 4 * g + 4] for g in range(len(sizes))]


def attend_kernel(
    blocks, length, q_ref, m_ref, l_ref, acc_ref, kv_any, mine_ref, theirs_ref, sbuf, kv_ref, sems
):
    quarters = sems.shape[0]
    share = kv_ref.shape[0] // quarters

    def quarter(k):
        owners = pl.ds(pl.multiple_of(k * share, share), share)
        return pltpu.make_async_copy(
            kv_any.at[owners, pl.ds(0, kv_ref.shape[1])], kv_ref.at[owners], sems.at[k]
        )

    def wait(k, _):
        quarter(k).wait()
        return 0

    for k in range(quarters):
        quarter(k).start()
    rows = q_ref.shape[0]
    tok = mine_ref.shape[0] * 2
    heads = rows // tok
    q = q_ref[...]

    def half(i, u, value):
        place = blocks[0, i * CHUNK + u]
        start = pl.multiple_of((place % 2) * 256 + 128 * value, 128)
        return kv_ref[place // 2, pl.ds(start, 128), :]

    def values_of(i):
        return jnp.concatenate([half(i, u, 1) for u in range(CHUNK)], axis=1)

    def scores(i):
        keys = jnp.concatenate([half(i, u, 0) for u in range(CHUNK)], axis=0)
        return lax.dot_general(keys, q, NT, preferred_element_type=jnp.float32)

    n = length[0]
    full = n // CHUNK
    last = 2 * kv_ref.shape[0] // CHUNK - 1
    opening = sum(jnp.where(blocks[1, k] < CHUNK, 1, 0) for k in range(quarters - 1))
    lax.fori_loop(0, opening + 1, wait, 0)
    sbuf[0] = scores(0)

    def step(i, state, a):
        sbuf[1 - a] = scores(jnp.minimum(i + 1, last))
        return accumulate(state, sbuf[a], values_of(i))

    def two(i, state):
        return step(2 * i + 1, step(2 * i, state, 0), 1)

    def upto(k):
        some = jnp.maximum(blocks[1, k] // CHUNK - 1, 0) // 2
        return jnp.where(k == quarters - 1, full // 2, some)

    def part(k, state):
        lax.fori_loop(jnp.where(k == opening, k + 1, k), k + 1, wait, 0)
        start = jnp.where(k == opening, 0, upto(jnp.maximum(k - 1, 0)))
        return lax.fori_loop(start, upto(k), two, state)

    state = (m_ref[...], l_ref[...], acc_ref[...])
    state = lax.fori_loop(opening, quarters, part, state)
    state = lax.fori_loop(full // 2 * 2, full, lambda i, st: step(i, st, 0), state)

    def tail(i, state):
        position = i * (CHUNK * 128) + lax.broadcasted_iota(jnp.int32, (CHUNK * 128, rows), 0)
        s = jnp.where(position < n * 128, scores(i), -jnp.inf)
        return accumulate(state, s, values_of(i))

    m, l, acc = lax.fori_loop(full, (n + CHUNK - 1) // CHUNK, tail, state)
    context = (acc / l).T.astype(jnp.bfloat16)
    own = tok // 2
    for h in range(heads):
        mine_ref[:, h * HEAD : (h + 1) * HEAD] = context[h * tok : h * tok + own]
        theirs_ref[:, h * HEAD : (h + 1) * HEAD] = context[h * tok + own : (h + 1) * tok]


def attend(start, kv, blocks, length, heads, group):
    q, m, l, acc = start
    rows = q.shape[0]
    out = jax.ShapeDtypeStruct((rows // heads // 2, heads * HEAD), jnp.bfloat16)
    return pl.pallas_call(
        attend_kernel,
        out_shape=(out, out),
        in_specs=[SMEM, SMEM, VMEM, VMEM, VMEM, VMEM, HBM],
        out_specs=(VMEM, VMEM),
        scratch_shapes=[
            pltpu.VMEM((2, CHUNK * 128, rows), jnp.float32),
            pltpu.VMEM((kv.shape[0], 512, 128), kv.dtype),
            pltpu.SemaphoreType.DMA((4,)),
        ],
        compiler_params=limit(50),
        name=f"attend{group}",
    )(blocks, length, q, m, l, acc, kv)


def project_kernel(a_ref, b_ref, wa_any, wb_any, *refs):
    outs, (wa_ref, wb_ref, sems) = refs[:-3], refs[-3:]
    tiles = sems.shape[0]
    tile = wa_ref.shape[1] // tiles
    copies = []
    for j in range(tiles):
        cols = pl.ds(j * tile, tile)
        copies.append(
            (
                pltpu.make_async_copy(wa_any.at[:, cols], wa_ref.at[:, cols], sems.at[j, 0]),
                pltpu.make_async_copy(wb_any.at[:, cols], wb_ref.at[:, cols], sems.at[j, 1]),
            )
        )
        for copy in copies[-1]:
            copy.start()
    for j in range(tiles):
        cols = slice(j * tile, (j + 1) * tile)
        for copy in copies[j]:
            copy.wait()
        total = jnp.dot(a_ref[...], wa_ref[:, cols], preferred_element_type=jnp.float32)
        total += jnp.dot(b_ref[...], wb_ref[:, cols], preferred_element_type=jnp.float32)
        for i, out_ref in enumerate(outs):
            out_ref[:, cols] = total[i * PART : (i + 1) * PART].astype(jnp.bfloat16)


def project(a, b, wa, wb):
    out = jax.ShapeDtypeStruct((PART, wa.shape[1]), jnp.bfloat16)
    parts = a.shape[0] // PART
    return pl.pallas_call(
        project_kernel,
        out_shape=(out,) * parts,
        in_specs=[VMEM, VMEM, HBM, HBM],
        out_specs=(VMEM,) * parts,
        scratch_shapes=[
            pltpu.VMEM(wa.shape, wa.dtype),
            pltpu.VMEM(wb.shape, wb.dtype),
            pltpu.SemaphoreType.DMA((10, 2)),
        ],
        compiler_params=limit(50),
        name=f"project{parts}",
    )(a, b, wa, wb)


def add_kernel(up, down, through_up, through_down, out_up, out_down):
    for own, arrived, out in ((up, through_up, out_up), (down, through_down, out_down)):
        total = own[...].astype(jnp.float32) + arrived[...].astype(jnp.float32)
        out[...] = total.astype(jnp.bfloat16)


def add_arrived(*parts):
    out = jax.ShapeDtypeStruct(parts[0].shape, parts[0].dtype)
    return pl.pallas_call(
        add_kernel,
        out_shape=(out, out),
        in_specs=[VMEM] * 4,
        out_specs=(VMEM, VMEM),
        compiler_params=limit(8),
        name="add",
    )(*parts)


def combine_kernel(top, bottom, far_up, near_down, near_up, far_down, o_ref):
    half = top.shape[0]
    for rows, parts in ((0, (top, far_up, near_down)), (half, (bottom, near_up, far_down))):
        total = sum(part[...].astype(jnp.float32) for part in parts)
        o_ref[rows : rows + half, :] = total.astype(jnp.bfloat16)


def combine(*parts):
    rows, width = parts[0].shape
    return pl.pallas_call(
        combine_kernel,
        out_shape=jax.ShapeDtypeStruct((2 * rows, width), jnp.bfloat16),
        in_specs=[VMEM] * 6,
        out_specs=VMEM,
        compiler_params=limit(8),
        name="combine",
    )(*parts)


def copy_kernel(x_ref, o_ref, buf, sem):
    for source, target in ((x_ref, buf), (buf, o_ref)):
        copy = pltpu.make_async_copy(source, target, sem)
        copy.start()
        copy.wait()


def copy_pool(x):
    return pl.pallas_call(
        copy_kernel,
        out_shape=jax.ShapeDtypeStruct(x.shape, x.dtype),
        in_specs=[HBM],
        out_specs=HBM,
        scratch_shapes=[pltpu.VMEM(x.shape, x.dtype), pltpu.SemaphoreType.DMA],
        compiler_params=limit(4),
        name="copy_pool",
    )(x)


def write_kernel(slots, fresh_ref, kept_ref, out_ref, sems):
    del kept_ref
    for b in range(fresh_ref.shape[0]):

        @pl.when(slots[b] >= 0)
        def _(b=b):
            copy = pltpu.make_async_copy(fresh_ref.at[b], out_ref.at[slots[b]], sems.at[b])
            copy.start()
            copy.wait()


def write_back(slots, fresh, kept):
    return pl.pallas_call(
        write_kernel,
        out_shape=jax.ShapeDtypeStruct(kept.shape, kept.dtype),
        in_specs=[SMEM, VMEM, ANY],
        out_specs=ANY,
        input_output_aliases={2: 0},
        scratch_shapes=[pltpu.SemaphoreType.DMA((fresh.shape[0],))],
        compiler_params=limit(4),
        name="write",
    )(slots, fresh, kept)


def swap_pool(x):
    return lax.all_to_all(x, "pool", split_axis=0, concat_axis=0, tiled=True)


def on_device(
    queries,
    new_key_value,
    saved,
    out_weight,
    hist_owner,
    hist_block,
    hist_len,
    evict,
    dest_owner,
    dest_slot,
):
    pool = lax.axis_size("pool")
    me = lax.axis_index("pool")
    chips = lax.axis_size("tensor") // 2
    chip, core = lax.axis_index("tensor") // 2, lax.axis_index("tensor") % 2
    other_core = [(2 * z + c, 2 * z + 1 - c) for z in range(chips) for c in range(2)]
    upward = [(2 * z + c, 2 * ((z + 1) % chips) + c) for z in range(chips) for c in range(2)]
    downward = [(target, source) for source, target in upward]
    swap = functools.partial(lax.ppermute, axis_name="tensor", perm=other_core)
    send_up = functools.partial(lax.ppermute, axis_name="tensor", perm=upward)
    send_down = functools.partial(lax.ppermute, axis_name="tensor", perm=downward)

    def part(offset, c, half):
        return 128 * ((chip + offset) % chips) + 64 * c + PART * half

    plan = (((2, 0), (2, 1), (1, 1), (3, 0)), ((1, 0), (3, 1)), ((0, 0), (0, 1)))
    base = jnp.stack(
        [part(o, c, h) for parts in plan for c in (core, 1 - core) for o, h in parts]
    ).astype(jnp.int32)

    new_blocks = new_key_value.reshape(-1, 256, 128)
    table, blocks = exchange_table(
        hist_owner, hist_block, hist_len, dest_owner, dest_slot, evict, new_blocks, pool
    )
    arrived = swap_pool(table)
    pool_blocks = split_blocks(saved.reshape(-1, 256, 128))
    told = arrived[:, 32, :].astype(jnp.int32)
    kv = swap_pool(gather_blocks(told, pool_blocks, arrived[:, :32]))
    starts = begin(
        queries, split_blocks(new_blocks), base, [2 * len(parts) for parts in plan]
    )
    other_weight = swap(out_weight)
    kept = copy_pool(saved.reshape(-1, 256, 128))

    heads = queries.shape[1] // HEAD

    def contexts(group, after, before_swap=()):
        used, _ = lax.optimization_barrier((blocks, after))
        mine, theirs = attend(starts[group], kv, used, hist_len, heads, group)
        theirs, _ = lax.optimization_barrier((theirs, before_swap))
        return mine, swap(theirs)

    up, down, near_up, near_down = project(
        *contexts(0, (kept, starts)), out_weight, other_weight
    )
    through_up, through_down = send_up(up), send_down(down)
    near_up, near_down = send_up(near_up), send_down(near_down)
    up, down = project(*contexts(1, up), out_weight, other_weight)

    returned = kv[:, 512:].reshape(pool, 4, 8, 128).transpose(1, 0, 2, 3)
    mine = (told[:, 2:6] == me) & (told[:, 10:11] > 0)
    slots = jnp.max(jnp.where(mine, told[:, 6:10], -1), axis=0)
    returned, _ = lax.optimization_barrier((returned, up))
    pool_out = write_back(slots, returned.reshape(4, 256, 128), kept)
    (up, down), _ = lax.optimization_barrier(((up, down), pool_out))
    up, down = add_arrived(up, down, through_up, through_down)
    far_up, far_down = send_up(up), send_down(down)

    top, bottom = project(
        *contexts(2, up, (near_up, near_down)), out_weight, other_weight
    )
    pool_out = pool_out.reshape(saved.shape)
    attn_out = combine(top, bottom, far_up, near_down, near_up, far_down)
    return attn_out, pool_out


def solution(mesh):
    in_specs = (
        P("pool", "tensor"),
        P("pool", None, "tensor"),
        P("pool", None, None, "tensor"),
        P("tensor", None),
        P("pool", None),
        P("pool", None),
        P("pool"),
        P("pool"),
        P("pool", None),
        P("pool", None),
    )
    out_specs = (P(("pool", "tensor"), None), P("pool", None, None, "tensor"))
    return jax.shard_map(
        on_device, mesh=mesh, in_specs=in_specs, out_specs=out_specs, check_vma=False
    )
```

```python
import functools
import math

import jax
import jax.numpy as jnp
from jax import lax
from jax.experimental import pallas as pl
from jax.experimental.pallas import tpu as pltpu
from jax.sharding import PartitionSpec as P

HEAD = 128
CHUNK = 8
PART = 32
NT = (((1,), (1,)), ((), ()))
SMEM = pl.BlockSpec(memory_space=pltpu.SMEM)
VMEM = pl.BlockSpec(memory_space=pltpu.VMEM)
ANY = pl.BlockSpec(memory_space=pl.ANY)
HBM = pl.BlockSpec(memory_space=pltpu.HBM)


def limit(mebibytes):
    return pltpu.CompilerParams(vmem_limit_bytes=mebibytes * 2**20)


def table_kernel(
    length, dest_owner, dest_slot, evict, owner_ref, block_ref, new_ref, table_ref, list_ref, rows_ref
):
    pool, entries = table_ref.shape[0], owner_ref.shape[1]
    owner = jnp.broadcast_to(owner_ref[...], (pool, entries))
    block = jnp.broadcast_to(block_ref[...], (pool, entries))
    row = lax.broadcasted_iota(jnp.int32, (pool, entries), 0)
    col = lax.broadcasted_iota(jnp.int32, (pool, entries), 1)
    match = owner == row
    first = jnp.min(jnp.where(match, col, entries), axis=1, keepdims=True)
    second = jnp.max(jnp.where(match, col, -1), axis=1, keepdims=True)
    want0 = jnp.sum(jnp.where(match & (col == first), block, 0), axis=1, keepdims=True)
    want1 = jnp.sum(jnp.where(match & (col == second), block, 0), axis=1, keepdims=True)
    row = lax.broadcasted_iota(jnp.int32, (pool, 128), 0)
    lane = lax.broadcasted_iota(jnp.int32, (pool, 128), 1)
    used0 = jnp.where(jnp.broadcast_to(first, (pool, 128)) < length[0], 1, 0)
    used1 = jnp.where(jnp.broadcast_to(second, (pool, 128)) < length[0], 1, 0)
    used = (used0 + used1).astype(jnp.float32)
    earlier = jnp.where(
        lax.broadcasted_iota(jnp.int32, (pool, pool), 1)
        < lax.broadcasted_iota(jnp.int32, (pool, pool), 0),
        1.0,
        0.0,
    )
    before = jnp.dot(earlier, used, preferred_element_type=jnp.float32).astype(jnp.int32)
    place = jnp.where((used0 > 0) & (before == lane), 2 * row, 0)
    place += jnp.where((used1 > 0) & (before + used0 == lane), 2 * row + 1, 0)
    quarter = pool // 4
    counts = jnp.where(row < quarter * (lane + 1), used0 + used1, 0)
    list_ref[...] = jnp.zeros(list_ref.shape, jnp.int32)
    list_ref[0:1] = jnp.sum(place, axis=0, keepdims=True)
    list_ref[1:2] = jnp.sum(counts, axis=0, keepdims=True)

    out = jnp.where(lane == 0, want0, jnp.where(lane == 1, want1, 0))
    for b in range(4):
        out = jnp.where(lane == 2 + b, dest_owner[0, b], out)
        out = jnp.where(lane == 6 + b, dest_slot[0, b], out)
    out = jnp.where(lane == 10, evict[0], out).astype(jnp.float32)
    for b in range(4):
        fresh = new_ref[b].astype(jnp.float32)
        for o in range(pool):
            rows_ref[o, 8 * b : 8 * b + 8, :] = fresh[8 * o : 8 * o + 8]
    for o in range(pool):
        rows_ref[o, 32:48, :] = jnp.broadcast_to(out[o : o + 1], (16, 128))
    table_ref[...] = rows_ref[...].astype(jnp.bfloat16)


def exchange_table(hist_owner, hist_block, hist_len, dest_owner, dest_slot, evict, new_blocks, pool):
    return pl.pallas_call(
        table_kernel,
        out_shape=(
            jax.ShapeDtypeStruct((pool, 48, 128), jnp.bfloat16),
            jax.ShapeDtypeStruct((8, 128), jnp.int32),
        ),
        in_specs=[SMEM, SMEM, SMEM, SMEM, VMEM, VMEM, VMEM],
        out_specs=(VMEM, VMEM),
        scratch_shapes=[pltpu.VMEM((pool, 48, 128), jnp.float32)],
        compiler_params=limit(58),
        name="table",
    )(hist_len, dest_owner, dest_slot, evict, hist_owner, hist_block, new_blocks)


def split_kernel(x_ref, o_ref):
    row = lax.broadcasted_iota(jnp.int32, (128, 256), 0)
    source = lax.broadcasted_iota(jnp.int32, (128, 256), 1)
    pick_k = jnp.where(source == 2 * row, 1.0, 0.0).astype(jnp.bfloat16)
    pick_v = jnp.where(source == 2 * row + 1, 1.0, 0.0).astype(jnp.bfloat16)
    for b in range(x_ref.shape[0]):
        x = x_ref[b]
        k = jnp.dot(pick_k, x, preferred_element_type=jnp.float32)
        v = jnp.dot(pick_v, x, preferred_element_type=jnp.float32)
        o_ref[b, 0:128, :] = k.astype(jnp.bfloat16)
        o_ref[b, 128:256, :] = v.T.astype(jnp.bfloat16)


def split_blocks(x):
    return pl.pallas_call(
        split_kernel,
        out_shape=jax.ShapeDtypeStruct(x.shape, x.dtype),
        in_specs=[VMEM],
        out_specs=VMEM,
        compiler_params=limit(12),
        name=f"split{x.shape[0]}",
    )(x)


def gather_kernel(told, pool_ref, held_ref, out_ref, held, onward, packed, sems):
    pool, rows = packed.shape[:2]
    copies = []
    for p in range(pool):
        for r in range(2):
            copies.append(
                pltpu.make_async_copy(
                    pool_ref.at[told[p, r]], out_ref.at[p, pl.ds(256 * r, 256)], sems.at[2 * p + r]
                )
            )
            copies[-1].start()
    held[...] = held_ref[...].astype(jnp.float32)
    for b in range(4):
        for p in range(pool):
            onward[told[p, 2 + b], 8 * b : 8 * b + 8, :] = held[p, 8 * b : 8 * b + 8, :]
    packed[...] = onward[...].astype(jnp.bfloat16)
    copies.append(
        pltpu.make_async_copy(packed, out_ref.at[:, pl.ds(512, rows)], sems.at[2 * pool])
    )
    copies[-1].start()
    for copy in copies:
        copy.wait()


def gather_blocks(told, pool_blocks, held):
    pool, rows, _ = held.shape
    return pl.pallas_call(
        gather_kernel,
        out_shape=jax.ShapeDtypeStruct((pool, 512 + rows, 128), pool_blocks.dtype),
        in_specs=[SMEM, VMEM, VMEM],
        out_specs=HBM,
        scratch_shapes=[
            pltpu.VMEM(held.shape, jnp.float32),
            pltpu.VMEM(held.shape, jnp.float32),
            pltpu.VMEM(held.shape, jnp.bfloat16),
            pltpu.SemaphoreType.DMA((2 * pool + 1,)),
        ],
        compiler_params=limit(51),
        name="gather",
    )(told, pool_blocks, held)


def accumulate(state, s, vt):
    m, l, acc = state
    c = math.log2(math.e) / math.sqrt(HEAD)
    top = jnp.maximum(m, jnp.max(s, axis=0, keepdims=True))
    p = jnp.exp2(s * c - top * c)
    keep = jnp.exp2((m - top) * c)
    l = l * keep + jnp.sum(p, axis=0, keepdims=True)
    acc = acc * keep + jnp.dot(vt, p.astype(jnp.bfloat16), preferred_element_type=jnp.float32)
    return top, l, acc


def begin_kernel(base, q_ref, new_ref, *refs):
    c = math.log2(math.e) / math.sqrt(HEAD)
    heads = q_ref.shape[1] // HEAD
    blocks = new_ref.shape[0]
    k = jnp.concatenate([new_ref[i, 0:128, :] for i in range(blocks)], axis=0)
    vt = jnp.concatenate([new_ref[i, 128:256, :] for i in range(blocks)], axis=1)
    before = 0
    for group in range(len(refs) // 4):
        out_q, out_m, out_l, out_acc = refs[4 * group : 4 * group + 4]
        rows = out_q.shape[0]
        tok = rows // heads
        parts = tok // PART
        key = lax.broadcasted_iota(jnp.int32, (blocks * 128, rows), 0)
        at = lax.broadcasted_iota(jnp.int32, (1, rows), 1) & (tok - 1)
        token = base[before] + at
        for i in range(1, parts):
            token = jnp.where(at >= PART * i, base[before + i] + at - PART * i, token)
        for i in range(parts):
            first = pl.multiple_of(base[before + i], PART)
            for h in range(heads):
                out_q[pl.ds(h * tok + i * PART, PART), :] = q_ref[
                    pl.ds(first, PART), h * HEAD : (h + 1) * HEAD
                ]
        s = lax.dot_general(k, out_q[...], NT, preferred_element_type=jnp.float32)
        s = jnp.where(key <= token, s, -jnp.inf)
        m = jnp.max(s, axis=0, keepdims=True)
        p = jnp.exp2(s * c - m * c)
        out_m[...] = m
        out_l[...] = jnp.sum(p, axis=0, keepdims=True)
        out_acc[...] = jnp.dot(vt, p.astype(jnp.bfloat16), preferred_element_type=jnp.float32)
        before += parts


def begin(queries, fresh, base, sizes):
    out_shape = ()
    for parts in sizes:
        rows = parts * PART * queries.shape[1] // HEAD
        out_shape += (
            jax.ShapeDtypeStruct((rows, HEAD), queries.dtype),
            jax.ShapeDtypeStruct((1, rows), jnp.float32),
            jax.ShapeDtypeStruct((1, rows), jnp.float32),
            jax.ShapeDtypeStruct((HEAD, rows), jnp.float32),
        )
    out = pl.pallas_call(
        begin_kernel,
        out_shape=out_shape,
        in_specs=[SMEM, VMEM, VMEM],
        out_specs=(VMEM,) * len(out_shape),
        compiler_params=limit(24),
        name="begin",
    )(base, queries, fresh)
    return [out[4 * g : 4 * g + 4] for g in range(len(sizes))]


def attend_kernel(
    blocks, length, q_ref, m_ref, l_ref, acc_ref, kv_any, mine_ref, theirs_ref, sbuf, kv_ref, sems
):
    quarters = sems.shape[0]
    share = kv_ref.shape[0] // quarters

    def quarter(k):
        owners = pl.ds(pl.multiple_of(k * share, share), share)
        return pltpu.make_async_copy(
            kv_any.at[owners, pl.ds(0, kv_ref.shape[1])], kv_ref.at[owners], sems.at[k]
        )

    def wait(k, _):
        quarter(k).wait()
        return 0

    for k in range(quarters):
        quarter(k).start()
    rows = q_ref.shape[0]
    tok = mine_ref.shape[0] * 2
    heads = rows // tok
    q = q_ref[...]

    def half(i, u, value):
        place = blocks[0, i * CHUNK + u]
        start = pl.multiple_of((place % 2) * 256 + 128 * value, 128)
        return kv_ref[place // 2, pl.ds(start, 128), :]

    def values_of(i):
        return jnp.concatenate([half(i, u, 1) for u in range(CHUNK)], axis=1)

    def scores(i):
        keys = jnp.concatenate([half(i, u, 0) for u in range(CHUNK)], axis=0)
        return lax.dot_general(keys, q, NT, preferred_element_type=jnp.float32)

    n = length[0]
    full = n // CHUNK
    last = 2 * kv_ref.shape[0] // CHUNK - 1
    opening = sum(jnp.where(blocks[1, k] < CHUNK, 1, 0) for k in range(quarters - 1))
    lax.fori_loop(0, opening + 1, wait, 0)
    sbuf[0] = scores(0)

    def step(i, state, a):
        sbuf[1 - a] = scores(jnp.minimum(i + 1, last))
        return accumulate(state, sbuf[a], values_of(i))

    def two(i, state):
        return step(2 * i + 1, step(2 * i, state, 0), 1)

    def upto(k):
        some = jnp.maximum(blocks[1, k] // CHUNK - 1, 0) // 2
        return jnp.where(k == quarters - 1, full // 2, some)

    def part(k, state):
        lax.fori_loop(jnp.where(k == opening, k + 1, k), k + 1, wait, 0)
        start = jnp.where(k == opening, 0, upto(jnp.maximum(k - 1, 0)))
        return lax.fori_loop(start, upto(k), two, state)

    state = (m_ref[...], l_ref[...], acc_ref[...])
    state = lax.fori_loop(opening, quarters, part, state)
    state = lax.fori_loop(full // 2 * 2, full, lambda i, st: step(i, st, 0), state)

    def tail(i, state):
        position = i * (CHUNK * 128) + lax.broadcasted_iota(jnp.int32, (CHUNK * 128, rows), 0)
        s = jnp.where(position < n * 128, scores(i), -jnp.inf)
        return accumulate(state, s, values_of(i))

    m, l, acc = lax.fori_loop(full, (n + CHUNK - 1) // CHUNK, tail, state)
    context = (acc / l).T.astype(jnp.bfloat16)
    own = tok // 2
    for h in range(heads):
        mine_ref[:, h * HEAD : (h + 1) * HEAD] = context[h * tok : h * tok + own]
        theirs_ref[:, h * HEAD : (h + 1) * HEAD] = context[h * tok + own : (h + 1) * tok]


def attend(start, kv, blocks, length, heads, group):
    q, m, l, acc = start
    rows = q.shape[0]
    out = jax.ShapeDtypeStruct((rows // heads // 2, heads * HEAD), jnp.bfloat16)
    return pl.pallas_call(
        attend_kernel,
        out_shape=(out, out),
        in_specs=[SMEM, SMEM, VMEM, VMEM, VMEM, VMEM, HBM],
        out_specs=(VMEM, VMEM),
        scratch_shapes=[
            pltpu.VMEM((2, CHUNK * 128, rows), jnp.float32),
            pltpu.VMEM((kv.shape[0], 512, 128), kv.dtype),
            pltpu.SemaphoreType.DMA((4,)),
        ],
        compiler_params=limit(50),
        name=f"attend{group}",
    )(blocks, length, q, m, l, acc, kv)


def project_kernel(a_ref, b_ref, wa_any, wb_any, *refs):
    outs, (wa_ref, wb_ref, sems) = refs[:-3], refs[-3:]
    half = a_ref.shape[0] // 2
    tiles = sems.shape[0]
    tile = wa_ref.shape[1] // tiles
    copies = []
    for j in range(tiles):
        cols = pl.ds(j * tile, tile)
        copies.append(
            (
                pltpu.make_async_copy(wa_any.at[:, cols], wa_ref.at[:, cols], sems.at[j, 0]),
                pltpu.make_async_copy(wb_any.at[:, cols], wb_ref.at[:, cols], sems.at[j, 1]),
            )
        )
        for copy in copies[-1]:
            copy.start()
    for j in range(tiles):
        cols = slice(j * tile, (j + 1) * tile)
        for copy in copies[j]:
            copy.wait()
        total = jnp.dot(a_ref[...], wa_ref[:, cols], preferred_element_type=jnp.float32)
        total += jnp.dot(b_ref[...], wb_ref[:, cols], preferred_element_type=jnp.float32)
        for i, out_ref in enumerate(outs):
            out_ref[:, cols] = total[i * half : (i + 1) * half].astype(jnp.bfloat16)


def project(a, b, wa, wb):
    out = jax.ShapeDtypeStruct((a.shape[0] // 2, wa.shape[1]), jnp.bfloat16)
    return pl.pallas_call(
        project_kernel,
        out_shape=(out, out),
        in_specs=[VMEM, VMEM, HBM, HBM],
        out_specs=(VMEM, VMEM),
        scratch_shapes=[
            pltpu.VMEM(wa.shape, wa.dtype),
            pltpu.VMEM(wb.shape, wb.dtype),
            pltpu.SemaphoreType.DMA((10, 2)),
        ],
        compiler_params=limit(50),
        name=f"project{a.shape[0]}",
    )(a, b, wa, wb)


def add_kernel(up, down, from_below, from_above, out_up, out_down):
    for own, arrived, out in ((up, from_below, out_up), (down, from_above, out_down)):
        total = own[...].astype(jnp.float32) + arrived[0:PART, :].astype(jnp.float32)
        out[...] = total.astype(jnp.bfloat16)


def add_arrived(*parts):
    out = jax.ShapeDtypeStruct(parts[0].shape, parts[0].dtype)
    return pl.pallas_call(
        add_kernel,
        out_shape=(out, out),
        in_specs=[VMEM] * 4,
        out_specs=(VMEM, VMEM),
        compiler_params=limit(8),
        name="add",
    )(*parts)


def combine_kernel(top, bottom, far_up, from_above, from_below, far_down, o_ref):
    near = pl.ds(PART, PART)
    for rows, own, far, arrived in (
        (0, top, far_up, from_above),
        (PART, bottom, far_down, from_below),
    ):
        total = own[...].astype(jnp.float32) + far[...].astype(jnp.float32)
        total += arrived[near, :].astype(jnp.float32)
        o_ref[rows : rows + PART, :] = total.astype(jnp.bfloat16)


def combine(*parts):
    rows, width = parts[0].shape
    return pl.pallas_call(
        combine_kernel,
        out_shape=jax.ShapeDtypeStruct((2 * rows, width), jnp.bfloat16),
        in_specs=[VMEM] * 6,
        out_specs=VMEM,
        compiler_params=limit(8),
        name="combine",
    )(*parts)


def copy_kernel(x_ref, o_ref, buf, sem):
    for source, target in ((x_ref, buf), (buf, o_ref)):
        copy = pltpu.make_async_copy(source, target, sem)
        copy.start()
        copy.wait()


def copy_pool(x):
    return pl.pallas_call(
        copy_kernel,
        out_shape=jax.ShapeDtypeStruct(x.shape, x.dtype),
        in_specs=[HBM],
        out_specs=HBM,
        scratch_shapes=[pltpu.VMEM(x.shape, x.dtype), pltpu.SemaphoreType.DMA],
        compiler_params=limit(4),
        name="copy_pool",
    )(x)


def write_kernel(slots, fresh_ref, kept_ref, out_ref, sems):
    del kept_ref
    for b in range(fresh_ref.shape[0]):

        @pl.when(slots[b] >= 0)
        def _(b=b):
            copy = pltpu.make_async_copy(fresh_ref.at[b], out_ref.at[slots[b]], sems.at[b])
            copy.start()
            copy.wait()


def write_back(slots, fresh, kept):
    return pl.pallas_call(
        write_kernel,
        out_shape=jax.ShapeDtypeStruct(kept.shape, kept.dtype),
        in_specs=[SMEM, VMEM, ANY],
        out_specs=ANY,
        input_output_aliases={2: 0},
        scratch_shapes=[pltpu.SemaphoreType.DMA((fresh.shape[0],))],
        compiler_params=limit(4),
        name="write",
    )(slots, fresh, kept)


def swap_pool(x):
    return lax.all_to_all(x, "pool", split_axis=0, concat_axis=0, tiled=True)


def on_device(
    queries,
    new_key_value,
    saved,
    out_weight,
    hist_owner,
    hist_block,
    hist_len,
    evict,
    dest_owner,
    dest_slot,
):
    pool = lax.axis_size("pool")
    me = lax.axis_index("pool")
    chips = lax.axis_size("tensor") // 2
    chip, core = lax.axis_index("tensor") // 2, lax.axis_index("tensor") % 2
    other_core = [(2 * z + c, 2 * z + 1 - c) for z in range(chips) for c in range(2)]
    upward = [(2 * z + c, 2 * ((z + 1) % chips) + c) for z in range(chips) for c in range(2)]
    downward = [(target, source) for source, target in upward]
    swap = functools.partial(lax.ppermute, axis_name="tensor", perm=other_core)
    send_up = functools.partial(lax.ppermute, axis_name="tensor", perm=upward)
    send_down = functools.partial(lax.ppermute, axis_name="tensor", perm=downward)

    def part(offset, c, half):
        return 128 * ((chip + offset) % chips) + 64 * c + PART * half

    plan = (((2, 0), (1, 1), (2, 1), (3, 0)), ((1, 0), (3, 1)), ((0, 0), (0, 1)))
    base = jnp.stack(
        [part(o, c, h) for parts in plan for c in (core, 1 - core) for o, h in parts]
    ).astype(jnp.int32)

    new_blocks = new_key_value.reshape(-1, 256, 128)
    table, blocks = exchange_table(
        hist_owner, hist_block, hist_len, dest_owner, dest_slot, evict, new_blocks, pool
    )
    arrived = swap_pool(table)
    pool_blocks = split_blocks(saved.reshape(-1, 256, 128))
    told = arrived[:, 32, :].astype(jnp.int32)
    kv = swap_pool(gather_blocks(told, pool_blocks, arrived[:, :32]))
    starts = begin(
        queries, split_blocks(new_blocks), base, [2 * len(parts) for parts in plan]
    )
    other_weight = swap(out_weight)
    kept = copy_pool(saved.reshape(-1, 256, 128))

    heads = queries.shape[1] // HEAD

    def contexts(group, after):
        used, _ = lax.optimization_barrier((blocks, after))
        mine, theirs = attend(starts[group], kv, used, hist_len, heads, group)
        return mine, swap(theirs)

    up, down = project(*contexts(0, (kept, starts)), out_weight, other_weight)
    from_below, from_above = send_up(up), send_down(down)
    up, down = project(*contexts(1, up), out_weight, other_weight)

    returned = kv[:, 512:].reshape(pool, 4, 8, 128).transpose(1, 0, 2, 3)
    mine = (told[:, 2:6] == me) & (told[:, 10:11] > 0)
    slots = jnp.max(jnp.where(mine, told[:, 6:10], -1), axis=0)
    returned, _ = lax.optimization_barrier((returned, up))
    pool_out = write_back(slots, returned.reshape(4, 256, 128), kept)
    (up, down), _ = lax.optimization_barrier(((up, down), pool_out))
    up, down = add_arrived(up, down, from_below, from_above)
    far_up, far_down = send_up(up), send_down(down)

    top, bottom = project(
        *contexts(2, up), out_weight, other_weight
    )
    pool_out = pool_out.reshape(saved.shape)
    attn_out = combine(top, bottom, far_up, from_above, from_below, far_down)
    return attn_out, pool_out


def solution(mesh):
    in_specs = (
        P("pool", "tensor"),
        P("pool", None, "tensor"),
        P("pool", None, None, "tensor"),
        P("tensor", None),
        P("pool", None),
        P("pool", None),
        P("pool"),
        P("pool"),
        P("pool", None),
        P("pool", None),
    )
    out_specs = (P(("pool", "tensor"), None), P("pool", None, None, "tensor"))
    return jax.shard_map(
        on_device, mesh=mesh, in_specs=in_specs, out_specs=out_specs, check_vma=False
    )
```

```python
import functools
import math

import jax
import jax.numpy as jnp
from jax import lax
from jax.experimental import pallas as pl
from jax.experimental.pallas import tpu as pltpu
from jax.sharding import PartitionSpec as P

HEAD = 128
CHUNK = 8
PART = 32
NT = (((1,), (1,)), ((), ()))
SMEM = pl.BlockSpec(memory_space=pltpu.SMEM)
VMEM = pl.BlockSpec(memory_space=pltpu.VMEM)
ANY = pl.BlockSpec(memory_space=pl.ANY)
HBM = pl.BlockSpec(memory_space=pltpu.HBM)


def limit(mebibytes):
    return pltpu.CompilerParams(vmem_limit_bytes=mebibytes * 2**20)


def table_kernel(
    length, dest_owner, dest_slot, evict, owner_ref, block_ref, new_ref, table_ref, list_ref, rows_ref
):
    pool, entries = table_ref.shape[0], owner_ref.shape[1]
    owner = jnp.broadcast_to(owner_ref[...], (pool, entries))
    block = jnp.broadcast_to(block_ref[...], (pool, entries))
    row = lax.broadcasted_iota(jnp.int32, (pool, entries), 0)
    col = lax.broadcasted_iota(jnp.int32, (pool, entries), 1)
    match = owner == row
    first = jnp.min(jnp.where(match, col, entries), axis=1, keepdims=True)
    second = jnp.max(jnp.where(match, col, -1), axis=1, keepdims=True)
    want0 = jnp.sum(jnp.where(match & (col == first), block, 0), axis=1, keepdims=True)
    want1 = jnp.sum(jnp.where(match & (col == second), block, 0), axis=1, keepdims=True)
    row = lax.broadcasted_iota(jnp.int32, (pool, 128), 0)
    lane = lax.broadcasted_iota(jnp.int32, (pool, 128), 1)
    used0 = jnp.where(jnp.broadcast_to(first, (pool, 128)) < length[0], 1, 0)
    used1 = jnp.where(jnp.broadcast_to(second, (pool, 128)) < length[0], 1, 0)
    used = (used0 + used1).astype(jnp.float32)
    earlier = jnp.where(
        lax.broadcasted_iota(jnp.int32, (pool, pool), 1)
        < lax.broadcasted_iota(jnp.int32, (pool, pool), 0),
        1.0,
        0.0,
    )
    before = jnp.dot(earlier, used, preferred_element_type=jnp.float32).astype(jnp.int32)
    place = jnp.where((used0 > 0) & (before == lane), 2 * row, 0)
    place += jnp.where((used1 > 0) & (before + used0 == lane), 2 * row + 1, 0)
    quarter = pool // 4
    counts = jnp.where(row < quarter * (lane + 1), used0 + used1, 0)
    list_ref[...] = jnp.zeros(list_ref.shape, jnp.int32)
    list_ref[0:1] = jnp.sum(place, axis=0, keepdims=True)
    list_ref[1:2] = jnp.sum(counts, axis=0, keepdims=True)

    out = jnp.where(lane == 0, want0, jnp.where(lane == 1, want1, 0))
    for b in range(4):
        out = jnp.where(lane == 2 + b, dest_owner[0, b], out)
        out = jnp.where(lane == 6 + b, dest_slot[0, b], out)
    out = jnp.where(lane == 10, evict[0], out).astype(jnp.float32)
    for b in range(4):
        fresh = new_ref[b].astype(jnp.float32)
        for o in range(pool):
            rows_ref[o, 8 * b : 8 * b + 8, :] = fresh[8 * o : 8 * o + 8]
    for o in range(pool):
        rows_ref[o, 32:48, :] = jnp.broadcast_to(out[o : o + 1], (16, 128))
    table_ref[...] = rows_ref[...].astype(jnp.bfloat16)


def exchange_table(hist_owner, hist_block, hist_len, dest_owner, dest_slot, evict, new_blocks, pool):
    return pl.pallas_call(
        table_kernel,
        out_shape=(
            jax.ShapeDtypeStruct((pool, 48, 128), jnp.bfloat16),
            jax.ShapeDtypeStruct((8, 128), jnp.int32),
        ),
        in_specs=[SMEM, SMEM, SMEM, SMEM, VMEM, VMEM, VMEM],
        out_specs=(VMEM, VMEM),
        scratch_shapes=[pltpu.VMEM((pool, 48, 128), jnp.float32)],
        compiler_params=limit(58),
        name="table",
    )(hist_len, dest_owner, dest_slot, evict, hist_owner, hist_block, new_blocks)


def split_kernel(x_ref, o_ref):
    row = lax.broadcasted_iota(jnp.int32, (128, 256), 0)
    source = lax.broadcasted_iota(jnp.int32, (128, 256), 1)
    pick_k = jnp.where(source == 2 * row, 1.0, 0.0).astype(jnp.bfloat16)
    pick_v = jnp.where(source == 2 * row + 1, 1.0, 0.0).astype(jnp.bfloat16)
    for b in range(x_ref.shape[0]):
        x = x_ref[b]
        k = jnp.dot(pick_k, x, preferred_element_type=jnp.float32)
        v = jnp.dot(pick_v, x, preferred_element_type=jnp.float32)
        o_ref[b, 0:128, :] = k.astype(jnp.bfloat16)
        o_ref[b, 128:256, :] = v.T.astype(jnp.bfloat16)


def split_blocks(x):
    return pl.pallas_call(
        split_kernel,
        out_shape=jax.ShapeDtypeStruct(x.shape, x.dtype),
        in_specs=[VMEM],
        out_specs=VMEM,
        compiler_params=limit(12),
        name=f"split{x.shape[0]}",
    )(x)


def gather_kernel(told, pool_ref, held_ref, out_ref, held, onward, packed, sems):
    pool, rows = packed.shape[:2]
    copies = []
    for p in range(pool):
        for r in range(2):
            copies.append(
                pltpu.make_async_copy(
                    pool_ref.at[told[p, r]], out_ref.at[p, pl.ds(256 * r, 256)], sems.at[2 * p + r]
                )
            )
            copies[-1].start()
    held[...] = held_ref[...].astype(jnp.float32)
    for b in range(4):
        for p in range(pool):
            onward[told[p, 2 + b], 8 * b : 8 * b + 8, :] = held[p, 8 * b : 8 * b + 8, :]
    packed[...] = onward[...].astype(jnp.bfloat16)
    copies.append(
        pltpu.make_async_copy(packed, out_ref.at[:, pl.ds(512, rows)], sems.at[2 * pool])
    )
    copies[-1].start()
    for copy in copies:
        copy.wait()


def gather_blocks(told, pool_blocks, held):
    pool, rows, _ = held.shape
    return pl.pallas_call(
        gather_kernel,
        out_shape=jax.ShapeDtypeStruct((pool, 512 + rows, 128), pool_blocks.dtype),
        in_specs=[SMEM, VMEM, VMEM],
        out_specs=HBM,
        scratch_shapes=[
            pltpu.VMEM(held.shape, jnp.float32),
            pltpu.VMEM(held.shape, jnp.float32),
            pltpu.VMEM(held.shape, jnp.bfloat16),
            pltpu.SemaphoreType.DMA((2 * pool + 1,)),
        ],
        compiler_params=limit(51),
        name="gather",
    )(told, pool_blocks, held)


def accumulate(state, s, vt):
    m, l, acc = state
    c = math.log2(math.e) / math.sqrt(HEAD)
    top = jnp.maximum(m, jnp.max(s, axis=0, keepdims=True))
    p = jnp.exp2(s * c - top * c)
    keep = jnp.exp2((m - top) * c)
    l = l * keep + jnp.sum(p, axis=0, keepdims=True)
    acc = acc * keep + jnp.dot(vt, p.astype(jnp.bfloat16), preferred_element_type=jnp.float32)
    return top, l, acc


def begin_kernel(base, q_ref, new_ref, *refs):
    c = math.log2(math.e) / math.sqrt(HEAD)
    heads = q_ref.shape[1] // HEAD
    blocks = new_ref.shape[0]
    k = jnp.concatenate([new_ref[i, 0:128, :] for i in range(blocks)], axis=0)
    vt = jnp.concatenate([new_ref[i, 128:256, :] for i in range(blocks)], axis=1)
    before = 0
    for group in range(len(refs) // 4):
        out_q, out_m, out_l, out_acc = refs[4 * group : 4 * group + 4]
        rows = out_q.shape[0]
        tok = rows // heads
        parts = tok // PART
        key = lax.broadcasted_iota(jnp.int32, (blocks * 128, rows), 0)
        at = lax.broadcasted_iota(jnp.int32, (1, rows), 1) & (tok - 1)
        token = base[before] + at
        for i in range(1, parts):
            token = jnp.where(at >= PART * i, base[before + i] + at - PART * i, token)
        for i in range(parts):
            first = pl.multiple_of(base[before + i], PART)
            for h in range(heads):
                out_q[pl.ds(h * tok + i * PART, PART), :] = q_ref[
                    pl.ds(first, PART), h * HEAD : (h + 1) * HEAD
                ]
        s = lax.dot_general(k, out_q[...], NT, preferred_element_type=jnp.float32)
        s = jnp.where(key <= token, s, -jnp.inf)
        m = jnp.max(s, axis=0, keepdims=True)
        p = jnp.exp2(s * c - m * c)
        out_m[...] = m
        out_l[...] = jnp.sum(p, axis=0, keepdims=True)
        out_acc[...] = jnp.dot(vt, p.astype(jnp.bfloat16), preferred_element_type=jnp.float32)
        before += parts


def begin(queries, fresh, base, sizes):
    out_shape = ()
    for parts in sizes:
        rows = parts * PART * queries.shape[1] // HEAD
        out_shape += (
            jax.ShapeDtypeStruct((rows, HEAD), queries.dtype),
            jax.ShapeDtypeStruct((1, rows), jnp.float32),
            jax.ShapeDtypeStruct((1, rows), jnp.float32),
            jax.ShapeDtypeStruct((HEAD, rows), jnp.float32),
        )
    out = pl.pallas_call(
        begin_kernel,
        out_shape=out_shape,
        in_specs=[SMEM, VMEM, VMEM],
        out_specs=(VMEM,) * len(out_shape),
        compiler_params=limit(24),
        name="begin",
    )(base, queries, fresh)
    return [out[4 * g : 4 * g + 4] for g in range(len(sizes))]


def attend_kernel(
    blocks, length, q_ref, m_ref, l_ref, acc_ref, kv_any, mine_ref, theirs_ref, sbuf, kv_ref, sems
):
    quarters = sems.shape[0]
    share = kv_ref.shape[0] // quarters

    def quarter(k):
        owners = pl.ds(pl.multiple_of(k * share, share), share)
        return pltpu.make_async_copy(
            kv_any.at[owners, pl.ds(0, kv_ref.shape[1])], kv_ref.at[owners], sems.at[k]
        )

    def wait(k, _):
        quarter(k).wait()
        return 0

    for k in range(quarters):
        quarter(k).start()
    rows = q_ref.shape[0]
    tok = mine_ref.shape[0] * 2
    heads = rows // tok
    q = q_ref[...]

    def half(i, u, value):
        place = blocks[0, i * CHUNK + u]
        start = pl.multiple_of((place % 2) * 256 + 128 * value, 128)
        return kv_ref[place // 2, pl.ds(start, 128), :]

    def values_of(i):
        return jnp.concatenate([half(i, u, 1) for u in range(CHUNK)], axis=1)

    def scores(i):
        keys = jnp.concatenate([half(i, u, 0) for u in range(CHUNK)], axis=0)
        return lax.dot_general(keys, q, NT, preferred_element_type=jnp.float32)

    n = length[0]
    full = n // CHUNK
    last = 2 * kv_ref.shape[0] // CHUNK - 1
    opening = sum(jnp.where(blocks[1, k] < CHUNK, 1, 0) for k in range(quarters - 1))
    lax.fori_loop(0, opening + 1, wait, 0)
    sbuf[0] = scores(0)

    def step(i, state, a):
        sbuf[1 - a] = scores(jnp.minimum(i + 1, last))
        return accumulate(state, sbuf[a], values_of(i))

    def two(i, state):
        return step(2 * i + 1, step(2 * i, state, 0), 1)

    def upto(k):
        some = jnp.maximum(blocks[1, k] // CHUNK - 1, 0) // 2
        return jnp.where(k == quarters - 1, full // 2, some)

    def part(k, state):
        lax.fori_loop(jnp.where(k == opening, k + 1, k), k + 1, wait, 0)
        start = jnp.where(k == opening, 0, upto(jnp.maximum(k - 1, 0)))
        return lax.fori_loop(start, upto(k), two, state)

    state = (m_ref[...], l_ref[...], acc_ref[...])
    state = lax.fori_loop(opening, quarters, part, state)
    state = lax.fori_loop(full // 2 * 2, full, lambda i, st: step(i, st, 0), state)

    def tail(i, state):
        position = i * (CHUNK * 128) + lax.broadcasted_iota(jnp.int32, (CHUNK * 128, rows), 0)
        s = jnp.where(position < n * 128, scores(i), -jnp.inf)
        return accumulate(state, s, values_of(i))

    m, l, acc = lax.fori_loop(full, (n + CHUNK - 1) // CHUNK, tail, state)
    context = (acc / l).T.astype(jnp.bfloat16)
    own = tok // 2
    for h in range(heads):
        mine_ref[:, h * HEAD : (h + 1) * HEAD] = context[h * tok : h * tok + own]
        theirs_ref[:, h * HEAD : (h + 1) * HEAD] = context[h * tok + own : (h + 1) * tok]


def attend(start, kv, blocks, length, heads, group):
    q, m, l, acc = start
    rows = q.shape[0]
    out = jax.ShapeDtypeStruct((rows // heads // 2, heads * HEAD), jnp.bfloat16)
    return pl.pallas_call(
        attend_kernel,
        out_shape=(out, out),
        in_specs=[SMEM, SMEM, VMEM, VMEM, VMEM, VMEM, HBM],
        out_specs=(VMEM, VMEM),
        scratch_shapes=[
            pltpu.VMEM((2, CHUNK * 128, rows), jnp.float32),
            pltpu.VMEM((kv.shape[0], 512, 128), kv.dtype),
            pltpu.SemaphoreType.DMA((4,)),
        ],
        compiler_params=limit(50),
        name=f"attend{group}",
    )(blocks, length, q, m, l, acc, kv)


def project_kernel(a_ref, b_ref, wa_any, wb_any, *refs):
    outs, (wa_ref, wb_ref, sems) = refs[:-3], refs[-3:]
    tiles = sems.shape[0]
    tile = wa_ref.shape[1] // tiles
    copies = []
    for j in range(tiles):
        cols = pl.ds(j * tile, tile)
        copies.append(
            (
                pltpu.make_async_copy(wa_any.at[:, cols], wa_ref.at[:, cols], sems.at[j, 0]),
                pltpu.make_async_copy(wb_any.at[:, cols], wb_ref.at[:, cols], sems.at[j, 1]),
            )
        )
        for copy in copies[-1]:
            copy.start()
    for j in range(tiles):
        cols = slice(j * tile, (j + 1) * tile)
        for copy in copies[j]:
            copy.wait()
        total = jnp.dot(a_ref[...], wa_ref[:, cols], preferred_element_type=jnp.float32)
        total += jnp.dot(b_ref[...], wb_ref[:, cols], preferred_element_type=jnp.float32)
        for i, out_ref in enumerate(outs):
            out_ref[:, cols] = total[i * PART : (i + 1) * PART].astype(jnp.bfloat16)


def project(a, b, wa, wb):
    out = jax.ShapeDtypeStruct((PART, wa.shape[1]), jnp.bfloat16)
    parts = a.shape[0] // PART
    return pl.pallas_call(
        project_kernel,
        out_shape=(out,) * parts,
        in_specs=[VMEM, VMEM, HBM, HBM],
        out_specs=(VMEM,) * parts,
        scratch_shapes=[
            pltpu.VMEM(wa.shape, wa.dtype),
            pltpu.VMEM(wb.shape, wb.dtype),
            pltpu.SemaphoreType.DMA((10, 2)),
        ],
        compiler_params=limit(50),
        name=f"project{parts}",
    )(a, b, wa, wb)


def add_kernel(up, down, through_up, through_down, out_up, out_down):
    for own, arrived, out in ((up, through_up, out_up), (down, through_down, out_down)):
        total = own[...].astype(jnp.float32) + arrived[...].astype(jnp.float32)
        out[...] = total.astype(jnp.bfloat16)


def add_arrived(*parts):
    out = jax.ShapeDtypeStruct(parts[0].shape, parts[0].dtype)
    return pl.pallas_call(
        add_kernel,
        out_shape=(out, out),
        in_specs=[VMEM] * 4,
        out_specs=(VMEM, VMEM),
        compiler_params=limit(8),
        name="add",
    )(*parts)


def combine_kernel(top, bottom, far_up, near_down, near_up, far_down, o_ref):
    half = top.shape[0]
    for rows, parts in ((0, (top, far_up, near_down)), (half, (bottom, near_up, far_down))):
        total = sum(part[...].astype(jnp.float32) for part in parts)
        o_ref[rows : rows + half, :] = total.astype(jnp.bfloat16)


def combine(*parts):
    rows, width = parts[0].shape
    return pl.pallas_call(
        combine_kernel,
        out_shape=jax.ShapeDtypeStruct((2 * rows, width), jnp.bfloat16),
        in_specs=[VMEM] * 6,
        out_specs=VMEM,
        compiler_params=limit(8),
        name="combine",
    )(*parts)


def copy_kernel(x_ref, o_ref, buf, sem):
    for source, target in ((x_ref, buf), (buf, o_ref)):
        copy = pltpu.make_async_copy(source, target, sem)
        copy.start()
        copy.wait()


def copy_pool(x):
    return pl.pallas_call(
        copy_kernel,
        out_shape=jax.ShapeDtypeStruct(x.shape, x.dtype),
        in_specs=[HBM],
        out_specs=HBM,
        scratch_shapes=[pltpu.VMEM(x.shape, x.dtype), pltpu.SemaphoreType.DMA],
        compiler_params=limit(4),
        name="copy_pool",
    )(x)


def write_kernel(slots, fresh_ref, kept_ref, out_ref, sems):
    del kept_ref
    for b in range(fresh_ref.shape[0]):

        @pl.when(slots[b] >= 0)
        def _(b=b):
            copy = pltpu.make_async_copy(fresh_ref.at[b], out_ref.at[slots[b]], sems.at[b])
            copy.start()
            copy.wait()


def write_back(slots, fresh, kept):
    return pl.pallas_call(
        write_kernel,
        out_shape=jax.ShapeDtypeStruct(kept.shape, kept.dtype),
        in_specs=[SMEM, VMEM, ANY],
        out_specs=ANY,
        input_output_aliases={2: 0},
        scratch_shapes=[pltpu.SemaphoreType.DMA((fresh.shape[0],))],
        compiler_params=limit(4),
        name="write",
    )(slots, fresh, kept)


def swap_pool(x):
    return lax.all_to_all(x, "pool", split_axis=0, concat_axis=0, tiled=True)


def on_device(
    queries,
    new_key_value,
    saved,
    out_weight,
    hist_owner,
    hist_block,
    hist_len,
    evict,
    dest_owner,
    dest_slot,
):
    pool = lax.axis_size("pool")
    me = lax.axis_index("pool")
    chips = lax.axis_size("tensor") // 2
    chip, core = lax.axis_index("tensor") // 2, lax.axis_index("tensor") % 2
    other_core = [(2 * z + c, 2 * z + 1 - c) for z in range(chips) for c in range(2)]
    upward = [(2 * z + c, 2 * ((z + 1) % chips) + c) for z in range(chips) for c in range(2)]
    downward = [(target, source) for source, target in upward]
    swap = functools.partial(lax.ppermute, axis_name="tensor", perm=other_core)
    send_up = functools.partial(lax.ppermute, axis_name="tensor", perm=upward)
    send_down = functools.partial(lax.ppermute, axis_name="tensor", perm=downward)

    def part(offset, c, half):
        return 128 * ((chip + offset) % chips) + 64 * c + PART * half

    plan = (((2, 0), (2, 1), (1, 1), (3, 0)), ((1, 0), (3, 1)), ((0, 0), (0, 1)))
    base = jnp.stack(
        [part(o, c, h) for parts in plan for c in (core, 1 - core) for o, h in parts]
    ).astype(jnp.int32)

    new_blocks = new_key_value.reshape(-1, 256, 128)
    table, blocks = exchange_table(
        hist_owner, hist_block, hist_len, dest_owner, dest_slot, evict, new_blocks, pool
    )
    arrived = swap_pool(table)
    pool_blocks = split_blocks(saved.reshape(-1, 256, 128))
    told = arrived[:, 32, :].astype(jnp.int32)
    kv = swap_pool(gather_blocks(told, pool_blocks, arrived[:, :32]))
    starts = begin(
        queries, split_blocks(new_blocks), base, [2 * len(parts) for parts in plan]
    )
    other_weight = swap(out_weight)
    kept = copy_pool(saved.reshape(-1, 256, 128))

    heads = queries.shape[1] // HEAD

    def contexts(group, after, before_swap=()):
        used, _ = lax.optimization_barrier((blocks, after))
        mine, theirs = attend(starts[group], kv, used, hist_len, heads, group)
        theirs, _ = lax.optimization_barrier((theirs, before_swap))
        return mine, swap(theirs)

    up, down, near_up, near_down = project(
        *contexts(0, (kept, starts)), out_weight, other_weight
    )
    through_up, through_down = send_up(up), send_down(down)
    near_up, near_down = send_up(near_up), send_down(near_down)
    up, down = project(*contexts(1, up), out_weight, other_weight)

    returned = kv[:, 512:].reshape(pool, 4, 8, 128).transpose(1, 0, 2, 3)
    mine = (told[:, 2:6] == me) & (told[:, 10:11] > 0)
    slots = jnp.max(jnp.where(mine, told[:, 6:10], -1), axis=0)
    up, down = add_arrived(up, down, through_up, through_down)
    far_up, far_down = send_up(up), send_down(down)

    top, bottom = project(
        *contexts(2, up, (near_up, near_down)), out_weight, other_weight
    )
    returned, _ = lax.optimization_barrier((returned, top))
    pool_out = write_back(slots, returned.reshape(4, 256, 128), kept).reshape(saved.shape)
    attn_out = combine(top, bottom, far_up, near_down, near_up, far_down)
    return attn_out, pool_out


def solution(mesh):
    in_specs = (
        P("pool", "tensor"),
        P("pool", None, "tensor"),
        P("pool", None, None, "tensor"),
        P("tensor", None),
        P("pool", None),
        P("pool", None),
        P("pool"),
        P("pool"),
        P("pool", None),
        P("pool", None),
    )
    out_specs = (P(("pool", "tensor"), None), P("pool", None, None, "tensor"))
    return jax.shard_map(
        on_device, mesh=mesh, in_specs=in_specs, out_specs=out_specs, check_vma=False
    )
```

```python
import functools
import math

import jax
import jax.numpy as jnp
from jax import lax
from jax.experimental import pallas as pl
from jax.experimental.pallas import tpu as pltpu
from jax.sharding import PartitionSpec as P

HEAD = 128
CHUNK = 8
PART = 32
NT = (((1,), (1,)), ((), ()))
SMEM = pl.BlockSpec(memory_space=pltpu.SMEM)
VMEM = pl.BlockSpec(memory_space=pltpu.VMEM)
ANY = pl.BlockSpec(memory_space=pl.ANY)
HBM = pl.BlockSpec(memory_space=pltpu.HBM)


def limit(mebibytes):
    return pltpu.CompilerParams(vmem_limit_bytes=mebibytes * 2**20)


def table_kernel(
    length, dest_owner, dest_slot, evict, owner_ref, block_ref, new_ref, table_ref, list_ref, rows_ref
):
    pool, entries = table_ref.shape[0], owner_ref.shape[1]
    owner = jnp.broadcast_to(owner_ref[...], (pool, entries))
    block = jnp.broadcast_to(block_ref[...], (pool, entries))
    row = lax.broadcasted_iota(jnp.int32, (pool, entries), 0)
    col = lax.broadcasted_iota(jnp.int32, (pool, entries), 1)
    match = owner == row
    first = jnp.min(jnp.where(match, col, entries), axis=1, keepdims=True)
    second = jnp.max(jnp.where(match, col, -1), axis=1, keepdims=True)
    want0 = jnp.sum(jnp.where(match & (col == first), block, 0), axis=1, keepdims=True)
    want1 = jnp.sum(jnp.where(match & (col == second), block, 0), axis=1, keepdims=True)
    row = lax.broadcasted_iota(jnp.int32, (pool, 128), 0)
    lane = lax.broadcasted_iota(jnp.int32, (pool, 128), 1)
    used0 = jnp.where(jnp.broadcast_to(first, (pool, 128)) < length[0], 1, 0)
    used1 = jnp.where(jnp.broadcast_to(second, (pool, 128)) < length[0], 1, 0)
    used = (used0 + used1).astype(jnp.float32)
    earlier = jnp.where(
        lax.broadcasted_iota(jnp.int32, (pool, pool), 1)
        < lax.broadcasted_iota(jnp.int32, (pool, pool), 0),
        1.0,
        0.0,
    )
    before = jnp.dot(earlier, used, preferred_element_type=jnp.float32).astype(jnp.int32)
    place = jnp.where((used0 > 0) & (before == lane), 2 * row, 0)
    place += jnp.where((used1 > 0) & (before + used0 == lane), 2 * row + 1, 0)
    quarter = pool // 4
    counts = jnp.where(row < quarter * (lane + 1), used0 + used1, 0)
    list_ref[...] = jnp.zeros(list_ref.shape, jnp.int32)
    list_ref[0:1] = jnp.sum(place, axis=0, keepdims=True)
    list_ref[1:2] = jnp.sum(counts, axis=0, keepdims=True)

    out = jnp.where(lane == 0, want0, jnp.where(lane == 1, want1, 0))
    for b in range(4):
        out = jnp.where(lane == 2 + b, dest_owner[0, b], out)
        out = jnp.where(lane == 6 + b, dest_slot[0, b], out)
    out = jnp.where(lane == 10, evict[0], out).astype(jnp.float32)
    for b in range(4):
        fresh = new_ref[b].astype(jnp.float32)
        for o in range(pool):
            rows_ref[o, 8 * b : 8 * b + 8, :] = fresh[8 * o : 8 * o + 8]
    for o in range(pool):
        rows_ref[o, 32:48, :] = jnp.broadcast_to(out[o : o + 1], (16, 128))
    table_ref[...] = rows_ref[...].astype(jnp.bfloat16)


def exchange_table(hist_owner, hist_block, hist_len, dest_owner, dest_slot, evict, new_blocks, pool):
    return pl.pallas_call(
        table_kernel,
        out_shape=(
            jax.ShapeDtypeStruct((pool, 48, 128), jnp.bfloat16),
            jax.ShapeDtypeStruct((8, 128), jnp.int32),
        ),
        in_specs=[SMEM, SMEM, SMEM, SMEM, VMEM, VMEM, VMEM],
        out_specs=(VMEM, VMEM),
        scratch_shapes=[pltpu.VMEM((pool, 48, 128), jnp.float32)],
        compiler_params=limit(58),
        name="table",
    )(hist_len, dest_owner, dest_slot, evict, hist_owner, hist_block, new_blocks)


def split_kernel(x_ref, o_ref):
    row = lax.broadcasted_iota(jnp.int32, (128, 256), 0)
    source = lax.broadcasted_iota(jnp.int32, (128, 256), 1)
    pick_k = jnp.where(source == 2 * row, 1.0, 0.0).astype(jnp.bfloat16)
    pick_v = jnp.where(source == 2 * row + 1, 1.0, 0.0).astype(jnp.bfloat16)
    for b in range(x_ref.shape[0]):
        x = x_ref[b]
        k = jnp.dot(pick_k, x, preferred_element_type=jnp.float32)
        v = jnp.dot(pick_v, x, preferred_element_type=jnp.float32)
        o_ref[b, 0:128, :] = k.astype(jnp.bfloat16)
        o_ref[b, 128:256, :] = v.T.astype(jnp.bfloat16)


def split_blocks(x):
    return pl.pallas_call(
        split_kernel,
        out_shape=jax.ShapeDtypeStruct(x.shape, x.dtype),
        in_specs=[VMEM],
        out_specs=VMEM,
        compiler_params=limit(12),
        name=f"split{x.shape[0]}",
    )(x)


def gather_kernel(told, pool_ref, held_ref, out_ref, held, onward, packed, sems):
    pool, rows = packed.shape[:2]
    copies = []
    for p in range(pool):
        for r in range(2):
            copies.append(
                pltpu.make_async_copy(
                    pool_ref.at[told[p, r]], out_ref.at[p, pl.ds(256 * r, 256)], sems.at[2 * p + r]
                )
            )
            copies[-1].start()
    held[...] = held_ref[...].astype(jnp.float32)
    for b in range(4):
        for p in range(pool):
            onward[told[p, 2 + b], 8 * b : 8 * b + 8, :] = held[p, 8 * b : 8 * b + 8, :]
    packed[...] = onward[...].astype(jnp.bfloat16)
    copies.append(
        pltpu.make_async_copy(packed, out_ref.at[:, pl.ds(512, rows)], sems.at[2 * pool])
    )
    copies[-1].start()
    for copy in copies:
        copy.wait()


def gather_blocks(told, pool_blocks, held):
    pool, rows, _ = held.shape
    return pl.pallas_call(
        gather_kernel,
        out_shape=jax.ShapeDtypeStruct((pool, 512 + rows, 128), pool_blocks.dtype),
        in_specs=[SMEM, VMEM, VMEM],
        out_specs=HBM,
        scratch_shapes=[
            pltpu.VMEM(held.shape, jnp.float32),
            pltpu.VMEM(held.shape, jnp.float32),
            pltpu.VMEM(held.shape, jnp.bfloat16),
            pltpu.SemaphoreType.DMA((2 * pool + 1,)),
        ],
        compiler_params=limit(51),
        name="gather",
    )(told, pool_blocks, held)


def accumulate(state, s, vt):
    m, l, acc = state
    c = math.log2(math.e) / math.sqrt(HEAD)
    top = jnp.maximum(m, jnp.max(s, axis=0, keepdims=True))
    p = jnp.exp2(s * c - top * c)
    keep = jnp.exp2((m - top) * c)
    l = l * keep + jnp.sum(p, axis=0, keepdims=True)
    acc = acc * keep + jnp.dot(vt, p.astype(jnp.bfloat16), preferred_element_type=jnp.float32)
    return top, l, acc


def begin_kernel(base, q_ref, new_ref, *refs):
    c = math.log2(math.e) / math.sqrt(HEAD)
    heads = q_ref.shape[1] // HEAD
    blocks = new_ref.shape[0]
    k = jnp.concatenate([new_ref[i, 0:128, :] for i in range(blocks)], axis=0)
    vt = jnp.concatenate([new_ref[i, 128:256, :] for i in range(blocks)], axis=1)
    before = 0
    for group in range(len(refs) // 4):
        out_q, out_m, out_l, out_acc = refs[4 * group : 4 * group + 4]
        rows = out_q.shape[0]
        tok = rows // heads
        parts = tok // PART
        key = lax.broadcasted_iota(jnp.int32, (blocks * 128, rows), 0)
        at = lax.broadcasted_iota(jnp.int32, (1, rows), 1) & (tok - 1)
        token = base[before] + at
        for i in range(1, parts):
            token = jnp.where(at >= PART * i, base[before + i] + at - PART * i, token)
        for i in range(parts):
            first = pl.multiple_of(base[before + i], PART)
            for h in range(heads):
                out_q[pl.ds(h * tok + i * PART, PART), :] = q_ref[
                    pl.ds(first, PART), h * HEAD : (h + 1) * HEAD
                ]
        s = lax.dot_general(k, out_q[...], NT, preferred_element_type=jnp.float32)
        s = jnp.where(key <= token, s, -jnp.inf)
        m = jnp.max(s, axis=0, keepdims=True)
        p = jnp.exp2(s * c - m * c)
        out_m[...] = m
        out_l[...] = jnp.sum(p, axis=0, keepdims=True)
        out_acc[...] = jnp.dot(vt, p.astype(jnp.bfloat16), preferred_element_type=jnp.float32)
        before += parts


def begin(queries, fresh, base, sizes):
    out_shape = ()
    for parts in sizes:
        rows = parts * PART * queries.shape[1] // HEAD
        out_shape += (
            jax.ShapeDtypeStruct((rows, HEAD), queries.dtype),
            jax.ShapeDtypeStruct((1, rows), jnp.float32),
            jax.ShapeDtypeStruct((1, rows), jnp.float32),
            jax.ShapeDtypeStruct((HEAD, rows), jnp.float32),
        )
    out = pl.pallas_call(
        begin_kernel,
        out_shape=out_shape,
        in_specs=[SMEM, VMEM, VMEM],
        out_specs=(VMEM,) * len(out_shape),
        compiler_params=limit(24),
        name="begin",
    )(base, queries, fresh)
    return [out[4 * g : 4 * g + 4] for g in range(len(sizes))]


def attend_kernel(
    blocks, length, q_ref, m_ref, l_ref, acc_ref, kv_any, mine_ref, theirs_ref, sbuf, kv_ref, sems
):
    quarters = sems.shape[0]
    share = kv_ref.shape[0] // quarters

    def quarter(k):
        owners = pl.ds(pl.multiple_of(k * share, share), share)
        return pltpu.make_async_copy(
            kv_any.at[owners, pl.ds(0, kv_ref.shape[1])], kv_ref.at[owners], sems.at[k]
        )

    def wait(k, _):
        quarter(k).wait()
        return 0

    for k in range(quarters):
        quarter(k).start()
    rows = q_ref.shape[0]
    tok = mine_ref.shape[0] * 2
    heads = rows // tok
    q = q_ref[...]

    def half(i, u, value):
        place = blocks[0, i * CHUNK + u]
        start = pl.multiple_of((place % 2) * 256 + 128 * value, 128)
        return kv_ref[place // 2, pl.ds(start, 128), :]

    def values_of(i):
        return jnp.concatenate([half(i, u, 1) for u in range(CHUNK)], axis=1)

    def scores(i):
        keys = jnp.concatenate([half(i, u, 0) for u in range(CHUNK)], axis=0)
        return lax.dot_general(keys, q, NT, preferred_element_type=jnp.float32)

    n = length[0]
    full = n // CHUNK
    last = 2 * kv_ref.shape[0] // CHUNK - 1
    opening = sum(jnp.where(blocks[1, k] < CHUNK, 1, 0) for k in range(quarters - 1))
    lax.fori_loop(0, opening + 1, wait, 0)
    sbuf[0] = scores(0)

    def step(i, state, a):
        sbuf[1 - a] = scores(jnp.minimum(i + 1, last))
        return accumulate(state, sbuf[a], values_of(i))

    def two(i, state):
        return step(2 * i + 1, step(2 * i, state, 0), 1)

    def upto(k):
        some = jnp.maximum(blocks[1, k] // CHUNK - 1, 0) // 2
        return jnp.where(k == quarters - 1, full // 2, some)

    def part(k, state):
        lax.fori_loop(jnp.where(k == opening, k + 1, k), k + 1, wait, 0)
        start = jnp.where(k == opening, 0, upto(jnp.maximum(k - 1, 0)))
        return lax.fori_loop(start, upto(k), two, state)

    state = (m_ref[...], l_ref[...], acc_ref[...])
    state = lax.fori_loop(opening, quarters, part, state)
    state = lax.fori_loop(full // 2 * 2, full, lambda i, st: step(i, st, 0), state)

    def tail(i, state):
        position = i * (CHUNK * 128) + lax.broadcasted_iota(jnp.int32, (CHUNK * 128, rows), 0)
        s = jnp.where(position < n * 128, scores(i), -jnp.inf)
        return accumulate(state, s, values_of(i))

    m, l, acc = lax.fori_loop(full, (n + CHUNK - 1) // CHUNK, tail, state)
    context = (acc / l).T.astype(jnp.bfloat16)
    own = tok // 2
    for h in range(heads):
        mine_ref[:, h * HEAD : (h + 1) * HEAD] = context[h * tok : h * tok + own]
        theirs_ref[:, h * HEAD : (h + 1) * HEAD] = context[h * tok + own : (h + 1) * tok]


def attend(start, kv, blocks, length, heads, group):
    q, m, l, acc = start
    rows = q.shape[0]
    out = jax.ShapeDtypeStruct((rows // heads // 2, heads * HEAD), jnp.bfloat16)
    return pl.pallas_call(
        attend_kernel,
        out_shape=(out, out),
        in_specs=[SMEM, SMEM, VMEM, VMEM, VMEM, VMEM, HBM],
        out_specs=(VMEM, VMEM),
        scratch_shapes=[
            pltpu.VMEM((2, CHUNK * 128, rows), jnp.float32),
            pltpu.VMEM((kv.shape[0], 512, 128), kv.dtype),
            pltpu.SemaphoreType.DMA((4,)),
        ],
        compiler_params=limit(50),
        name=f"attend{group}",
    )(blocks, length, q, m, l, acc, kv)


def project_kernel(a_ref, b_ref, wa_any, wb_any, *refs):
    outs, (wa_ref, wb_ref, sems) = refs[:-3], refs[-3:]
    tiles = sems.shape[0]
    tile = wa_ref.shape[1] // tiles
    copies = []
    for j in range(tiles):
        cols = pl.ds(j * tile, tile)
        copies.append(
            (
                pltpu.make_async_copy(wa_any.at[:, cols], wa_ref.at[:, cols], sems.at[j, 0]),
                pltpu.make_async_copy(wb_any.at[:, cols], wb_ref.at[:, cols], sems.at[j, 1]),
            )
        )
        for copy in copies[-1]:
            copy.start()
    for j in range(tiles):
        cols = slice(j * tile, (j + 1) * tile)
        for copy in copies[j]:
            copy.wait()
        total = jnp.dot(a_ref[...], wa_ref[:, cols], preferred_element_type=jnp.float32)
        total += jnp.dot(b_ref[...], wb_ref[:, cols], preferred_element_type=jnp.float32)
        for i, out_ref in enumerate(outs):
            out_ref[:, cols] = total[i * PART : (i + 1) * PART].astype(jnp.bfloat16)


def project(a, b, wa, wb):
    out = jax.ShapeDtypeStruct((PART, wa.shape[1]), jnp.bfloat16)
    parts = a.shape[0] // PART
    return pl.pallas_call(
        project_kernel,
        out_shape=(out,) * parts,
        in_specs=[VMEM, VMEM, HBM, HBM],
        out_specs=(VMEM,) * parts,
        scratch_shapes=[
            pltpu.VMEM(wa.shape, wa.dtype),
            pltpu.VMEM(wb.shape, wb.dtype),
            pltpu.SemaphoreType.DMA((10, 2)),
        ],
        compiler_params=limit(50),
        name=f"project{parts}",
    )(a, b, wa, wb)


def add_kernel(up, down, through_up, through_down, out_up, out_down):
    for own, arrived, out in ((up, through_up, out_up), (down, through_down, out_down)):
        total = own[...].astype(jnp.float32) + arrived[...].astype(jnp.float32)
        out[...] = total.astype(jnp.bfloat16)


def add_arrived(*parts):
    out = jax.ShapeDtypeStruct(parts[0].shape, parts[0].dtype)
    return pl.pallas_call(
        add_kernel,
        out_shape=(out, out),
        in_specs=[VMEM] * 4,
        out_specs=(VMEM, VMEM),
        compiler_params=limit(8),
        name="add",
    )(*parts)


def combine_kernel(top, bottom, far_up, near_down, near_up, far_down, o_ref):
    half = top.shape[0]
    for rows, parts in ((0, (top, far_up, near_down)), (half, (bottom, near_up, far_down))):
        total = sum(part[...].astype(jnp.float32) for part in parts)
        o_ref[rows : rows + half, :] = total.astype(jnp.bfloat16)


def combine(*parts):
    rows, width = parts[0].shape
    return pl.pallas_call(
        combine_kernel,
        out_shape=jax.ShapeDtypeStruct((2 * rows, width), jnp.bfloat16),
        in_specs=[VMEM] * 6,
        out_specs=VMEM,
        compiler_params=limit(8),
        name="combine",
    )(*parts)


def copy_kernel(x_ref, o_ref, buf, sem):
    for source, target in ((x_ref, buf), (buf, o_ref)):
        copy = pltpu.make_async_copy(source, target, sem)
        copy.start()
        copy.wait()


def copy_pool(x):
    return pl.pallas_call(
        copy_kernel,
        out_shape=jax.ShapeDtypeStruct(x.shape, x.dtype),
        in_specs=[HBM],
        out_specs=HBM,
        scratch_shapes=[pltpu.VMEM(x.shape, x.dtype), pltpu.SemaphoreType.DMA],
        compiler_params=limit(4),
        name="copy_pool",
    )(x)


def write_kernel(slots, fresh_ref, kept_ref, out_ref, sems):
    del kept_ref

    def block(b):
        slot = jnp.maximum(slots[b], 0)
        return pltpu.make_async_copy(fresh_ref.at[b], out_ref.at[slot], sems.at[b])

    for b in range(fresh_ref.shape[0]):

        @pl.when(slots[b] >= 0)
        def _(b=b):
            block(b).start()

    for b in range(fresh_ref.shape[0]):

        @pl.when(slots[b] >= 0)
        def _(b=b):
            block(b).wait()


def write_back(slots, fresh, kept):
    return pl.pallas_call(
        write_kernel,
        out_shape=jax.ShapeDtypeStruct(kept.shape, kept.dtype),
        in_specs=[SMEM, VMEM, ANY],
        out_specs=ANY,
        input_output_aliases={2: 0},
        scratch_shapes=[pltpu.SemaphoreType.DMA((fresh.shape[0],))],
        compiler_params=limit(4),
        name="write",
    )(slots, fresh, kept)


def swap_pool(x):
    return lax.all_to_all(x, "pool", split_axis=0, concat_axis=0, tiled=True)


def on_device(
    queries,
    new_key_value,
    saved,
    out_weight,
    hist_owner,
    hist_block,
    hist_len,
    evict,
    dest_owner,
    dest_slot,
):
    pool = lax.axis_size("pool")
    me = lax.axis_index("pool")
    chips = lax.axis_size("tensor") // 2
    chip, core = lax.axis_index("tensor") // 2, lax.axis_index("tensor") % 2
    other_core = [(2 * z + c, 2 * z + 1 - c) for z in range(chips) for c in range(2)]
    upward = [(2 * z + c, 2 * ((z + 1) % chips) + c) for z in range(chips) for c in range(2)]
    downward = [(target, source) for source, target in upward]
    swap = functools.partial(lax.ppermute, axis_name="tensor", perm=other_core)
    send_up = functools.partial(lax.ppermute, axis_name="tensor", perm=upward)
    send_down = functools.partial(lax.ppermute, axis_name="tensor", perm=downward)

    def part(offset, c, half):
        return 128 * ((chip + offset) % chips) + 64 * c + PART * half

    plan = (((2, 0), (2, 1), (1, 1), (3, 0)), ((1, 0), (3, 1)), ((0, 0), (0, 1)))
    base = jnp.stack(
        [part(o, c, h) for parts in plan for c in (core, 1 - core) for o, h in parts]
    ).astype(jnp.int32)

    new_blocks = new_key_value.reshape(-1, 256, 128)
    table, blocks = exchange_table(
        hist_owner, hist_block, hist_len, dest_owner, dest_slot, evict, new_blocks, pool
    )
    arrived = swap_pool(table)
    pool_blocks = split_blocks(saved.reshape(-1, 256, 128))
    told = arrived[:, 32, :].astype(jnp.int32)
    kv = swap_pool(gather_blocks(told, pool_blocks, arrived[:, :32]))
    starts = begin(
        queries, split_blocks(new_blocks), base, [2 * len(parts) for parts in plan]
    )
    other_weight = swap(out_weight)
    kept = copy_pool(saved.reshape(-1, 256, 128))

    heads = queries.shape[1] // HEAD

    def contexts(group, after, before_swap=()):
        used, _ = lax.optimization_barrier((blocks, after))
        mine, theirs = attend(starts[group], kv, used, hist_len, heads, group)
        theirs, _ = lax.optimization_barrier((theirs, before_swap))
        return mine, swap(theirs)

    up, down, near_up, near_down = project(
        *contexts(0, (kept, starts)), out_weight, other_weight
    )
    through_up, through_down = send_up(up), send_down(down)
    near_up, near_down = send_up(near_up), send_down(near_down)
    up, down = project(*contexts(1, up), out_weight, other_weight)

    returned = kv[:, 512:].reshape(pool, 4, 8, 128).transpose(1, 0, 2, 3)
    mine = (told[:, 2:6] == me) & (told[:, 10:11] > 0)
    slots = jnp.max(jnp.where(mine, told[:, 6:10], -1), axis=0)
    up, down = add_arrived(up, down, through_up, through_down)
    far_up, far_down = send_up(up), send_down(down)

    top, bottom = project(
        *contexts(2, up, (near_up, near_down)), out_weight, other_weight
    )
    returned, _ = lax.optimization_barrier((returned, top))
    pool_out = write_back(slots, returned.reshape(4, 256, 128), kept).reshape(saved.shape)
    attn_out = combine(top, bottom, far_up, near_down, near_up, far_down)
    return attn_out, pool_out


def solution(mesh):
    in_specs = (
        P("pool", "tensor"),
        P("pool", None, "tensor"),
        P("pool", None, None, "tensor"),
        P("tensor", None),
        P("pool", None),
        P("pool", None),
        P("pool"),
        P("pool"),
        P("pool", None),
        P("pool", None),
    )
    out_specs = (P(("pool", "tensor"), None), P("pool", None, None, "tensor"))
    return jax.shard_map(
        on_device, mesh=mesh, in_specs=in_specs, out_specs=out_specs, check_vma=False
    )
```
